32 devices in a mesh: strip: 16 (over z, y, core), canvas: 2 (over x).
Axes of the slice: x: 2, y: 2, z: 4, core: 2. Of those that a mesh axis runs over, the one named last changes fastest.
Arguments:
- latent_in: bfloat16 [8, 64, 176, 256], P('canvas', 'strip'), may hold values from -6 to 6
- crop_code: int32 [8, 64, 176], P('canvas', 'strip'), may hold values from 0 to 255, as said below
- code_index: int32 [8, 64, 176], P('canvas', 'strip'), may hold values from 0 to 511
- conv_weight: bfloat16 [3, 3, 256, 256], replicated, may hold values from -0.25 to 0.25
- conv_bias: bfloat16 [256], replicated, may hold values from -3 to 3
- mix_weight: bfloat16 [256, 256], replicated, may hold values from -1 to 1
- mix_bias: bfloat16 [256], replicated, may hold values from -3 to 3
- proj_weight: bfloat16 [256, 64], replicated, may hold values from -0.375 to 0.375
- proj_bias: bfloat16 [64], replicated, may hold values from -3 to 3
- codebook: bfloat16 [512, 64], replicated, may hold values from -6 to 6
- decode_weight: bfloat16 [64, 256], replicated, may hold values from -0.75 to 0.75
- decode_bias: bfloat16 [256], replicated, may hold values from -3 to 3
- out_grad: bfloat16 [8, 64, 176, 256], P('canvas', 'strip'), may hold values from -6 to 6
Outputs:
- decoded: bfloat16 [8, 64, 176, 256], P('canvas', 'strip')
- latent_grad: bfloat16 [8, 64, 176, 256], P('canvas', 'strip')
- conv_weight_grad: float32 [3, 3, 256, 256], replicated
- conv_bias_grad: float32 [256], replicated
- mix_weight_grad: float32 [256, 256], replicated
- mix_bias_grad: float32 [256], replicated
- proj_weight_grad: float32 [256, 64], replicated
- proj_bias_grad: float32 [64], replicated
- codebook_grad: float32 [512, 64], replicated
- decode_weight_grad: float32 [64, 256], replicated
- decode_bias_grad: float32 [256], replicated
The draws below stay inside these ranges and needn't reach their ends.
Inputs may be any that keep to these rules, and one draw needn't show every extreme that they name: Crops are rectangles of a canvas. Bit b of crop_code (b = 0 to 7, for the neighbours (a, b') in row-major order over the finite set (-1, 0, 1) x the finite set (-1, 0, 1) without (0, 0)) is 1 exactly when that neighbour lies inside the canvas and in the same crop; higher bits are 0.
All inputs are finite; a program needn't handle non-finite values.
Results may differ from the reference program's by a relative error of at most 0.0068.
Values may be sent and summed in bfloat16 or wider, within the bound.
No kernel may reach another device: no remote copies, remote signals or barrier semaphores. Data moves between devices by JAX's collectives and lax.ppermute only.
A program may use at most 128 MiB of HBM per device.

```python
import jax
import jax.numpy as jnp
from jax import lax

C = 256
E = 64
K = 512
COLS = 176
HEIGHT = 64
CANVASES = 8


def canvas_codes(key):
    key_list = jax.random.split(key, 3)
    columns = jnp.arange(COLS, dtype=jnp.int32)
    col_cuts = jax.random.randint(key_list[0], (3,), 1, COLS)
    col_band = jnp.sum((col_cuts[None, :] <= columns[:, None]).astype(jnp.int32), axis=1)
    row_cuts = jax.random.randint(key_list[1], (4, 3), 1, HEIGHT)
    chosen = jax.random.randint(key_list[2], (), 0, COLS)
    whole_band = col_band[chosen]
    row_cuts = jnp.where(jnp.arange(4, dtype=jnp.int32)[:, None] == whole_band, HEIGHT, row_cuts)
    row_index = jnp.arange(HEIGHT, dtype=jnp.int32)
    segment = jnp.sum((row_cuts[None, :, :] <= row_index[:, None, None]).astype(jnp.int32), axis=2)
    crop_ids = jnp.take(segment, col_band, axis=1) + 4 * col_band[None, :]
    padded = jnp.pad(crop_ids, 1, constant_values=-1)
    result = jnp.zeros((HEIGHT, COLS), jnp.int32)
    for offset in range(9):
        if offset != 4:
            shift_row = offset // 3
            shift_col = offset % 3
            neighbour = padded[shift_row:shift_row + HEIGHT, shift_col:shift_col + COLS]
            bit_place = offset if offset < 4 else offset - 1
            result = result + (neighbour == crop_ids).astype(jnp.int32) * 2 ** bit_place
    return result


def draw_crop_code(key, part):
    key = jax.random.fold_in(key, 7)
    return jax.vmap(canvas_codes)(jax.random.split(key, CANVASES))


def place_ends(values, rng, least, largest):
    dims = values.shape
    spot = [jax.random.randint(jax.random.fold_in(rng, axis), (), 0, dims[axis]) for axis in range(len(dims))]
    values = values.at[tuple(spot)].set(least)
    longest = dims.index(max(dims))
    spot[longest] = (spot[longest] + 1) % dims[longest]
    return values.at[tuple(spot)].set(largest)


def block_levels(own_key, dims, pieces, least, high):
    level = 1.0
    for axis_at, blocks in pieces:
        heights = jax.random.uniform(jax.random.fold_in(jax.random.fold_in(own_key, 6), axis_at), (blocks,), jnp.float32, least / len(pieces), high / len(pieces))
        level = level * jnp.repeat(jnp.exp(heights), dims[axis_at] // blocks).reshape((-1,) + (1,) * (len(dims) - 1 - axis_at))
    return level


def centred(own_key, dims, spread, most, shards=(), kind=jnp.bfloat16):
    factor_of = block_levels(own_key, dims, shards, -0.22, 0.18) if shards else 1.0
    values = jax.random.normal(own_key, dims, jnp.float32) * spread * factor_of
    return jnp.minimum(jnp.maximum(values, -most), most).astype(kind)


def setup_inputs(seed: int = 0) -> dict:
    keys = jax.random.split(jax.random.key(seed), 14)
    return {
        "latent_in": centred(keys[0], (CANVASES, HEIGHT, COLS, C), 1.0, 6.0, ((0, 2), (1, 16))),
        "crop_code": draw_crop_code(jax.random.fold_in(keys[13], 71), 0),
        "code_index": place_ends(jax.random.randint(keys[2], (CANVASES, HEIGHT, COLS), 0, K), jax.random.fold_in(keys[2], 1), 0, K - 1).astype(jnp.int32),
        "conv_weight": centred(keys[3], (3, 3, C, C), (9 * C // 4) ** -0.5, 0.25),
        "conv_bias": centred(keys[4], (C,), 0.5, 3.0),
        "mix_weight": centred(keys[5], (C, C), (C // 8) ** -0.5, 1.0),
        "mix_bias": centred(keys[6], (C,), 0.5, 3.0),
        "proj_weight": centred(keys[7], (C, E), C ** -0.5, 0.375),
        "proj_bias": centred(keys[8], (E,), 0.5, 3.0),
        "codebook": centred(keys[9], (K, E), 1.0, 6.0),
        "decode_weight": centred(keys[10], (E, C), E ** -0.5, 0.75),
        "decode_bias": centred(keys[11], (C,), 0.5, 3.0),
        "out_grad": centred(keys[12], (CANVASES, HEIGHT, COLS, C), 1.0, 6.0, ((0, 2), (1, 16))),
    }


@jax.custom_vjp
def low(v):
    return lax.optimization_barrier(v.astype(jnp.bfloat16)).astype(jnp.float32)

@jax.custom_vjp
def low_back(v):
    return v

def low_keep(v):
    return (low(v), None)

def low_pass(kept, grad):
    return (grad,)

def back_keep(v):
    return (v, None)

def back_low(kept, grad):
    return (low(grad),)
low.defvjp(low_keep, low_pass)
low_back.defvjp(back_keep, back_low)
commit_weight = 0.25
highest = lax.Precision.HIGHEST

def mask_planes(code_map):
    planes = []
    for offset in range(9):
        if offset == 4:
            planes.append(jnp.ones(code_map.shape, jnp.float32))
        else:
            bit_place = offset if offset < 4 else offset - 1
            planes.append((code_map // 2 ** bit_place % 2).astype(jnp.float32))
    return jnp.stack(planes, axis=2)

def conv_masked(active, conv_weight, mask_set):
    count_rows = active.shape[0]
    across = active.shape[1]
    framed = jnp.pad(active, ((1, 1), (1, 1), (0, 0)))
    summed = jnp.zeros((count_rows, across, conv_weight.shape[3]), active.dtype)
    for row_step in range(3):
        for col_step in range(3):
            offset = row_step * 3 + col_step
            window = framed[row_step:row_step + count_rows, col_step:col_step + across] * mask_set[:, :, offset:offset + 1]
            summed = summed + jnp.einsum('hwc,cd->hwd', window, conv_weight[row_step, col_step], precision=highest)
    return summed

def forward(weights, latent, mask_set, matches, fixed_code, fixed_latent):
    conv_weight, conv_bias, mix_weight, mix_bias, proj_weight, proj_bias, codebook, decode_weight, decode_bias = weights
    activated = low(jax.nn.silu(latent))
    conv_out = low_back(conv_masked(activated, conv_weight, mask_set) + conv_bias)
    second = low(jax.nn.silu(conv_out))
    branch = low_back(jnp.einsum('hwc,cd->hwd', second, mix_weight, precision=highest) + mix_bias)
    stream = low(latent + branch)
    encoded = low_back(jnp.einsum('hwc,ce->hwe', stream, proj_weight, precision=highest) + proj_bias)
    quantized = low(encoded + (fixed_code - fixed_latent))
    decoded = jnp.einsum('hwe,ec->hwc', quantized, decode_weight, precision=highest) + decode_bias
    looked_up = jnp.einsum('hwk,ke->hwe', matches, codebook, precision=highest)
    code_loss = jnp.sum((fixed_latent - looked_up) ** 2) + commit_weight * jnp.sum((encoded - fixed_code) ** 2)
    return ((decoded, code_loss), encoded)

def one_canvas(weights, latent_in, code_map, index_map, out_grad):
    latent = latent_in.astype(jnp.float32)
    mask_set = mask_planes(code_map)
    entries = weights[6].shape[0]
    matches = (index_map[:, :, None] == jnp.arange(entries, dtype=jnp.int32)[None, None, :]).astype(jnp.float32)
    fixed_code = jnp.einsum('hwk,ke->hwe', matches, weights[6], precision=highest)
    blank_code = jnp.zeros_like(fixed_code)
    first_pass = forward(weights, latent, mask_set, matches, blank_code, blank_code)
    fixed_latent = first_pass[1]

    def wrapped(params, inputs):
        return forward(params, inputs, mask_set, matches, fixed_code, fixed_latent)
    outputs, pullback, unused = jax.vjp(wrapped, weights, latent, has_aux=True)
    param_grads, input_grad = pullback((out_grad.astype(jnp.float32), jnp.ones((), outputs[1].dtype)))
    return (outputs[0].astype(jnp.bfloat16), input_grad.astype(jnp.bfloat16), param_grads)

def reference(latent_in, crop_code, code_index, conv_weight, conv_bias, mix_weight, mix_bias, proj_weight, proj_bias, codebook, decode_weight, decode_bias, out_grad):
    weights = tuple((tensor.astype(jnp.float32) for tensor in (conv_weight, conv_bias, mix_weight, mix_bias, proj_weight, proj_bias, codebook, decode_weight, decode_bias)))
    starting = tuple((jnp.zeros_like(tensor) for tensor in weights))

    def canvas_step(totals, slices):
        decoded, input_grad, param_grads = one_canvas(weights, slices[0], slices[1], slices[2], slices[3])
        return (jax.tree.map(jnp.add, totals, param_grads), (decoded, input_grad))
    totals, stacked = lax.scan(canvas_step, starting, (latent_in, crop_code, code_index, out_grad))
    return (stacked[0], stacked[1], totals[0], totals[1], totals[2], totals[3], totals[4], totals[5], totals[6], totals[7], totals[8])
```

```python
import functools

import jax
import jax.numpy as jnp
from jax import lax
from jax.experimental import pallas as pl
from jax.experimental.pallas import tpu as pltpu
from jax.sharding import PartitionSpec as P

commit_weight = 0.25
low = jnp.bfloat16
wide = jnp.float32
bit_up, bit_left, bit_right, bit_down = 1, 3, 4, 6
tile_rows = 16
vmem_bytes = 44 * 2**20


def mm(lhs, rhs):
    return jnp.dot(lhs, rhs, preferred_element_type=wide)


def mm_nt(lhs, rhs):
    return lax.dot_general(lhs, rhs, (((1,), (1,)), ((), ())), preferred_element_type=wide)


def mm_tn(lhs, rhs):
    return lax.dot_general(lhs, rhs, (((0,), (0,)), ((), ())), preferred_element_type=wide)


def sigmoid(values):
    return 0.5 * jnp.tanh(0.5 * values) + 0.5


def code_columns(code_ref):
    canvases, rows, across = code_ref.shape
    flat = code_ref[...].reshape(canvases * rows, across)
    extra = -across % 128
    if extra:
        flat = jnp.concatenate([flat, jnp.zeros((canvases * rows, extra), flat.dtype)], axis=1)
    return flat.T[:across]


def row_codes(columns, row, canvases, rows, lanes):
    pieces = [
        jnp.broadcast_to(
            columns[:, n * rows + row : n * rows + row + 1], (columns.shape[0], lanes)
        )
        for n in range(canvases)
    ]
    return jnp.concatenate(pieces, axis=0)


def bit_mask(codes, bit, channels):
    plane = ((codes >> bit) & 1).astype(wide)
    return jnp.concatenate([plane] * (channels // codes.shape[1]), axis=1)


def store_slab(slab_ref, at, values, left, right):
    count, channels = values.shape
    span = pl.ds(at, count)
    slab_ref[span, :channels] = (pltpu.roll(values, 1, 0) * left).astype(low)
    slab_ref[span, channels : 2 * channels] = values.astype(low)
    slab_ref[span, 2 * channels :] = (pltpu.roll(values, count - 1, 0) * right).astype(low)


def decoder_kernel(
    index_ref,
    out_grad_ref,
    codebook_ref,
    decode_weight_ref,
    decode_bias_ref,
    proj_bias_ref,
    decoded_ref,
    code_term_ref,
    weight_grad_ref,
    bias_grad_ref,
):
    canvases, rows, across = index_ref.shape
    entries, size = codebook_ref.shape
    channels = decode_weight_ref.shape[1]
    codebook = codebook_ref[...]
    both = jnp.concatenate([codebook * low(-0.5), codebook * low(2.0)], axis=1)
    blank = jnp.zeros((size, channels), low)
    weight = decode_weight_ref[...]
    weight_top = jnp.concatenate([weight, blank], axis=0)
    weight_end = jnp.concatenate([blank, weight * low(0.5)], axis=0)
    shift = proj_bias_ref[...].astype(wide)
    shift = jnp.concatenate([0.5 * shift, -2.0 * shift], axis=1)
    bias = decode_bias_ref[...].astype(wide)
    columns = code_columns(index_ref)
    weight_sum, bias_sum = None, None
    for row in range(rows):
        codes = row_codes(columns, row, canvases, rows, entries)
        picks = lax.broadcasted_iota(jnp.int32, codes.shape, 1) == codes
        picks = picks.astype(wide).astype(low)
        grad = out_grad_ref[:, row].reshape(canvases * across, channels)
        term = mm(picks, both) + mm_nt(grad, weight_top)
        code_term_ref[row] = term + shift
        code = term.astype(low)
        decoded = (mm(code, weight_end) + bias).astype(low)
        decoded_ref[:, row] = decoded.reshape(canvases, across, channels)
        weight_part = mm_tn(code, grad)
        bias_part = jnp.sum(grad.astype(wide), axis=0, keepdims=True)
        weight_sum = weight_part if weight_sum is None else weight_sum + weight_part
        bias_sum = bias_part if bias_sum is None else bias_sum + bias_part
    weight_grad_ref[...] = 0.5 * weight_sum[size:]
    bias_grad_ref[...] = bias_sum


def block_kernel(
    plan,
    crop_ref,
    index_ref,
    latent_ref,
    mate_ref,
    other_ref,
    code_term_ref,
    conv_weight_ref,
    conv_bias_ref,
    mix_weight_ref,
    mix_bias_ref,
    proj_weight_ref,
    decode_weight_grad_ref,
    decode_bias_grad_ref,
    grad_ref,
    branch_grad_ref,
    edge_mate_ref,
    edge_other_ref,
    keep_ref,
    send_ref,
    slab_ref,
    up_ref,
    down_ref,
    second_ref,
    stream_ref,
    codes_ref,
    picks_ref,
    message_ref,
):
    canvases, rows, across = crop_ref.shape
    channels = latent_ref.shape[3]
    size = proj_weight_ref.shape[1]
    entries = picks_ref.shape[1]
    count = canvases * across
    odd = lax.axis_index("strip") % 2
    columns = code_columns(crop_ref)
    index_columns = code_columns(index_ref)
    codes = [row_codes(columns, row, canvases, rows, 128) for row in range(rows)]

    def silu_low(values):
        values = values.astype(wide)
        return (values * sigmoid(values)).astype(low).astype(wide)

    def sides(row):
        return (bit_mask(codes[row], bit_left, channels), bit_mask(codes[row], bit_right, channels))

    for row in range(rows):
        values = silu_low(latent_ref[:, row].reshape(count, channels))
        store_slab(slab_ref, (row + 1) * count, values, *sides(row))
    above = jnp.where(odd == 1, mate_ref[...], other_ref[...]).reshape(count, channels)
    below = jnp.where(odd == 1, other_ref[...], mate_ref[...]).reshape(count, channels)
    store_slab(slab_ref, 0, silu_low(above), *sides(0))
    store_slab(slab_ref, (rows + 1) * count, silu_low(below), *sides(rows - 1))

    proj = proj_weight_ref[...]
    proj_both = jnp.concatenate([proj * low(2 * commit_weight), proj * low(-2.0)], axis=1)
    proj_top = jnp.concatenate([proj, jnp.zeros_like(proj)], axis=1)
    conv_bias = conv_bias_ref[...].astype(wide)
    mix_bias = mix_bias_ref[...].astype(wide)
    sums = [None, None, None]
    for row in range(rows):
        up = bit_mask(codes[row], bit_up, channels)
        down = bit_mask(codes[row], bit_down, channels)
        at = row * count
        conv = mm(slab_ref[pl.ds(at + count, count)], conv_weight_ref[1])
        conv = conv + up * mm(slab_ref[pl.ds(at, count)], conv_weight_ref[0])
        conv = conv + down * mm(slab_ref[pl.ds(at + 2 * count, count)], conv_weight_ref[2])
        conv = conv + conv_bias
        gate = sigmoid(conv)
        second = (conv * gate).astype(low)
        slope = gate * (1.0 + conv * (1.0 - gate))
        branch = mm(second, mix_weight_ref[...]) + mix_bias
        latent = latent_ref[:, row].reshape(count, channels).astype(wide)
        stream = (latent + branch).astype(low)
        code = (mm(stream, proj_both) + code_term_ref[row]).astype(low)
        branch_grad = mm_nt(code, proj_top).astype(low)
        grad = (mm_nt(branch_grad, mix_weight_ref[...]) * slope).astype(low)
        grad_wide = grad.astype(wide)
        branch_grad_ref[row] = branch_grad
        grad_ref[pl.ds(at, count)] = grad
        up_ref[pl.ds(at, count)] = (grad_wide * up).astype(low)
        down_ref[pl.ds(at, count)] = (grad_wide * down).astype(low)
        second_ref[pl.ds(at, count)] = second
        stream_ref[pl.ds(at, count)] = stream
        codes_ref[pl.ds(at, count)] = code
        picked = row_codes(index_columns, row, canvases, rows, entries)
        picks = lax.broadcasted_iota(jnp.int32, picked.shape, 1) == picked
        picks_ref[pl.ds(at, count)] = picks.astype(wide).astype(low)
        for place, values in enumerate((grad, branch_grad, code)):
            part = jnp.sum(values.astype(wide), axis=0, keepdims=True)
            sums[place] = part if sums[place] is None else sums[place] + part

    first, last = grad_ref[pl.ds(0, count)], grad_ref[pl.ds((rows - 1) * count, count)]
    edge_mate_ref[...] = jnp.where(odd == 1, first, last)
    edge_other_ref[...] = jnp.where(odd == 1, last, first)

    total = rows * count
    triple = 3 * channels
    for row_step, weighted_ref in enumerate((up_ref, grad_ref, down_ref)):
        part = mm_tn(slab_ref[pl.ds(row_step * count, total)], weighted_ref[...])
        message_ref[pl.ds(row_step * triple, triple)] = part.astype(low)
    at = 3 * triple
    mix_part = mm_tn(second_ref[...], branch_grad_ref[...].reshape(total, channels))
    message_ref[pl.ds(at, channels)] = mix_part.astype(low)
    at += channels
    message_ref[pl.ds(at, size)] = decode_weight_grad_ref[...].astype(low)
    at += size
    proj_part = mm_tn(codes_ref[...], stream_ref[...])
    message_ref[pl.ds(at, size)] = proj_part[:size].astype(low)
    at += size
    code_part = mm_tn(codes_ref[...], picks_ref[...])[size:].astype(low)
    for piece in range(entries // channels):
        message_ref[pl.ds(at, size)] = code_part[:, piece * channels : (piece + 1) * channels]
        at += size
    proj_sum = jnp.concatenate([sums[2]] * (channels // sums[2].shape[1]), axis=1)
    biases = [sums[0], sums[1], decode_bias_grad_ref[...], proj_sum]
    biases.append(jnp.zeros((tile_rows - len(biases), channels), wide))
    message_ref[pl.ds(at, tile_rows)] = jnp.concatenate(biases, axis=0).astype(low)
    at += tile_rows
    rest = message_ref.shape[0] - at
    if rest:
        message_ref[pl.ds(at, rest)] = jnp.zeros((rest, channels), low)

    me = plan.index()
    half, piece_rows = plan.shards // 2, plan.piece_rows
    mine, place = me // half, me % half
    for piece in range(half):
        near = pl.multiple_of((mine * half + piece) * piece_rows, piece_rows)
        far = pl.multiple_of(((1 - mine) * half + piece) * piece_rows, piece_rows)
        keep_ref[piece ^ place] = message_ref[pl.ds(near, piece_rows)]
        send_ref[piece ^ place] = message_ref[pl.ds(far, piece_rows)]


def input_kernel(
    crop_ref,
    latent_ref,
    grad_ref,
    mate_ref,
    other_ref,
    branch_grad_ref,
    conv_weight_ref,
    latent_grad_ref,
    slab_ref,
):
    canvases, rows, across = crop_ref.shape
    channels = latent_ref.shape[3]
    count = canvases * across
    odd = lax.axis_index("strip") % 2
    columns = code_columns(crop_ref)
    codes = [row_codes(columns, row, canvases, rows, 128) for row in range(rows)]

    def sides(row):
        return (bit_mask(codes[row], bit_left, channels), bit_mask(codes[row], bit_right, channels))

    for row in range(rows):
        values = grad_ref[pl.ds(row * count, count)].astype(wide)
        store_slab(slab_ref, (row + 1) * count, values, *sides(row))
    above = jnp.where(odd == 1, mate_ref[...], other_ref[...])
    below = jnp.where(odd == 1, other_ref[...], mate_ref[...])
    store_slab(slab_ref, 0, above.astype(wide), *sides(0))
    store_slab(slab_ref, (rows + 1) * count, below.astype(wide), *sides(rows - 1))

    for row in range(rows):
        spread = None
        for row_step, bit in ((1, None), (0, bit_up), (2, bit_down)):
            part = None
            for col_step in range(3):
                weight = conv_weight_ref[
                    2 - row_step, (2 - col_step) * channels : (3 - col_step) * channels
                ]
                span = pl.ds((row + row_step) * count, count)
                term = mm_nt(
                    slab_ref[span, col_step * channels : (col_step + 1) * channels], weight
                )
                part = term if part is None else part + term
            if bit is not None:
                part = part * bit_mask(codes[row], bit, channels)
            spread = part if spread is None else spread + part
        latent = latent_ref[:, row].reshape(count, channels).astype(wide)
        gate = sigmoid(latent)
        slope = gate * (1.0 + latent * (1.0 - gate))
        out = branch_grad_ref[row].astype(wide) + spread * slope
        latent_grad_ref[:, row] = out.astype(low).reshape(canvases, across, channels)


class Plan:
    def __init__(self, sizes, rows):
        self.sizes = sizes
        bits = {axis: [(axis, b) for b in range(size.bit_length() - 1)] for axis, size in sizes.items()}
        strip, canvas = bits["strip"], bits["canvas"]
        self.stages = [strip[:1], [*strip[1:2], *canvas[:1]], strip[2:4]]
        rest = [*strip[4:], *canvas[1:]]
        self.stages += [rest[i : i + 2] for i in range(0, len(rest), 2)]
        self.stages = [stage for stage in self.stages if stage]
        self.shards = sizes["strip"] * sizes["canvas"]
        self.piece_rows = -(-rows // (self.shards * tile_rows)) * tile_rows
        self.rows = self.shards * self.piece_rows

    def index(self):
        number = 0
        for stage in self.stages:
            for axis, bit in stage:
                number = number * 2 + (lax.axis_index(axis) // 2**bit) % 2
        return number

    def partner(self, stage, step):
        change = {"strip": 0, "canvas": 0}
        for place, (axis, bit) in enumerate(reversed(stage)):
            if step >> place & 1:
                change[axis] |= 1 << bit
        width = self.sizes["canvas"]
        return [
            (s * width + c, (s ^ change["strip"]) * width + (c ^ change["canvas"]))
            for s in range(self.sizes["strip"])
            for c in range(width)
        ]

    def swap(self, values, stage, step):
        return lax.ppermute(values, ("strip", "canvas"), self.partner(stage, step))


def add_kernel(count, *refs):
    ins, outs = refs[:count], refs[count:]
    depth = outs[0].shape[0]
    for place, out_ref in enumerate(outs):
        span = pl.ds(place * depth, depth)
        total = ins[0][span].astype(wide)
        for ref in ins[1:]:
            total = total + ref[span].astype(wide)
        out_ref[...] = total.astype(low)


def add_split(arrays, parts):
    depth, rows, channels = arrays[0].shape
    shape = jax.ShapeDtypeStruct((depth // parts, rows, channels), low)
    return pl.pallas_call(
        functools.partial(add_kernel, len(arrays)),
        out_shape=[shape] * parts,
        compiler_params=pltpu.CompilerParams(vmem_limit_bytes=vmem_bytes),
    )(*arrays)


def final_kernel(plan, count, sizes, *refs):
    ins, outs, gathered_ref = refs[:count], refs[count:-1], refs[-1]
    channels, size, entries = sizes
    me = plan.index()
    at = 0
    for ref in ins:
        for piece in range(ref.shape[0]):
            start = pl.multiple_of((me ^ at) * plan.piece_rows, plan.piece_rows)
            gathered_ref[pl.ds(start, plan.piece_rows)] = ref[piece]
            at += 1
    conv_ref, conv_bias_ref, mix_ref, mix_bias_ref, proj_ref, proj_bias_ref = outs[:6]
    codebook_ref, decode_ref, decode_bias_ref = outs[6:]
    at = 9 * channels
    conv_ref[...] = gathered_ref[pl.ds(0, at)].astype(wide)
    mix_ref[...] = gathered_ref[pl.ds(at, channels)].astype(wide)
    at += channels
    decode_ref[...] = gathered_ref[pl.ds(at, size)].astype(wide)
    at += size
    proj_ref[...] = gathered_ref[pl.ds(at, size)].astype(wide).T
    at += size
    for piece in range(entries // channels):
        rows = gathered_ref[pl.ds(at, size)].astype(wide).T
        codebook_ref[pl.ds(piece * channels, channels)] = rows
        at += size
    biases = gathered_ref[pl.ds(at, tile_rows)].astype(wide)
    conv_bias_ref[...] = biases[0:1]
    mix_bias_ref[...] = biases[1:2]
    decode_bias_ref[...] = biases[2:3]
    proj_bias_ref[...] = biases[3:4, :size]


def per_device(
    plan,
    latent_in,
    crop_code,
    code_index,
    conv_weight,
    conv_bias,
    mix_weight,
    mix_bias,
    proj_weight,
    proj_bias,
    codebook,
    decode_weight,
    decode_bias,
    out_grad,
):
    canvases, rows, across, channels = latent_in.shape
    entries, size = codebook.shape
    count = canvases * across
    total = rows * count
    params = pltpu.CompilerParams(vmem_limit_bytes=vmem_bytes)
    strips = plan.sizes["strip"]

    def line(values):
        return values.reshape(1, -1)

    def trade(mate, other):
        near = [(i, i ^ 1) for i in range(strips)]
        far = [(i, i + 1) for i in range(1, strips - 1, 2)]
        far += [(target, source) for source, target in far]
        return lax.ppermute(mate, "strip", near), lax.ppermute(other, "strip", far)

    odd = lax.axis_index("strip") % 2
    edge = (rows - 1) * (1 - odd)
    mate, other = trade(
        lax.dynamic_index_in_dim(latent_in, edge, axis=1, keepdims=False),
        lax.dynamic_index_in_dim(latent_in, rows - 1 - edge, axis=1, keepdims=False),
    )
    decoded, code_term, decode_weight_grad, decode_bias_grad = pl.pallas_call(
        decoder_kernel,
        out_shape=[
            jax.ShapeDtypeStruct(out_grad.shape, low),
            jax.ShapeDtypeStruct((rows, count, 2 * size), wide),
            jax.ShapeDtypeStruct((size, channels), wide),
            jax.ShapeDtypeStruct((1, channels), wide),
        ],
        compiler_params=params,
    )(code_index, out_grad, codebook, decode_weight, line(decode_bias), line(proj_bias))
    flat_weight = conv_weight.reshape(3, 3 * channels, channels)
    half = jax.ShapeDtypeStruct((plan.shards // 2, plan.piece_rows, channels), low)
    edge_shape = jax.ShapeDtypeStruct((count, channels), low)
    flat = pltpu.VMEM((total, channels), low)
    slab = pltpu.VMEM((total + 2 * count, 3 * channels), low)
    grad, branch_grad, edge_mate, edge_other, keep, send = pl.pallas_call(
        functools.partial(block_kernel, plan),
        out_shape=[
            jax.ShapeDtypeStruct((total, channels), low),
            jax.ShapeDtypeStruct((rows, count, channels), low),
            edge_shape,
            edge_shape,
            half,
            half,
        ],
        scratch_shapes=[
            slab,
            flat,
            flat,
            flat,
            flat,
            pltpu.VMEM((total, 2 * size), low),
            pltpu.VMEM((total, entries), low),
            pltpu.VMEM((plan.rows, channels), low),
        ],
        compiler_params=params,
    )(
        crop_code,
        code_index,
        latent_in,
        mate,
        other,
        code_term,
        flat_weight,
        line(conv_bias),
        mix_weight,
        line(mix_bias),
        proj_weight,
        decode_weight_grad,
        decode_bias_grad,
    )

    arrays = [keep, plan.swap(send, plan.stages[0], 1)]
    grad_mate, grad_other = trade(edge_mate, edge_other)
    for stage in plan.stages[1:]:
        parts = add_split(arrays, 2 ** len(stage))
        arrays = [parts[0]]
        arrays += [plan.swap(parts[i], stage, i) for i in range(1, len(parts))]
    gathered = add_split(arrays, 1)[0]
    latent_grad = pl.pallas_call(
        input_kernel,
        out_shape=jax.ShapeDtypeStruct(latent_in.shape, low),
        scratch_shapes=[slab],
        compiler_params=params,
    )(crop_code, latent_in, grad, grad_mate, grad_other, branch_grad, flat_weight)
    for stage in reversed(plan.stages[1:]):
        others = [plan.swap(gathered, stage, i) for i in range(1, 2 ** len(stage))]
        gathered = jnp.concatenate([gathered, *others], axis=0)
    arrays = [gathered, plan.swap(gathered, plan.stages[0], 1)]

    results = pl.pallas_call(
        functools.partial(final_kernel, plan, len(arrays), (channels, size, entries)),
        out_shape=[
            jax.ShapeDtypeStruct((9 * channels, channels), wide),
            jax.ShapeDtypeStruct((1, channels), wide),
            jax.ShapeDtypeStruct((channels, channels), wide),
            jax.ShapeDtypeStruct((1, channels), wide),
            jax.ShapeDtypeStruct((channels, size), wide),
            jax.ShapeDtypeStruct((1, size), wide),
            jax.ShapeDtypeStruct((entries, size), wide),
            jax.ShapeDtypeStruct((size, channels), wide),
            jax.ShapeDtypeStruct((1, channels), wide),
        ],
        scratch_shapes=[pltpu.VMEM((plan.rows, channels), low)],
        compiler_params=params,
    )(*arrays)
    return (
        decoded,
        latent_grad,
        results[0].reshape(3, 3, channels, channels),
        results[1].reshape(-1),
        results[2],
        results[3].reshape(-1),
        results[4],
        results[5].reshape(-1),
        results[6],
        results[7],
        results[8].reshape(-1),
    )


def solution(mesh):
    sizes = {axis: mesh.shape[axis] for axis in ("strip", "canvas")}
    shared = P("canvas", "strip", None, None)
    codes = P("canvas", "strip", None)

    def wrapped(*args):
        channels = args[0].shape[3]
        entries, size = args[9].shape
        rows = 10 * channels + 2 * size + size * (entries // channels) + tile_rows
        plan = Plan(sizes, rows)
        return jax.shard_map(
            functools.partial(per_device, plan),
            mesh=mesh,
            in_specs=(shared, codes, codes, *[P()] * 9, shared),
            out_specs=(shared, shared, *[P()] * 9),
            check_vma=False,
        )(*args)

    return wrapped
```

```python
import functools

import jax
import jax.numpy as jnp
from jax import lax
from jax.experimental import pallas as pl
from jax.experimental.pallas import tpu as pltpu
from jax.sharding import PartitionSpec as P

commit_weight = 0.25
low = jnp.bfloat16
wide = jnp.float32
bit_up, bit_left, bit_right, bit_down = 1, 3, 4, 6
tile_rows = 16
vmem_bytes = 28 * 2**20
in_hbm = pl.BlockSpec(memory_space=pltpu.HBM)
anywhere = pl.BlockSpec(memory_space=pl.ANY)
in_vmem = pl.BlockSpec(memory_space=pltpu.VMEM)


def mm(lhs, rhs):
    return jnp.dot(lhs, rhs, preferred_element_type=wide)


def mm_nt(lhs, rhs):
    return lax.dot_general(lhs, rhs, (((1,), (1,)), ((), ())), preferred_element_type=wide)


def mm_tn(lhs, rhs):
    return lax.dot_general(lhs, rhs, (((0,), (0,)), ((), ())), preferred_element_type=wide)


def sigmoid(values):
    return 0.5 * jnp.tanh(0.5 * values) + 0.5


def code_columns(code_ref):
    canvases, rows, across = code_ref.shape
    flat = code_ref[...].reshape(canvases * rows, across)
    extra = -across % 128
    if extra:
        flat = jnp.concatenate([flat, jnp.zeros((canvases * rows, extra), flat.dtype)], axis=1)
    return flat.T[:across]


def row_codes(columns, row, canvases, rows, lanes):
    pieces = [
        jnp.broadcast_to(
            columns[:, n * rows + row : n * rows + row + 1], (columns.shape[0], lanes)
        )
        for n in range(canvases)
    ]
    return jnp.concatenate(pieces, axis=0)


def chunks(count):
    return [(at, pl.ds(at, tile_rows)) for at in range(0, count, tile_rows)]


def pick(codes, bit, values):
    chosen = (codes & 2**bit) != 0
    parts = []
    for at in range(0, values.shape[1], 128):
        part = values[:, at : at + 128]
        parts.append(jnp.where(chosen, part, jnp.zeros_like(part)))
    return jnp.concatenate(parts, axis=1)


def store_slab(slab_ref, at, codes, values):
    count = codes.shape[0]
    channels = slab_ref.shape[1] // 3
    steps = chunks(count)
    held = [values(start) for start, _ in steps]
    for place, (start, _) in enumerate(steps):
        here = held[place]
        span = pl.ds(at + start, tile_rows)
        spots = codes[start : start + tile_rows]
        before = held[place - 1][tile_rows - 8 :]
        after = held[(place + 1) % len(steps)][:8]
        left = pltpu.roll(jnp.concatenate([before, here], axis=0), 1, 0)[8:]
        right = jnp.concatenate([here, after], axis=0)
        right = pltpu.roll(right, right.shape[0] - 1, 0)[:tile_rows]
        slab_ref[span, :channels] = pick(spots, bit_left, left).astype(low)
        slab_ref[span, channels : 2 * channels] = here.astype(low)
        slab_ref[span, 2 * channels :] = pick(spots, bit_right, right).astype(low)


def edge_kernel(latent_ref, mate_ref, other_ref, sems):
    rows = latent_ref.shape[1]
    odd = lax.axis_index("strip") % 2
    edge = (rows - 1) * (1 - odd)
    near = pltpu.make_async_copy(latent_ref.at[:, edge], mate_ref, sems.at[0])
    far = pltpu.make_async_copy(latent_ref.at[:, rows - 1 - edge], other_ref, sems.at[1])
    near.start()
    far.start()
    near.wait()
    far.wait()


def code_kernel(
    index_hbm,
    codebook_hbm,
    decode_weight_hbm,
    out_grad_hbm,
    latent_hbm,
    crop_hbm,
    conv_weight_hbm,
    mix_weight_hbm,
    term_ref,
    picks_ref,
    weight_grad_ref,
    bias_grad_ref,
    latent_ref,
    crop_ref,
    conv_weight_ref,
    mix_weight_ref,
    index_ref,
    codebook_ref,
    decode_weight_ref,
    out_grad_ref,
    sems,
):
    canvases, rows, across = index_ref.shape
    size, entries = codebook_ref.shape
    channels = decode_weight_ref.shape[1]
    count = canvases * across
    pairs = [
        (index_hbm, index_ref),
        (codebook_hbm, codebook_ref),
        (decode_weight_hbm, decode_weight_ref),
    ]
    pairs += [(out_grad_hbm.at[:, row], out_grad_ref.at[row]) for row in range(rows)]
    pairs += [
        (latent_hbm, latent_ref),
        (crop_hbm, crop_ref),
        (conv_weight_hbm, conv_weight_ref),
        (mix_weight_hbm, mix_weight_ref),
    ]
    copies = [
        pltpu.make_async_copy(source, target, sems.at[place])
        for place, (source, target) in enumerate(pairs)
    ]
    for copy in copies:
        copy.start()
    for copy in copies[:3]:
        copy.wait()
    codebook = codebook_ref[...]
    both = jnp.concatenate([codebook * low(-0.5), codebook * low(2.0)], axis=0)
    weight = decode_weight_ref[...]
    weight_top = jnp.concatenate([weight, jnp.zeros_like(weight)], axis=0)
    columns = code_columns(index_ref)
    weight_sum, bias_sum = None, None
    for row in range(rows):
        codes = row_codes(columns, row, canvases, rows, entries)
        picks = lax.broadcasted_iota(jnp.int32, codes.shape, 1) == codes
        picks = picks.astype(wide).astype(low)
        picks_ref[pl.ds(row * count, count)] = picks
        copies[3 + row].wait()
        grad = out_grad_ref[row].reshape(count, channels)
        term = mm_nt(picks, both) + mm_nt(grad, weight_top)
        term_ref[row] = term
        weight_part = mm_tn(term.astype(low), grad)
        bias_part = jnp.sum(grad.astype(wide), axis=0, keepdims=True)
        weight_sum = weight_part if weight_sum is None else weight_sum + weight_part
        bias_sum = bias_part if bias_sum is None else bias_sum + bias_part
    weight_grad_ref[...] = 0.5 * weight_sum[size:]
    bias_grad_ref[...] = bias_sum
    for copy in copies[3 + rows :]:
        copy.wait()


def decoded_kernel(term_ref, decode_weight_ref, decode_bias_ref, after_ref, decoded_ref):
    canvases, rows, across, channels = decoded_ref.shape
    weight = decode_weight_ref[...] * low(0.5)
    weight = jnp.concatenate([jnp.zeros_like(weight), weight], axis=0)
    bias = decode_bias_ref[...].astype(wide).reshape(1, channels)
    for row in range(rows):
        decoded = (mm(term_ref[row].astype(low), weight) + bias).astype(low)
        decoded_ref[:, row] = decoded.reshape(canvases, across, channels)


def rows_kernel(
    mine,
    crop_ref,
    latent_ref,
    term_ref,
    conv_weight_ref,
    conv_bias_ref,
    mix_weight_ref,
    mix_bias_ref,
    proj_weight_ref,
    proj_bias_ref,
    *refs,
):
    outs = refs[-9:]
    slab_ref, grad_ref, up_ref, down_ref, second_ref, stream_ref, codes_ref = outs[:7]
    branch_grad_ref, sums_ref = outs[7:]
    canvases, rows, across = crop_ref.shape
    channels = latent_ref.shape[3]
    size = proj_weight_ref.shape[0]
    count = canvases * across
    odd = lax.axis_index("strip") % 2
    columns = code_columns(crop_ref)
    codes = [row_codes(columns, row, canvases, rows, 128) for row in range(rows)]

    def silu(values):
        values = values.astype(wide)
        return values * sigmoid(values)

    def own(row):
        def values(at):
            return silu(latent_ref[at // across, row, pl.ds(at % across, tile_rows)])

        return values

    def beside(first_ref, second_ref, swap):
        def values(at):
            span = pl.ds(at % across, tile_rows)
            one, two = first_ref[at // across, span], second_ref[at // across, span]
            return silu(jnp.where(swap, one, two))

        return values

    inner = 0 not in mine or rows == 1
    if inner or rows <= 2:
        for row in range(rows):
            store_slab(slab_ref, (row + 1) * count, codes[row], own(row))
    if 0 in mine:
        mate_ref, other_ref = refs[:2]
        store_slab(slab_ref, 0, codes[0], beside(mate_ref, other_ref, odd == 1))
        end = (rows + 1) * count
        store_slab(slab_ref, end, codes[rows - 1], beside(other_ref, mate_ref, odd == 1))

    proj = proj_weight_ref[...]
    proj_both = jnp.concatenate([proj * low(2 * commit_weight), proj * low(-2.0)], axis=0)
    proj_top = jnp.concatenate([proj, jnp.zeros_like(proj)], axis=0)
    conv_bias = conv_bias_ref[...].astype(wide).reshape(1, channels)
    mix_bias = mix_bias_ref[...].astype(wide).reshape(1, channels)
    proj_bias = proj_bias_ref[...].astype(wide).reshape(1, size)
    proj_bias = jnp.concatenate([2 * commit_weight * proj_bias, -2.0 * proj_bias], axis=1)
    sums = [None, None, None]
    steps = chunks(count)

    def add_to(place, values):
        values = values[:8] + values[8:]
        sums[place] = values if sums[place] is None else sums[place] + values

    held = None
    for row, was in zip((*mine, None), (None, *mine), strict=True):
        if row is not None:
            at = row * count
            conv_mid = mm(slab_ref[pl.ds(at + count, count)], conv_weight_ref[1])
        if was is not None:
            back = was * count
            slope = held
            branch = mm(second_ref[pl.ds(back, count)], mix_weight_ref[...])
            for start, _ in steps:
                span = pl.ds(back + start, tile_rows)
                latent = latent_ref[start // across, was, pl.ds(start % across, tile_rows)]
                part = latent.astype(wide) + (branch[start : start + tile_rows] + mix_bias)
                stream_ref[span] = part.astype(low)
        if row is not None:
            conv_up = mm(slab_ref[pl.ds(at, count)], conv_weight_ref[0])
        if was is not None:
            code = mm_nt(stream_ref[pl.ds(back, count)], proj_both)
            for start, near in steps:
                part = code[start : start + tile_rows] + (term_ref[was, near] + proj_bias)
                codes_ref[pl.ds(back + start, tile_rows)] = part.astype(low)
                add_to(2, part)
        if row is not None:
            conv_down = mm(slab_ref[pl.ds(at + 2 * count, count)], conv_weight_ref[2])
        if was is not None:
            branch_grad = mm(codes_ref[pl.ds(back, count)], proj_top)
            for start, near in steps:
                part = branch_grad[start : start + tile_rows]
                branch_grad_ref[was, near] = part.astype(low)
                add_to(1, part)
        if row is not None:
            held = []
            for start, _ in steps:
                some = slice(start, start + tile_rows)
                conv = pick(codes[row][some], bit_up, conv_up[some])
                conv = conv + pick(codes[row][some], bit_down, conv_down[some])
                conv = (conv + conv_mid[some]) + conv_bias
                gate = sigmoid(conv)
                second_ref[pl.ds(at + start, tile_rows)] = (conv * gate).astype(low)
                held.append(gate * (1.0 + conv * (1.0 - gate)))
        if was is not None:
            grad = mm_nt(branch_grad_ref[was], mix_weight_ref[...])
            for place, (start, _) in enumerate(steps):
                some = slice(start, start + tile_rows)
                span = pl.ds(back + start, tile_rows)
                part = grad[some] * slope[place]
                grad_ref[span] = part.astype(low)
                up_ref[span] = pick(codes[was][some], bit_up, part).astype(low)
                down_ref[span] = pick(codes[was][some], bit_down, part).astype(low)
                add_to(0, part)
    sums = [jnp.sum(values, axis=0, keepdims=True) for values in sums]
    sums[2] = jnp.concatenate([sums[2]] * (channels // sums[2].shape[1]), axis=1)
    blank = jnp.zeros((sums_ref.shape[0] - 3, channels), wide)
    sums = jnp.concatenate([*sums, blank], axis=0)
    if len(refs) > 9 + 2 * (0 in mine):
        sums = sums + refs[-10][...]
    sums_ref[...] = sums


def edge_rows_kernel(grad_ref, mate_ref, other_ref):
    count = mate_ref.shape[0]
    odd = lax.axis_index("strip") % 2
    first, last = grad_ref[pl.ds(0, count)], grad_ref[pl.ds(grad_ref.shape[0] - count, count)]
    mate_ref[...] = jnp.where(odd == 1, first, last)
    other_ref[...] = jnp.where(odd == 1, last, first)


def weight_kernel(
    plan,
    mine,
    slab_ref,
    grad_ref,
    up_ref,
    down_ref,
    second_ref,
    stream_ref,
    codes_ref,
    branch_grad_ref,
    sums_ref,
    picks_ref,
    decode_weight_grad_ref,
    decode_bias_grad_ref,
    after_ref,
    out_ref,
    message_ref,
):
    total, channels = grad_ref.shape
    rows, count, _ = branch_grad_ref.shape
    size = decode_weight_grad_ref.shape[0]
    entries = picks_ref.shape[1]
    triple = 3 * channels
    me = plan.index()
    half = plan.shards // 2
    core, place = me // half, me % half
    wanted = core if mine else 1 - core

    def step(row_step, weighted_ref):
        span = pl.ds(row_step * count, total)
        return mm_tn(slab_ref[span], weighted_ref[...]).astype(low)

    def fill(parts):
        at = 0
        for part in parts:
            message_ref[pl.ds(at, part.shape[0])] = part
            at += part.shape[0]
        rest = message_ref.shape[0] - at
        if rest:
            message_ref[pl.ds(at, rest)] = jnp.zeros((rest, channels), low)

    @pl.when(wanted == 0)
    def _():
        fill([step(0, up_ref), step(1, grad_ref)])

    @pl.when(wanted == 1)
    def _():
        code_part = mm_tn(codes_ref[...], picks_ref[...])[size:].astype(low)
        sums = sums_ref[...]
        biases = [sums[0:1], sums[1:2], decode_bias_grad_ref[...], sums[2:3]]
        biases.append(jnp.zeros((tile_rows - len(biases), channels), wide))
        fill(
            [
                step(2, down_ref),
                mm_tn(second_ref[...], branch_grad_ref[...].reshape(total, channels)).astype(low),
                decode_weight_grad_ref[...].astype(low),
                mm_tn(codes_ref[...], stream_ref[...])[:size].astype(low),
                *[code_part[:, i : i + channels] for i in range(0, entries, channels)],
                jnp.concatenate(biases, axis=0).astype(low),
            ]
        )

    for piece in range(half):
        rows_of = pl.ds(piece * plan.piece_rows, plan.piece_rows)
        out_ref[piece ^ place] = message_ref[rows_of]


def input_kernel(
    mine,
    crop_ref,
    latent_ref,
    grad_ref,
    mate_ref,
    other_ref,
    branch_grad_ref,
    conv_weight_ref,
    after_ref,
    *refs,
):
    latent_grad_ref, slab_ref, out_ref, sems = refs[-4:]
    canvases, rows, across = crop_ref.shape
    channels = latent_ref.shape[3]
    count = canvases * across
    odd = lax.axis_index("strip") % 2
    columns = code_columns(crop_ref)
    codes = [row_codes(columns, row, canvases, rows, 128) for row in range(rows)]

    steps = chunks(count)

    def own(row):
        def values(at):
            return grad_ref[pl.ds(row * count + at, tile_rows)].astype(wide)

        return values

    def beside(first_ref, second_ref, swap):
        def values(at):
            span = pl.ds(at, tile_rows)
            return jnp.where(swap, first_ref[span], second_ref[span]).astype(wide)

        return values

    for row in range(rows):
        if any(abs(row - near) < 2 for near in mine):
            store_slab(slab_ref, (row + 1) * count, codes[row], own(row))
    if 0 in mine:
        store_slab(slab_ref, 0, codes[0], beside(mate_ref, other_ref, odd == 1))
    if rows - 1 in mine:
        end = (rows + 1) * count
        store_slab(slab_ref, end, codes[rows - 1], beside(other_ref, mate_ref, odd == 1))

    copies = []
    for place, row in enumerate(mine):
        spreads = []
        for row_step in range(3):
            part = None
            for col_step in range(3):
                weight = conv_weight_ref[
                    2 - row_step, (2 - col_step) * channels : (3 - col_step) * channels
                ]
                span = pl.ds((row + row_step) * count, count)
                term = mm_nt(
                    slab_ref[span, col_step * channels : (col_step + 1) * channels], weight
                )
                part = term if part is None else part + term
            spreads.append(part)
        for start, near in steps:
            some = slice(start, start + tile_rows)
            spread = pick(codes[row][some], bit_up, spreads[0][some])
            spread = spread + pick(codes[row][some], bit_down, spreads[2][some])
            spread = spread + spreads[1][some]
            inside = pl.ds(start % across, tile_rows)
            latent = latent_ref[start // across, row, inside].astype(wide)
            gate = sigmoid(latent)
            slope = gate * (1.0 + latent * (1.0 - gate))
            out = branch_grad_ref[row, near].astype(wide) + spread * slope
            out_ref[place, start // across, inside] = out.astype(low)
        copies.append(
            pltpu.make_async_copy(out_ref.at[place], latent_grad_ref.at[:, row], sems.at[place])
        )
        copies[-1].start()
    for copy in copies:
        copy.wait()


class Plan:
    def __init__(self, sizes, half_rows):
        self.sizes = sizes
        bits = {axis: [(axis, b) for b in range(size.bit_length() - 1)] for axis, size in sizes.items()}
        strip, canvas = bits["strip"], bits["canvas"]
        self.stages = [strip[:1], [*strip[1:2], *canvas[:1]], strip[2:4]]
        rest = [*strip[4:], *canvas[1:]]
        self.stages += [rest[i : i + 2] for i in range(0, len(rest), 2)]
        self.stages = [stage for stage in self.stages if stage]
        self.shards = sizes["strip"] * sizes["canvas"]
        self.piece_rows = -(-half_rows // (self.shards // 2 * tile_rows)) * tile_rows
        self.half_rows = self.shards // 2 * self.piece_rows

    def index(self):
        number = 0
        for stage in self.stages:
            for axis, bit in stage:
                number = number * 2 + (lax.axis_index(axis) // 2**bit) % 2
        return number

    def partner(self, stage, step):
        change = {"strip": 0, "canvas": 0}
        for place, (axis, bit) in enumerate(reversed(stage)):
            if step >> place & 1:
                change[axis] |= 1 << bit
        width = self.sizes["canvas"]
        return [
            (s * width + c, (s ^ change["strip"]) * width + (c ^ change["canvas"]))
            for s in range(self.sizes["strip"])
            for c in range(width)
        ]

    def swap(self, values, stage, step):
        return lax.ppermute(values, ("strip", "canvas"), self.partner(stage, step))


def add_kernel(count, after, *refs):
    ins, outs = refs[:count], refs[count + after :]
    depth = outs[0].shape[0]
    for place, out_ref in enumerate(outs):
        span = pl.ds(place * depth, depth)
        total = ins[0][span].astype(wide)
        for ref in ins[1:]:
            total = total + ref[span].astype(wide)
        out_ref[...] = total.astype(low)


def add_split(arrays, parts, after=()):
    depth, rows, channels = arrays[0].shape
    shape = jax.ShapeDtypeStruct((depth // parts, rows, channels), low)
    return pl.pallas_call(
        functools.partial(add_kernel, len(arrays), len(after)),
        in_specs=[in_vmem] * len(arrays) + [anywhere] * len(after),
        out_specs=[in_vmem] * parts,
        out_shape=[shape] * parts,
        compiler_params=pltpu.CompilerParams(vmem_limit_bytes=vmem_bytes),
    )(*arrays, *after)


def gate_kernel(*refs):
    pass


def gate(array, *after):
    return pl.pallas_call(
        gate_kernel,
        in_specs=[in_vmem] + [anywhere] * len(after),
        out_specs=in_vmem,
        out_shape=jax.ShapeDtypeStruct(array.shape, array.dtype),
        input_output_aliases={0: 0},
        compiler_params=pltpu.CompilerParams(vmem_limit_bytes=vmem_bytes),
    )(array, *after)


def join_kernel(count, *refs):
    at = 0
    for ref in refs[:count]:
        refs[-1][pl.ds(at, ref.shape[0])] = ref[...]
        at += ref.shape[0]


def join(arrays, *after):
    depth, rows, channels = arrays[0].shape
    return pl.pallas_call(
        functools.partial(join_kernel, len(arrays)),
        in_specs=[in_vmem] * len(arrays) + [anywhere] * len(after),
        out_specs=in_vmem,
        out_shape=jax.ShapeDtypeStruct((depth * len(arrays), rows, channels), low),
        compiler_params=pltpu.CompilerParams(vmem_limit_bytes=vmem_bytes),
    )(*arrays, *after)


def final_kernel(plan, count, sizes, *refs):
    ins, outs, gathered_ref = refs[:count], refs[count:-1], refs[-1]
    channels, size, entries = sizes
    me = plan.index()
    at = 0
    for ref in ins:
        for piece in range(ref.shape[0]):
            start = pl.multiple_of((me ^ at) * plan.piece_rows, plan.piece_rows)
            gathered_ref[pl.ds(start, plan.piece_rows)] = ref[piece]
            at += 1
    conv_ref, conv_bias_ref, mix_ref, mix_bias_ref, proj_ref, proj_bias_ref = outs[:6]
    codebook_ref, decode_ref, decode_bias_ref = outs[6:]
    triple = 3 * channels
    conv_ref[pl.ds(0, 2 * triple)] = gathered_ref[pl.ds(0, 2 * triple)].astype(wide)
    at = plan.half_rows
    conv_ref[pl.ds(2 * triple, triple)] = gathered_ref[pl.ds(at, triple)].astype(wide)
    at += triple
    mix_ref[...] = gathered_ref[pl.ds(at, channels)].astype(wide)
    at += channels
    decode_ref[...] = gathered_ref[pl.ds(at, size)].astype(wide)
    at += size
    proj_ref[...] = gathered_ref[pl.ds(at, size)].astype(wide)
    at += size
    for piece in range(entries // channels):
        part = gathered_ref[pl.ds(at, size)].astype(wide)
        codebook_ref[:, piece * channels : (piece + 1) * channels] = part
        at += size
    biases = gathered_ref[pl.ds(at, tile_rows)].astype(wide)
    conv_bias_ref[...] = biases[0:1]
    mix_bias_ref[...] = biases[1:2]
    decode_bias_ref[...] = biases[2:3]
    proj_bias_ref[...] = biases[3:4, :size]


def per_device(
    plan,
    latent_in,
    crop_code,
    code_index,
    conv_weight,
    conv_bias,
    mix_weight,
    mix_bias,
    proj_weight,
    proj_bias,
    codebook,
    decode_weight,
    decode_bias,
    out_grad,
):
    canvases, rows, across, channels = latent_in.shape
    entries, size = codebook.shape
    count = canvases * across
    total = rows * count
    strips = plan.sizes["strip"]
    struct = jax.ShapeDtypeStruct
    flat_weight = conv_weight.reshape(3, 3 * channels, channels)

    def far_away(*arrays):
        return [pltpu.with_memory_space_constraint(array, pltpu.HBM) for array in arrays]

    def call(kernel, ins, outs, shapes, scratch=(), flops=0, aliases=None):
        return pl.pallas_call(
            kernel,
            in_specs=list(ins),
            out_specs=list(outs),
            out_shape=list(shapes),
            scratch_shapes=list(scratch),
            input_output_aliases=aliases or {},
            compiler_params=pltpu.CompilerParams(vmem_limit_bytes=vmem_bytes),
            cost_estimate=pl.CostEstimate(flops=flops, bytes_accessed=0, transcendentals=0),
        )

    def trade(mate, other):
        near = [(i, i ^ 1) for i in range(strips)]
        far = [(i, i + 1) for i in range(1, strips - 1, 2)]
        far += [(target, source) for source, target in far]
        return lax.ppermute(mate, "strip", near), lax.ppermute(other, "strip", far)

    edge_shape = struct((canvases, across, channels), low)
    edges = call(
        edge_kernel,
        [in_hbm],
        [in_vmem] * 2,
        [edge_shape] * 2,
        [pltpu.SemaphoreType.DMA((2,))],
    )(*far_away(latent_in))
    mate, other = trade(*edges)
    outs = [
        struct((rows, count, 2 * size), wide),
        struct((total, entries), low),
        struct((size, channels), wide),
        struct((1, channels), wide),
        struct(latent_in.shape, low),
        struct(crop_code.shape, crop_code.dtype),
        struct(flat_weight.shape, low),
        struct(mix_weight.shape, low),
    ]
    held = [
        pltpu.VMEM(code_index.shape, code_index.dtype),
        pltpu.VMEM((size, entries), low),
        pltpu.VMEM((size, channels), low),
        pltpu.VMEM((rows, canvases, across, channels), low),
        pltpu.SemaphoreType.DMA((rows + 7,)),
    ]
    term, picks, decode_weight_grad, decode_bias_grad, latent, crop, near_weight, near_mix = call(
        code_kernel,
        [in_hbm] * 8,
        [in_vmem] * 8,
        outs,
        held,
        flops=6 * total * channels * channels,
    )(
        *far_away(
            code_index,
            codebook.T,
            decode_weight,
            out_grad,
            latent_in,
            crop_code,
            flat_weight,
            mix_weight,
        )
    )
    slab_shape = struct((total + 2 * count, 3 * channels), low)
    flat = struct((total, channels), low)
    kept = [slab_shape, flat, flat, flat, flat, flat, struct((total, 2 * size), low)]
    kept += [struct((rows, count, channels), low), struct((8, channels), wide)]
    inner, outer = tuple(range(1, rows - 1)), tuple(sorted({0, rows - 1}))
    shared = [crop, latent, term, near_weight, conv_bias, near_mix, mix_bias, proj_weight.T, proj_bias]

    def block_rows(mine, halo, before):
        ins = [*shared, *halo, *before]
        first = len(ins) - len(before)
        return call(
            functools.partial(rows_kernel, mine),
            [in_vmem] * len(ins),
            [in_vmem] * len(kept),
            kept,
            flops=7 * len(mine) * total * channels * channels,
            aliases={first + i: i for i in range(len(before))},
        )(*ins)

    before = block_rows(inner, (), ()) if inner else ()
    before = block_rows(outer, (mate, other), before)
    slab, grad, up, down, second, stream, codes, branch_grad, sums = before
    edges = call(
        edge_rows_kernel,
        [in_vmem],
        [in_vmem] * 2,
        [struct((count, channels), low)] * 2,
    )(grad)

    def weight_half(mine, after):
        ins = [slab, grad, up, down, second, stream, codes, branch_grad, sums, picks]
        ins += [decode_weight_grad, decode_bias_grad]
        return call(
            functools.partial(weight_kernel, plan, mine),
            [in_vmem] * len(ins) + [anywhere],
            [in_vmem],
            [struct((plan.shards // 2, plan.piece_rows, channels), low)],
            [pltpu.VMEM((plan.half_rows, channels), low)],
            flops=10 * total * channels * channels,
        )(*ins, after)[0]

    send = weight_half(False, edges[0])
    keep = weight_half(True, send)

    def input_rows(mine, halo, after, *before):
        return call(
            functools.partial(input_kernel, mine),
            [in_vmem] * 7 + [anywhere] + [in_hbm] * len(before),
            [in_hbm],
            [pltpu.HBM(latent_in.shape, low)],
            [
                pltpu.VMEM(slab_shape.shape, low),
                pltpu.VMEM((len(mine), canvases, across, channels), low),
                pltpu.SemaphoreType.DMA((len(mine),)),
            ],
            flops=11 * total * channels * channels,
            aliases={8: 0} if before else {},
        )(crop, latent, grad, *halo, branch_grad, near_weight, after, *before)[0]

    arrays = [keep, plan.swap(send, plan.stages[0], 1)]
    after = []
    for place, stage in enumerate(plan.stages[1:]):
        parts = add_split(arrays, 2 ** len(stage), after)
        arrays = [parts[0]]
        arrays += [plan.swap(parts[i], stage, i) for i in reversed(range(1, len(parts)))]
        after = []
        if place == 0:
            latent_grad = input_rows(inner, edges, parts[0])
            after = far_away(latent_grad)
        elif place == 1:
            decoded = call(
                decoded_kernel,
                [in_vmem, in_vmem, in_vmem, anywhere],
                [pl.BlockSpec()],
                [pltpu.HBM(out_grad.shape, low)],
                flops=4 * total * channels * channels,
            )(term, decode_weight, decode_bias, parts[0])[0]
            after = far_away(decoded)
    pieces = add_split(arrays, 1, after)
    halo = trade(*[gate(edge, pieces[0]) for edge in edges])
    for stage in reversed(plan.stages[1:]):
        gathered = join(pieces, *halo) if len(pieces) > 1 else pieces[0]
        others = [plan.swap(gathered, stage, i) for i in range(1, 2 ** len(stage))]
        pieces = [gathered, *others]
    latent_grad = input_rows(outer, halo, gathered, latent_grad)
    done = far_away(latent_grad)
    pieces = [pieces[0], *[gate(piece, *done) for piece in pieces[1:]]]
    arrays = [*pieces, *[plan.swap(piece, plan.stages[0], 1) for piece in pieces]]

    results = call(
        functools.partial(final_kernel, plan, len(arrays), (channels, size, entries)),
        [in_vmem] * len(arrays),
        [pl.BlockSpec()] * 9,
        [
            struct((9 * channels, channels), wide),
            struct((1, channels), wide),
            struct((channels, channels), wide),
            struct((1, channels), wide),
            struct((size, channels), wide),
            struct((1, size), wide),
            struct((size, entries), wide),
            struct((size, channels), wide),
            struct((1, channels), wide),
        ],
        [pltpu.VMEM((2 * plan.half_rows, channels), low)],
    )(*arrays)
    return (
        decoded,
        latent_grad,
        results[0].reshape(3, 3, channels, channels),
        results[1].reshape(-1),
        results[2],
        results[3].reshape(-1),
        results[4].T,
        results[5].reshape(-1),
        results[6].T,
        results[7],
        results[8].reshape(-1),
    )


def solution(mesh):
    sizes = {axis: mesh.shape[axis] for axis in ("strip", "canvas")}
    shared = P("canvas", "strip", None, None)
    codes = P("canvas", "strip", None)

    def wrapped(*args):
        channels = args[0].shape[3]
        entries, size = args[9].shape
        others = 4 * channels + 2 * size + size * (entries // channels) + tile_rows
        plan = Plan(sizes, max(6 * channels, others))
        return jax.shard_map(
            functools.partial(per_device, plan),
            mesh=mesh,
            in_specs=(shared, codes, codes, *[P()] * 9, shared),
            out_specs=(shared, shared, *[P()] * 9),
            check_vma=False,
        )(*args)

    return wrapped
```

```python
import functools

import jax
import jax.numpy as jnp
from jax import lax
from jax.experimental import pallas as pl
from jax.experimental.pallas import tpu as pltpu
from jax.sharding import PartitionSpec as P

commit_weight = 0.25
low = jnp.bfloat16
wide = jnp.float32
bit_up, bit_left, bit_right, bit_down = 1, 3, 4, 6
tile_rows = 16
vmem_bytes = 28 * 2**20
in_hbm = pl.BlockSpec(memory_space=pltpu.HBM)
anywhere = pl.BlockSpec(memory_space=pl.ANY)
in_vmem = pl.BlockSpec(memory_space=pltpu.VMEM)


def mm(lhs, rhs):
    return jnp.dot(lhs, rhs, preferred_element_type=wide)


def mm_nt(lhs, rhs):
    return lax.dot_general(lhs, rhs, (((1,), (1,)), ((), ())), preferred_element_type=wide)


def mm_tn(lhs, rhs):
    return lax.dot_general(lhs, rhs, (((0,), (0,)), ((), ())), preferred_element_type=wide)


def sigmoid(values):
    return 0.5 * jnp.tanh(0.5 * values) + 0.5


def code_columns(code_ref):
    canvases, rows, across = code_ref.shape
    flat = code_ref[...].reshape(canvases * rows, across)
    extra = -across % 128
    if extra:
        flat = jnp.concatenate([flat, jnp.zeros((canvases * rows, extra), flat.dtype)], axis=1)
    return flat.T[:across]


def row_codes(columns, row, canvases, rows, lanes):
    pieces = [
        jnp.broadcast_to(
            columns[:, n * rows + row : n * rows + row + 1], (columns.shape[0], lanes)
        )
        for n in range(canvases)
    ]
    return jnp.concatenate(pieces, axis=0)


def chunks(count):
    return [(at, pl.ds(at, tile_rows)) for at in range(0, count, tile_rows)]


def pick(codes, bit, values):
    chosen = (codes & 2**bit) != 0
    parts = []
    for at in range(0, values.shape[1], 128):
        part = values[:, at : at + 128]
        parts.append(jnp.where(chosen, part, jnp.zeros_like(part)))
    return jnp.concatenate(parts, axis=1)


def store_slab(slab_ref, at, codes, values):
    count = codes.shape[0]
    channels = slab_ref.shape[1] // 3
    steps = chunks(count)
    held = [values(start) for start, _ in steps]
    for place, (start, _) in enumerate(steps):
        here = held[place]
        span = pl.ds(at + start, tile_rows)
        spots = codes[start : start + tile_rows]
        before = held[place - 1][tile_rows - 8 :]
        after = held[(place + 1) % len(steps)][:8]
        left = pltpu.roll(jnp.concatenate([before, here], axis=0), 1, 0)[8:]
        right = jnp.concatenate([here, after], axis=0)
        right = pltpu.roll(right, right.shape[0] - 1, 0)[:tile_rows]
        slab_ref[span, :channels] = pick(spots, bit_left, left).astype(low)
        slab_ref[span, channels : 2 * channels] = here.astype(low)
        slab_ref[span, 2 * channels :] = pick(spots, bit_right, right).astype(low)


def edge_kernel(latent_ref, mate_ref, other_ref, sems):
    rows = latent_ref.shape[1]
    odd = lax.axis_index("strip") % 2
    edge = (rows - 1) * (1 - odd)
    near = pltpu.make_async_copy(latent_ref.at[:, edge], mate_ref, sems.at[0])
    far = pltpu.make_async_copy(latent_ref.at[:, rows - 1 - edge], other_ref, sems.at[1])
    near.start()
    far.start()
    near.wait()
    far.wait()


def code_kernel(
    index_hbm,
    codebook_hbm,
    decode_weight_hbm,
    out_grad_hbm,
    latent_hbm,
    crop_hbm,
    conv_weight_hbm,
    mix_weight_hbm,
    term_ref,
    picks_ref,
    weight_grad_ref,
    bias_grad_ref,
    latent_ref,
    crop_ref,
    conv_weight_ref,
    mix_weight_ref,
    index_ref,
    codebook_ref,
    decode_weight_ref,
    out_grad_ref,
    sems,
):
    canvases, rows, across = index_ref.shape
    size, entries = codebook_ref.shape
    channels = decode_weight_ref.shape[1]
    count = canvases * across
    pairs = [
        (index_hbm, index_ref),
        (codebook_hbm, codebook_ref),
        (decode_weight_hbm, decode_weight_ref),
    ]
    pairs += [(out_grad_hbm.at[:, row], out_grad_ref.at[row]) for row in range(rows)]
    pairs += [
        (latent_hbm, latent_ref),
        (crop_hbm, crop_ref),
        (conv_weight_hbm, conv_weight_ref),
        (mix_weight_hbm, mix_weight_ref),
    ]
    copies = [
        pltpu.make_async_copy(source, target, sems.at[place])
        for place, (source, target) in enumerate(pairs)
    ]
    for copy in copies:
        copy.start()
    for copy in copies[:3]:
        copy.wait()
    codebook = codebook_ref[...]
    both = jnp.concatenate([codebook * low(-0.5), codebook * low(2.0)], axis=0)
    weight = decode_weight_ref[...]
    weight_top = jnp.concatenate([weight, jnp.zeros_like(weight)], axis=0)
    columns = code_columns(index_ref)
    lanes = lax.broadcasted_iota(jnp.int32, (tile_rows, 128), 1)
    for row in range(rows):
        codes = row_codes(columns, row, canvases, rows, 128)
        for start, _ in chunks(count):
            near = codes[start : start + tile_rows]
            for at in range(0, entries, 128):
                chosen = lanes + at == near
                part = jnp.where(chosen, 1.0, 0.0).astype(low)
                picks_ref[pl.ds(row * count + start, tile_rows), at : at + 128] = part
    term = mm_nt(picks_ref[...], both)
    for copy in copies[3 : 3 + rows]:
        copy.wait()
    grad = out_grad_ref[...].reshape(rows * count, channels)
    term = term + mm_nt(grad, weight_top)
    term_ref[...] = term.reshape(term_ref.shape)
    weight_grad_ref[...] = 0.5 * mm_tn(term.astype(low), grad)[size:]
    bias_sum = None
    for start, _ in chunks(rows * count):
        part = grad[start : start + tile_rows].astype(wide)
        part = part[:8] + part[8:]
        bias_sum = part if bias_sum is None else bias_sum + part
    bias_grad_ref[...] = jnp.sum(bias_sum, axis=0, keepdims=True)
    for copy in copies[3 + rows :]:
        copy.wait()


def decoded_kernel(term_ref, decode_weight_ref, decode_bias_ref, after_ref, decoded_ref):
    canvases, rows, across, channels = decoded_ref.shape
    weight = decode_weight_ref[...] * low(0.5)
    weight = jnp.concatenate([jnp.zeros_like(weight), weight], axis=0)
    bias = decode_bias_ref[...].astype(wide).reshape(1, channels)
    for row in range(rows):
        decoded = (mm(term_ref[row].astype(low), weight) + bias).astype(low)
        decoded_ref[:, row] = decoded.reshape(canvases, across, channels)


def rows_kernel(
    mine,
    crop_ref,
    latent_ref,
    term_ref,
    conv_weight_ref,
    conv_bias_ref,
    mix_weight_ref,
    mix_bias_ref,
    proj_weight_ref,
    proj_bias_ref,
    *refs,
):
    outs = refs[-9:]
    slab_ref, grad_ref, up_ref, down_ref, second_ref, stream_ref, codes_ref = outs[:7]
    branch_grad_ref, sums_ref = outs[7:]
    canvases, rows, across = crop_ref.shape
    channels = latent_ref.shape[3]
    size = proj_weight_ref.shape[0]
    count = canvases * across
    odd = lax.axis_index("strip") % 2
    columns = code_columns(crop_ref)
    codes = [row_codes(columns, row, canvases, rows, 128) for row in range(rows)]

    def silu(values):
        values = values.astype(wide)
        return values * sigmoid(values)

    def own(row):
        def values(at):
            return silu(latent_ref[at // across, row, pl.ds(at % across, tile_rows)])

        return values

    def beside(first_ref, second_ref, swap):
        def values(at):
            span = pl.ds(at % across, tile_rows)
            one, two = first_ref[at // across, span], second_ref[at // across, span]
            return silu(jnp.where(swap, one, two))

        return values

    inner = 0 not in mine or rows == 1
    if inner or rows <= 2:
        for row in range(rows):
            store_slab(slab_ref, (row + 1) * count, codes[row], own(row))
    if 0 in mine:
        mate_ref, other_ref = refs[:2]
        store_slab(slab_ref, 0, codes[0], beside(mate_ref, other_ref, odd == 1))
        end = (rows + 1) * count
        store_slab(slab_ref, end, codes[rows - 1], beside(other_ref, mate_ref, odd == 1))

    proj = proj_weight_ref[...]
    proj_both = jnp.concatenate([proj * low(2 * commit_weight), proj * low(-2.0)], axis=0)
    proj_top = jnp.concatenate([proj, jnp.zeros_like(proj)], axis=0)
    conv_bias = conv_bias_ref[...].astype(wide).reshape(1, channels)
    mix_bias = mix_bias_ref[...].astype(wide).reshape(1, channels)
    proj_bias = proj_bias_ref[...].astype(wide).reshape(1, size)
    proj_bias = jnp.concatenate([2 * commit_weight * proj_bias, -2.0 * proj_bias], axis=1)
    sums = [None, None, None]
    steps = chunks(count)

    def add_to(place, values):
        values = values[:8] + values[8:]
        sums[place] = values if sums[place] is None else sums[place] + values

    held = None
    for row, was in zip((*mine, None), (None, *mine), strict=True):
        if row is not None:
            at = row * count
            conv_mid = mm(slab_ref[pl.ds(at + count, count)], conv_weight_ref[1])
        if was is not None:
            back = was * count
            slope = held
            branch = mm(second_ref[pl.ds(back, count)], mix_weight_ref[...])
            for start, _ in steps:
                span = pl.ds(back + start, tile_rows)
                latent = latent_ref[start // across, was, pl.ds(start % across, tile_rows)]
                part = latent.astype(wide) + (branch[start : start + tile_rows] + mix_bias)
                stream_ref[span] = part.astype(low)
        if row is not None:
            conv_up = mm(slab_ref[pl.ds(at, count)], conv_weight_ref[0])
        if was is not None:
            code = mm_nt(stream_ref[pl.ds(back, count)], proj_both)
            for start, near in steps:
                part = code[start : start + tile_rows] + (term_ref[was, near] + proj_bias)
                codes_ref[pl.ds(back + start, tile_rows)] = part.astype(low)
                add_to(2, part)
        if row is not None:
            conv_down = mm(slab_ref[pl.ds(at + 2 * count, count)], conv_weight_ref[2])
        if was is not None:
            branch_grad = mm(codes_ref[pl.ds(back, count)], proj_top)
            for start, near in steps:
                part = branch_grad[start : start + tile_rows]
                branch_grad_ref[was, near] = part.astype(low)
                add_to(1, part)
        if row is not None:
            held = []
            for start, _ in steps:
                some = slice(start, start + tile_rows)
                conv = pick(codes[row][some], bit_up, conv_up[some])
                conv = conv + pick(codes[row][some], bit_down, conv_down[some])
                conv = (conv + conv_mid[some]) + conv_bias
                gate = sigmoid(conv)
                second_ref[pl.ds(at + start, tile_rows)] = (conv * gate).astype(low)
                held.append(gate * (1.0 + conv * (1.0 - gate)))
        if was is not None:
            grad = mm_nt(branch_grad_ref[was], mix_weight_ref[...])
            for place, (start, _) in enumerate(steps):
                some = slice(start, start + tile_rows)
                span = pl.ds(back + start, tile_rows)
                part = grad[some] * slope[place]
                grad_ref[span] = part.astype(low)
                up_ref[span] = pick(codes[was][some], bit_up, part).astype(low)
                down_ref[span] = pick(codes[was][some], bit_down, part).astype(low)
                add_to(0, part)
    sums = [jnp.sum(values, axis=0, keepdims=True) for values in sums]
    sums[2] = jnp.concatenate([sums[2]] * (channels // sums[2].shape[1]), axis=1)
    blank = jnp.zeros((sums_ref.shape[0] - 3, channels), wide)
    sums = jnp.concatenate([*sums, blank], axis=0)
    if len(refs) > 9 + 2 * (0 in mine):
        sums = sums + refs[-10][...]
    sums_ref[...] = sums


def edge_rows_kernel(grad_ref, mate_ref, other_ref):
    count = mate_ref.shape[0]
    odd = lax.axis_index("strip") % 2
    first, last = grad_ref[pl.ds(0, count)], grad_ref[pl.ds(grad_ref.shape[0] - count, count)]
    mate_ref[...] = jnp.where(odd == 1, first, last)
    other_ref[...] = jnp.where(odd == 1, last, first)


def weight_kernel(
    plan,
    mine,
    slab_ref,
    grad_ref,
    up_ref,
    down_ref,
    second_ref,
    stream_ref,
    codes_ref,
    branch_grad_ref,
    sums_ref,
    picks_ref,
    decode_weight_grad_ref,
    decode_bias_grad_ref,
    after_ref,
    out_ref,
    message_ref,
):
    total, channels = grad_ref.shape
    rows, count, _ = branch_grad_ref.shape
    size = decode_weight_grad_ref.shape[0]
    entries = picks_ref.shape[1]
    triple = 3 * channels
    half = plan.half
    core = lax.axis_index("strip") % 2
    wanted = core if mine else 1 - core
    place = plan.place(wanted)

    def step(row_step, weighted_ref):
        span = pl.ds(row_step * count, total)
        return mm_tn(slab_ref[span], weighted_ref[...]).astype(low)

    def fill(parts):
        at = 0
        for part in parts:
            message_ref[pl.ds(at, part.shape[0])] = part
            at += part.shape[0]
        rest = message_ref.shape[0] - at
        if rest:
            message_ref[pl.ds(at, rest)] = jnp.zeros((rest, channels), low)

    @pl.when(wanted == 0)
    def _():
        fill([step(0, up_ref), step(1, grad_ref)])

    @pl.when(wanted == 1)
    def _():
        code_part = mm_tn(codes_ref[...], picks_ref[...])[size:].astype(low)
        sums = sums_ref[...]
        biases = [sums[0:1], sums[1:2], decode_bias_grad_ref[...], sums[2:3]]
        biases.append(jnp.zeros((tile_rows - len(biases), channels), wide))
        fill(
            [
                step(2, down_ref),
                mm_tn(second_ref[...], branch_grad_ref[...].reshape(total, channels)).astype(low),
                decode_weight_grad_ref[...].astype(low),
                mm_tn(codes_ref[...], stream_ref[...])[:size].astype(low),
                *[code_part[:, i : i + channels] for i in range(0, entries, channels)],
                jnp.concatenate(biases, axis=0).astype(low),
            ]
        )

    for piece in range(half):
        rows_of = pl.ds(piece * plan.piece_rows, plan.piece_rows)
        out_ref[piece ^ place] = message_ref[rows_of]


def input_kernel(
    mine,
    crop_ref,
    latent_ref,
    grad_ref,
    mate_ref,
    other_ref,
    branch_grad_ref,
    conv_weight_ref,
    after_ref,
    *refs,
):
    latent_grad_ref, slab_ref, out_ref, sems = refs[-4:]
    canvases, rows, across = crop_ref.shape
    channels = latent_ref.shape[3]
    count = canvases * across
    odd = lax.axis_index("strip") % 2
    columns = code_columns(crop_ref)
    codes = [row_codes(columns, row, canvases, rows, 128) for row in range(rows)]

    steps = chunks(count)

    def own(row):
        def values(at):
            return grad_ref[pl.ds(row * count + at, tile_rows)].astype(wide)

        return values

    def beside(first_ref, second_ref, swap):
        def values(at):
            span = pl.ds(at, tile_rows)
            return jnp.where(swap, first_ref[span], second_ref[span]).astype(wide)

        return values

    for row in range(rows):
        if any(abs(row - near) < 2 for near in mine):
            store_slab(slab_ref, (row + 1) * count, codes[row], own(row))
    if 0 in mine:
        store_slab(slab_ref, 0, codes[0], beside(mate_ref, other_ref, odd == 1))
    if rows - 1 in mine:
        end = (rows + 1) * count
        store_slab(slab_ref, end, codes[rows - 1], beside(other_ref, mate_ref, odd == 1))

    copies = []
    for place, row in enumerate(mine):
        spreads = []
        for row_step in range(3):
            part = None
            for col_step in range(3):
                weight = conv_weight_ref[
                    2 - row_step, (2 - col_step) * channels : (3 - col_step) * channels
                ]
                span = pl.ds((row + row_step) * count, count)
                term = mm_nt(
                    slab_ref[span, col_step * channels : (col_step + 1) * channels], weight
                )
                part = term if part is None else part + term
            spreads.append(part)
        for start, near in steps:
            some = slice(start, start + tile_rows)
            spread = pick(codes[row][some], bit_up, spreads[0][some])
            spread = spread + pick(codes[row][some], bit_down, spreads[2][some])
            spread = spread + spreads[1][some]
            inside = pl.ds(start % across, tile_rows)
            latent = latent_ref[start // across, row, inside].astype(wide)
            gate = sigmoid(latent)
            slope = gate * (1.0 + latent * (1.0 - gate))
            out = branch_grad_ref[row, near].astype(wide) + spread * slope
            out_ref[place, start // across, inside] = out.astype(low)
        copies.append(
            pltpu.make_async_copy(out_ref.at[place], latent_grad_ref.at[:, row], sems.at[place])
        )
        copies[-1].start()
    for copy in copies:
        copy.wait()


class Plan:
    def __init__(self, sizes, half_rows):
        self.sizes = sizes
        bits = {axis: [(axis, b) for b in range(size.bit_length() - 1)] for axis, size in sizes.items()}
        strip, canvas = bits["strip"], bits["canvas"]
        near, far = [*canvas[:1], *strip[1:2]], strip[2:4][::-1]
        rest = [*strip[4:], *canvas[1:]]
        rest = [rest[i : i + 2] for i in range(0, len(rest), 2)]
        even, odd = [near, far, *rest], [far, near, *rest]
        if len(near) != len(far):
            odd = even
        self.stages = [tuple(zip(*pair, strict=True)) for pair in zip(even, odd, strict=True) if pair[0]]
        self.core = ((("strip", 0), ("strip", 0)),)
        self.half = sizes["strip"] * sizes["canvas"] // 2
        self.piece_rows = -(-half_rows // (self.half * tile_rows)) * tile_rows
        self.half_rows = self.half * self.piece_rows

    def place(self, core):
        number = 0
        for stage in self.stages:
            for spots in stage:
                even, odd = [(lax.axis_index(axis) // 2**bit) % 2 for axis, bit in spots]
                number = number * 2 + (even if spots[0] == spots[1] else jnp.where(core == 0, even, odd))
        return number

    def swap(self, values, stage, step):
        width = self.sizes["canvas"]
        pairs = []
        for strip in range(self.sizes["strip"]):
            change = {"strip": 0, "canvas": 0}
            for place, spots in enumerate(reversed(stage)):
                if step >> place & 1:
                    axis, bit = spots[strip % 2]
                    change[axis] |= 1 << bit
            for canvas in range(width):
                target = (strip ^ change["strip"]) * width + (canvas ^ change["canvas"])
                pairs.append((strip * width + canvas, target))
        return lax.ppermute(values, ("strip", "canvas"), pairs)


def add_kernel(count, after, *refs):
    ins, outs = refs[:count], refs[count + after :]
    depth = outs[0].shape[0]
    for place, out_ref in enumerate(outs):
        span = pl.ds(place * depth, depth)
        total = ins[0][span].astype(wide)
        for ref in ins[1:]:
            total = total + ref[span].astype(wide)
        out_ref[...] = total.astype(low)


def add_split(arrays, parts, after=()):
    depth, rows, channels = arrays[0].shape
    shape = jax.ShapeDtypeStruct((depth // parts, rows, channels), low)
    return pl.pallas_call(
        functools.partial(add_kernel, len(arrays), len(after)),
        in_specs=[in_vmem] * len(arrays) + [anywhere] * len(after),
        out_specs=[in_vmem] * parts,
        out_shape=[shape] * parts,
        compiler_params=pltpu.CompilerParams(vmem_limit_bytes=vmem_bytes),
    )(*arrays, *after)


def gate_kernel(*refs):
    pass


def gate(array, *after):
    return pl.pallas_call(
        gate_kernel,
        in_specs=[in_vmem] + [anywhere] * len(after),
        out_specs=in_vmem,
        out_shape=jax.ShapeDtypeStruct(array.shape, array.dtype),
        input_output_aliases={0: 0},
        compiler_params=pltpu.CompilerParams(vmem_limit_bytes=vmem_bytes),
    )(array, *after)


def join_kernel(count, *refs):
    at = 0
    for ref in refs[:count]:
        refs[-1][pl.ds(at, ref.shape[0])] = ref[...]
        at += ref.shape[0]


def join(arrays, *after):
    depth, rows, channels = arrays[0].shape
    return pl.pallas_call(
        functools.partial(join_kernel, len(arrays)),
        in_specs=[in_vmem] * len(arrays) + [anywhere] * len(after),
        out_specs=in_vmem,
        out_shape=jax.ShapeDtypeStruct((depth * len(arrays), rows, channels), low),
        compiler_params=pltpu.CompilerParams(vmem_limit_bytes=vmem_bytes),
    )(*arrays, *after)


def final_kernel(plan, count, sizes, *refs):
    ins, outs, gathered_ref = refs[:count], refs[count:-1], refs[-1]
    channels, size, entries = sizes
    core = lax.axis_index("strip") % 2
    at = 0
    for ref in ins:
        half = core if at < plan.half else 1 - core
        place = plan.place(half)
        for piece in range(ref.shape[0]):
            shard = half * plan.half + (place ^ at % plan.half)
            start = pl.multiple_of(shard * plan.piece_rows, plan.piece_rows)
            gathered_ref[pl.ds(start, plan.piece_rows)] = ref[piece]
            at += 1
    conv_ref, conv_bias_ref, mix_ref, mix_bias_ref, proj_ref, proj_bias_ref = outs[:6]
    codebook_ref, decode_ref, decode_bias_ref = outs[6:]
    triple = 3 * channels
    conv_ref[pl.ds(0, 2 * triple)] = gathered_ref[pl.ds(0, 2 * triple)].astype(wide)
    at = plan.half_rows
    conv_ref[pl.ds(2 * triple, triple)] = gathered_ref[pl.ds(at, triple)].astype(wide)
    at += triple
    mix_ref[...] = gathered_ref[pl.ds(at, channels)].astype(wide)
    at += channels
    decode_ref[...] = gathered_ref[pl.ds(at, size)].astype(wide)
    at += size
    proj_ref[...] = gathered_ref[pl.ds(at, size)].astype(wide)
    at += size
    for piece in range(entries // channels):
        part = gathered_ref[pl.ds(at, size)].astype(wide)
        codebook_ref[:, piece * channels : (piece + 1) * channels] = part
        at += size
    biases = gathered_ref[pl.ds(at, tile_rows)].astype(wide)
    conv_bias_ref[...] = biases[0:1]
    mix_bias_ref[...] = biases[1:2]
    decode_bias_ref[...] = biases[2:3]
    proj_bias_ref[...] = biases[3:4, :size]


def per_device(
    plan,
    latent_in,
    crop_code,
    code_index,
    conv_weight,
    conv_bias,
    mix_weight,
    mix_bias,
    proj_weight,
    proj_bias,
    codebook,
    decode_weight,
    decode_bias,
    out_grad,
):
    canvases, rows, across, channels = latent_in.shape
    entries, size = codebook.shape
    count = canvases * across
    total = rows * count
    strips = plan.sizes["strip"]
    struct = jax.ShapeDtypeStruct
    flat_weight = conv_weight.reshape(3, 3 * channels, channels)

    def far_away(*arrays):
        return [pltpu.with_memory_space_constraint(array, pltpu.HBM) for array in arrays]

    def call(kernel, ins, outs, shapes, scratch=(), flops=0, aliases=None):
        return pl.pallas_call(
            kernel,
            in_specs=list(ins),
            out_specs=list(outs),
            out_shape=list(shapes),
            scratch_shapes=list(scratch),
            input_output_aliases=aliases or {},
            compiler_params=pltpu.CompilerParams(vmem_limit_bytes=vmem_bytes),
            cost_estimate=pl.CostEstimate(flops=flops, bytes_accessed=0, transcendentals=0),
        )

    def trade(mate, other):
        near = [(i, i ^ 1) for i in range(strips)]
        far = [(i, i + 1) for i in range(1, strips - 1, 2)]
        far += [(target, source) for source, target in far]
        return lax.ppermute(mate, "strip", near), lax.ppermute(other, "strip", far)

    edge_shape = struct((canvases, across, channels), low)
    edges = call(
        edge_kernel,
        [in_hbm],
        [in_vmem] * 2,
        [edge_shape] * 2,
        [pltpu.SemaphoreType.DMA((2,))],
    )(*far_away(latent_in))
    mate, other = trade(*edges)
    outs = [
        struct((rows, count, 2 * size), wide),
        struct((total, entries), low),
        struct((size, channels), wide),
        struct((1, channels), wide),
        struct(latent_in.shape, low),
        struct(crop_code.shape, crop_code.dtype),
        struct(flat_weight.shape, low),
        struct(mix_weight.shape, low),
    ]
    held = [
        pltpu.VMEM(code_index.shape, code_index.dtype),
        pltpu.VMEM((size, entries), low),
        pltpu.VMEM((size, channels), low),
        pltpu.VMEM((rows, canvases, across, channels), low),
        pltpu.SemaphoreType.DMA((rows + 7,)),
    ]
    term, picks, decode_weight_grad, decode_bias_grad, latent, crop, near_weight, near_mix = call(
        code_kernel,
        [in_hbm] * 8,
        [in_vmem] * 8,
        outs,
        held,
        flops=6 * total * channels * channels,
    )(
        *far_away(
            code_index,
            codebook.T,
            decode_weight,
            out_grad,
            latent_in,
            crop_code,
            flat_weight,
            mix_weight,
        )
    )
    slab_shape = struct((total + 2 * count, 3 * channels), low)
    flat = struct((total, channels), low)
    kept = [slab_shape, flat, flat, flat, flat, flat, struct((total, 2 * size), low)]
    kept += [struct((rows, count, channels), low), struct((8, channels), wide)]
    inner, outer = tuple(range(1, rows - 1)), tuple(sorted({0, rows - 1}))
    shared = [crop, latent, term, near_weight, conv_bias, near_mix, mix_bias, proj_weight.T, proj_bias]

    def block_rows(mine, halo, before):
        ins = [*shared, *halo, *before]
        first = len(ins) - len(before)
        return call(
            functools.partial(rows_kernel, mine),
            [in_vmem] * len(ins),
            [in_vmem] * len(kept),
            kept,
            flops=7 * len(mine) * total * channels * channels,
            aliases={first + i: i for i in range(len(before))},
        )(*ins)

    before = block_rows(inner, (), ()) if inner else ()
    before = block_rows(outer, (mate, other), before)
    slab, grad, up, down, second, stream, codes, branch_grad, sums = before
    edges = call(
        edge_rows_kernel,
        [in_vmem],
        [in_vmem] * 2,
        [struct((count, channels), low)] * 2,
    )(grad)

    def weight_half(mine, after):
        ins = [slab, grad, up, down, second, stream, codes, branch_grad, sums, picks]
        ins += [decode_weight_grad, decode_bias_grad]
        return call(
            functools.partial(weight_kernel, plan, mine),
            [in_vmem] * len(ins) + [anywhere],
            [in_vmem],
            [struct((plan.half, plan.piece_rows, channels), low)],
            [pltpu.VMEM((plan.half_rows, channels), low)],
            flops=10 * total * channels * channels,
        )(*ins, after)[0]

    send = weight_half(False, edges[0])
    keep = weight_half(True, send)

    def input_rows(mine, halo, after, *before):
        return call(
            functools.partial(input_kernel, mine),
            [in_vmem] * 7 + [anywhere] + [in_hbm] * len(before),
            [in_hbm],
            [pltpu.HBM(latent_in.shape, low)],
            [
                pltpu.VMEM(slab_shape.shape, low),
                pltpu.VMEM((len(mine), canvases, across, channels), low),
                pltpu.SemaphoreType.DMA((len(mine),)),
            ],
            flops=11 * total * channels * channels,
            aliases={8: 0} if before else {},
        )(crop, latent, grad, *halo, branch_grad, near_weight, after, *before)[0]

    arrays = [keep, plan.swap(send, plan.core, 1)]
    after = []
    for place, stage in enumerate(plan.stages):
        parts = add_split(arrays, 2 ** len(stage), after)
        arrays = [parts[0]]
        arrays += [plan.swap(parts[i], stage, i) for i in reversed(range(1, len(parts)))]
        after = []
        if place == 0:
            latent_grad = input_rows(inner, edges, parts[0])
            after = far_away(latent_grad)
        elif place == 1:
            halo = trade(*[gate(edge, parts[0]) for edge in edges])
            decoded = call(
                decoded_kernel,
                [in_vmem, in_vmem, in_vmem, anywhere],
                [pl.BlockSpec()],
                [pltpu.HBM(out_grad.shape, low)],
                flops=4 * total * channels * channels,
            )(term, decode_weight, decode_bias, parts[0])[0]
            after = far_away(decoded)
    pieces = add_split(arrays, 1, after)
    for stage in reversed(plan.stages):
        gathered = join(pieces) if len(pieces) > 1 else pieces[0]
        others = [plan.swap(gathered, stage, i) for i in range(1, 2 ** len(stage))]
        pieces = [gathered, *others]
    latent_grad = input_rows(outer, halo, gathered, latent_grad)
    done = far_away(latent_grad)
    pieces = [pieces[0], *[gate(piece, *done) for piece in pieces[1:]]]
    arrays = [*pieces, *[plan.swap(piece, plan.core, 1) for piece in pieces]]

    results = call(
        functools.partial(final_kernel, plan, len(arrays), (channels, size, entries)),
        [in_vmem] * len(arrays),
        [pl.BlockSpec()] * 9,
        [
            struct((9 * channels, channels), wide),
            struct((1, channels), wide),
            struct((channels, channels), wide),
            struct((1, channels), wide),
            struct((size, channels), wide),
            struct((1, size), wide),
            struct((size, entries), wide),
            struct((size, channels), wide),
            struct((1, channels), wide),
        ],
        [pltpu.VMEM((2 * plan.half_rows, channels), low)],
    )(*arrays)
    return (
        decoded,
        latent_grad,
        results[0].reshape(3, 3, channels, channels),
        results[1].reshape(-1),
        results[2],
        results[3].reshape(-1),
        results[4].T,
        results[5].reshape(-1),
        results[6].T,
        results[7],
        results[8].reshape(-1),
    )


def solution(mesh):
    sizes = {axis: mesh.shape[axis] for axis in ("strip", "canvas")}
    shared = P("canvas", "strip", None, None)
    codes = P("canvas", "strip", None)

    def wrapped(*args):
        channels = args[0].shape[3]
        entries, size = args[9].shape
        others = 4 * channels + 2 * size + size * (entries // channels) + tile_rows
        plan = Plan(sizes, max(6 * channels, others))
        return jax.shard_map(
            functools.partial(per_device, plan),
            mesh=mesh,
            in_specs=(shared, codes, codes, *[P()] * 9, shared),
            out_specs=(shared, shared, *[P()] * 9),
            check_vma=False,
        )(*args)

    return wrapped
```

```python
import functools

import jax
import jax.numpy as jnp
from jax import lax
from jax.experimental import pallas as pl
from jax.experimental.pallas import tpu as pltpu
from jax.sharding import PartitionSpec as P

commit_weight = 0.25
low = jnp.bfloat16
wide = jnp.float32
bits = (1, 3, 4, 6)
up_plane, left_plane, right_plane, down_plane = range(4)
tile_rows = 16
vmem_bytes = 20 * 2**20
in_hbm = pl.BlockSpec(memory_space=pltpu.HBM)
anywhere = pl.BlockSpec(memory_space=pl.ANY)
in_vmem = pl.BlockSpec(memory_space=pltpu.VMEM)


def mm(lhs, rhs):
    return jnp.dot(lhs, rhs, preferred_element_type=wide)


def mm_nt(lhs, rhs):
    return lax.dot_general(lhs, rhs, (((1,), (1,)), ((), ())), preferred_element_type=wide)


def mm_tn(lhs, rhs):
    return lax.dot_general(lhs, rhs, (((0,), (0,)), ((), ())), preferred_element_type=wide)


def silu(values):
    half = 0.5 * values.astype(wide)
    return half * (1.0 + jnp.tanh(half))


def silu_slopes(half):
    turn = jnp.tanh(half)
    more = 1.0 + turn
    return half * more, more * (1.0 + half * (1.0 - turn))


def code_columns(code_ref):
    canvases, rows, across = code_ref.shape
    flat = code_ref[...].reshape(canvases * rows, across)
    extra = -across % 128
    if extra:
        flat = jnp.concatenate([flat, jnp.zeros((canvases * rows, extra), flat.dtype)], axis=1)
    return flat.T[:across]


def row_codes(columns, row, canvases, rows, lanes):
    pieces = [
        jnp.broadcast_to(
            columns[:, n * rows + row : n * rows + row + 1], (columns.shape[0], lanes)
        )
        for n in range(canvases)
    ]
    return jnp.concatenate(pieces, axis=0)


def chunks(count):
    return [(at, pl.ds(at, tile_rows)) for at in range(0, count, tile_rows)]


def masked(values, masks):
    return values * jnp.concatenate([masks] * (values.shape[1] // masks.shape[1]), axis=1)


def store_slab(slab_ref, at, left, right, values):
    channels = slab_ref.shape[1] // 3
    eight = tile_rows // 2
    place = lax.broadcasted_iota(jnp.int32, (eight, channels), 0)
    steps = chunks(left.count)

    def part(number):
        here = values(steps[number][0])
        halves = here[:eight], here[eight:]
        later = [pltpu.roll(half, 1, 0) for half in halves]
        sooner = [pltpu.roll(half, eight - 1, 0) for half in halves]
        return here, later, sooner

    now = part(0)
    before = now[1][1]
    for number, (start, _) in enumerate(steps):
        new = part(number + 1) if number + 1 < len(steps) else now
        here, later, sooner = now
        span = pl.ds(at + start, tile_rows)
        shifted = [
            jnp.where(place == 0, before, later[0]),
            jnp.where(place == 0, later[0], later[1]),
        ]
        shifted = jnp.concatenate(shifted, axis=0).astype(low)
        slab_ref[span, :channels] = masked(shifted, left(start))
        slab_ref[span, channels : 2 * channels] = here.astype(low)
        shifted = [
            jnp.where(place == eight - 1, sooner[1], sooner[0]),
            jnp.where(place == eight - 1, new[2][0], sooner[1]),
        ]
        shifted = jnp.concatenate(shifted, axis=0).astype(low)
        slab_ref[span, 2 * channels :] = masked(shifted, right(start))
        before = later[1]
        now = new


class Masks:
    def __init__(self, masks_ref, plane, at, count):
        self.masks_ref, self.plane, self.at, self.count = masks_ref, plane, at, count

    def __call__(self, start):
        at = self.at + start
        if not isinstance(at, int):
            at = pl.multiple_of(at, tile_rows)
        return self.masks_ref[self.plane, pl.ds(at, tile_rows)]


class Tape:
    def __init__(self):
        self.steps = []

    def add(self, unit, cost, after, step):
        self.steps.append((unit, cost, [a for a in after if a is not None], step))
        return len(self.steps) - 1

    def play(self):
        free = {"mxu": 0.0, "vpu": 0.0}
        lag = {"mxu": 0.1, "vpu": 0.02}
        ends = {}
        left = list(range(len(self.steps)))
        while left:
            best = None
            for number in left:
                unit, _, after, _ = self.steps[number]
                if all(a in ends for a in after):
                    start = max([free[unit], *[ends[a] for a in after]])
                    if best is None or (start, number) < best:
                        best = (start, number)
            start, number = best
            unit, cost, _, step = self.steps[number]
            free[unit] = start + cost
            ends[number] = start + cost + lag[unit]
            left.remove(number)
            step()


def edge_kernel(latent_ref, crop_hbm, mate_ref, other_ref, masks_ref, crop_ref, sems):
    canvases, rows, across = crop_ref.shape
    count = canvases * across
    odd = lax.axis_index("strip") % 2
    edge = (rows - 1) * (1 - odd)
    codes = pltpu.make_async_copy(crop_hbm, crop_ref, sems.at[0])
    near = pltpu.make_async_copy(latent_ref.at[:, edge], mate_ref, sems.at[1])
    far = pltpu.make_async_copy(latent_ref.at[:, rows - 1 - edge], other_ref, sems.at[2])
    codes.start()
    near.start()
    far.start()
    codes.wait()
    columns = code_columns(crop_ref)
    for row in range(rows):
        here = row_codes(columns, row, canvases, rows, 128)
        for start, _ in chunks(count):
            some = here[start : start + tile_rows]
            span = pl.ds(row * count + start, tile_rows)
            for plane, bit in enumerate(bits):
                masks_ref[plane, span] = jnp.where((some & 2**bit) != 0, 1.0, 0.0).astype(low)
    near.wait()
    far.wait()


def code_kernel(
    index_hbm,
    codebook_hbm,
    decode_weight_hbm,
    out_grad_hbm,
    latent_hbm,
    conv_weight_hbm,
    mix_weight_hbm,
    term_ref,
    picks_ref,
    weight_grad_ref,
    bias_grad_ref,
    latent_ref,
    conv_weight_ref,
    mix_weight_ref,
    index_ref,
    codebook_ref,
    decode_weight_ref,
    out_grad_ref,
    sems,
):
    canvases, rows, across = index_ref.shape
    size, entries = codebook_ref.shape
    channels = decode_weight_ref.shape[1]
    count = canvases * across
    pairs = [
        (index_hbm, index_ref),
        (codebook_hbm, codebook_ref),
        (decode_weight_hbm, decode_weight_ref),
    ]
    pairs += [(out_grad_hbm.at[:, row], out_grad_ref.at[row]) for row in range(rows)]
    pairs += [
        (conv_weight_hbm, conv_weight_ref),
        (latent_hbm, latent_ref),
        (mix_weight_hbm, mix_weight_ref),
    ]
    copies = [
        pltpu.make_async_copy(source, target, sems.at[place])
        for place, (source, target) in enumerate(pairs)
    ]
    for copy in copies:
        copy.start()
    for copy in copies[:3]:
        copy.wait()
    codebook = codebook_ref[...]
    both = jnp.concatenate([codebook * low(-0.5), codebook * low(2.0)], axis=0)
    weight = decode_weight_ref[...]
    weight_top = jnp.concatenate([weight, jnp.zeros_like(weight)], axis=0)
    columns = code_columns(index_ref)
    lanes = lax.broadcasted_iota(jnp.int32, (tile_rows, 128), 1)
    for row in range(rows):
        codes = row_codes(columns, row, canvases, rows, 128)
        for start, _ in chunks(count):
            near = codes[start : start + tile_rows]
            for at in range(0, entries, 128):
                chosen = lanes + at == near
                part = jnp.where(chosen, 1.0, 0.0).astype(low)
                picks_ref[pl.ds(row * count + start, tile_rows), at : at + 128] = part
    term = mm_nt(picks_ref[...], both)
    for copy in copies[3 : 3 + rows]:
        copy.wait()
    grad = out_grad_ref[...].reshape(rows * count, channels)
    term = term + mm_nt(grad, weight_top)
    term_ref[...] = term.reshape(term_ref.shape)
    weight_grad_ref[...] = 0.5 * mm_tn(term.astype(low), grad)[size:]
    bias_sum = None
    for start, _ in chunks(rows * count):
        part = grad[start : start + tile_rows].astype(wide)
        part = part[:8] + part[8:]
        bias_sum = part if bias_sum is None else bias_sum + part
    bias_grad_ref[...] = jnp.sum(bias_sum, axis=0, keepdims=True)
    for copy in copies[3 + rows :]:
        copy.wait()
    for row_step in range(3):
        for start, span in chunks(3 * channels):
            conv_weight_ref[row_step, span] = conv_weight_ref[row_step, span] * low(0.5)


def decoded_kernel(term_ref, decode_weight_ref, decode_bias_ref, after_ref, decoded_ref):
    canvases, rows, across, channels = decoded_ref.shape
    weight = decode_weight_ref[...] * low(0.5)
    weight = jnp.concatenate([jnp.zeros_like(weight), weight], axis=0)
    bias = decode_bias_ref[...].astype(wide).reshape(1, channels)
    for row in range(rows):
        decoded = (mm(term_ref[row].astype(low), weight) + bias).astype(low)
        decoded_ref[:, row] = decoded.reshape(canvases, across, channels)


class Places:
    mate, other = "mate", "other"

    def __init__(self, rows, count):
        self.rows, self.count = rows, count
        self.odd = lax.axis_index("strip") % 2 == 1
        self.inner = list(range(1, rows - 1))

    def row(self, unit):
        if unit == self.mate:
            return jnp.where(self.odd, 0, self.rows - 1)
        if unit == self.other:
            return jnp.where(self.odd, self.rows - 1, 0)
        return unit

    def halo(self, unit):
        first, last = 0, self.rows + 1
        return jnp.where(self.odd, *((first, last) if unit == self.mate else (last, first)))

    def span(self, number, at=0, size=None):
        start = number * self.count + at
        if not isinstance(start, int):
            start = pl.multiple_of(start, tile_rows)
        return pl.ds(start, size or self.count)

    def masks(self, masks_ref, plane, unit, canvas, across):
        return Masks(masks_ref, plane, self.row(unit) * self.count + canvas * across, across)


def rows_kernel(
    beyond,
    masks_ref,
    latent_ref,
    term_ref,
    conv_weight_ref,
    conv_bias_ref,
    mix_weight_ref,
    mix_bias_ref,
    proj_weight_ref,
    proj_bias_ref,
    halo_ref,
    *refs,
):
    outs = refs[-10:]
    slab_ref, grad_ref, up_ref, down_ref, second_ref, stream_ref, codes_ref = outs[:7]
    branch_grad_ref, sums_ref, edge_ref = outs[7:]
    canvases, rows, across, channels = latent_ref.shape
    size = proj_weight_ref.shape[0]
    count = canvases * across
    places = Places(rows, count)
    first = beyond == places.mate
    units = [*places.inner, places.mate] if first else [places.other]

    def own(row, canvas):
        return lambda at: silu(latent_ref[canvas, row, pl.ds(at, tile_rows)])

    def halo(canvas):
        return lambda at: silu(halo_ref[canvas, pl.ds(at, tile_rows)])

    proj = proj_weight_ref[...]
    proj_both = jnp.concatenate([proj * low(2 * commit_weight), proj * low(-2.0)], axis=0).T
    mix_back = (mix_weight_ref[...] * low(0.5)).T
    proj_top = jnp.concatenate([proj, jnp.zeros_like(proj)], axis=0)
    conv_bias = 0.5 * conv_bias_ref[...].astype(wide).reshape(1, channels)
    mix_bias = mix_bias_ref[...].astype(wide).reshape(1, channels)
    proj_bias = proj_bias_ref[...].astype(wide).reshape(1, size)
    proj_bias = jnp.concatenate([2 * commit_weight * proj_bias, -2.0 * proj_bias], axis=1)
    sums = [None, None, None]
    steps = chunks(across)
    tape = Tape()
    slabs = {}

    def add_to(place, values):
        values = values[:8] + values[8:]
        sums[place] = values if sums[place] is None else sums[place] + values

    def slab_of(row, canvas):
        if row != beyond and (not first or row == places.other):
            return None
        if (row, canvas) not in slabs:
            if row == beyond:
                place, values = places.halo(beyond), halo(canvas)
            else:
                place, values = row + 1, own(row, canvas)
            sides = [
                places.masks(masks_ref, plane, row, canvas, across)
                for plane in (left_plane, right_plane)
            ]
            start = places.span(place, canvas * across).start
            slabs[row, canvas] = tape.add(
                "vpu", 0.08, [], lambda: store_slab(slab_ref, start, *sides, values)
            )
        return slabs[row, canvas]

    group = canvases

    def tile(unit, canvas):
        inside = canvas * across
        there = places.row(unit)
        here = places.span(there, inside, group * across)
        above, below = [
            places.masks(masks_ref, plane, unit, canvas, across) for plane in (up_plane, down_plane)
        ]
        conv, slope, made = [], [], [None] * 4
        steps = chunks(group * across)

        def span(start):
            return places.span(there, inside + start, tile_rows)

        def multiply(place, step):
            def run():
                made[place] = step()

            return run

        def convolve(row_step):
            def run():
                rows_of = places.span(there + row_step, inside, group * across)
                conv.append(mm(slab_ref[rows_of], conv_weight_ref[row_step]))

            return run

        def activate():
            up, mid, down = conv
            for start, _ in steps:
                some = slice(start, start + tile_rows)
                total = masked(up[some], above(start).astype(wide))
                total = total + masked(down[some], below(start).astype(wide))
                second, twice = silu_slopes((total + mid[some]) + conv_bias)
                second_ref[span(start)] = second.astype(low)
                slope.append(twice)

        def add_latent():
            for start, _ in steps:
                latent = latent_ref[canvas + start // across, there, pl.ds(start % across, tile_rows)].astype(wide)
                part = latent + (made[0][start : start + tile_rows] + mix_bias)
                stream_ref[span(start)] = part.astype(low)

        def add_term():
            for start, _ in steps:
                part = made[1][start : start + tile_rows]
                part = part + (term_ref[there, pl.ds(inside + start, tile_rows)] + proj_bias)
                codes_ref[span(start)] = part.astype(low)
                add_to(2, part)

        def keep_branch():
            for start, _ in steps:
                part = made[2][start : start + tile_rows]
                branch_grad_ref[there, pl.ds(inside + start, tile_rows)] = part.astype(low)
                add_to(1, part)

        def keep_grad():
            for place, (start, _) in enumerate(steps):
                some = slice(start, start + tile_rows)
                part = made[3][some] * slope[place]
                rounded = part.astype(low)
                grad_ref[span(start)] = rounded
                up_ref[span(start)] = masked(rounded, above(start))
                down_ref[span(start)] = masked(rounded, below(start))
                if unit == beyond:
                    edge_ref[pl.ds(inside + start, tile_rows)] = rounded
                add_to(0, part)

        if unit == places.mate:
            needs = [*range(rows), unit]
        elif unit == places.other:
            needs = [unit]
        else:
            needs = [unit - 1, unit, unit + 1]
        needs = [slab_of(near, canvas + k) for near in needs for k in range(group)]
        last = [tape.add("mxu", 0.063 * group, needs, convolve(row_step)) for row_step in range(3)]
        last = tape.add("vpu", 0.1 * group, last, activate)
        chain = [
            (0.021, lambda: mm(second_ref[here], mix_weight_ref[...]), 0.04, add_latent),
            (0.021, lambda: mm(stream_ref[here], proj_both), 0.03, add_term),
            (0.021, lambda: mm(codes_ref[here], proj_top), 0.03, keep_branch),
            (
                0.021,
                lambda: mm(branch_grad_ref[there, pl.ds(inside, group * across)], mix_back),
                0.07,
                keep_grad,
            ),
        ]
        for place, (cost, product, later, rest) in enumerate(chain):
            last = tape.add("mxu", cost * group, [last], multiply(place, product))
            last = tape.add("vpu", later * group, [last], rest)

    for unit in units:
        for canvas in range(0, canvases, group):
            tile(unit, canvas)

    tape.play()
    sums = [jnp.sum(values, axis=0, keepdims=True) for values in sums]
    sums[2] = jnp.concatenate([sums[2]] * (channels // sums[2].shape[1]), axis=1)
    blank = jnp.zeros((sums_ref.shape[0] - 3, channels), wide)
    sums = jnp.concatenate([*sums, blank], axis=0)
    sums_ref[...] = sums if first else sums + refs[8][...]


def weight_kernel(
    plan,
    mine,
    slab_ref,
    grad_ref,
    up_ref,
    down_ref,
    second_ref,
    stream_ref,
    codes_ref,
    branch_grad_ref,
    sums_ref,
    picks_ref,
    decode_weight_grad_ref,
    decode_bias_grad_ref,
    after_ref,
    out_ref,
):
    total, channels = grad_ref.shape
    rows, count, _ = branch_grad_ref.shape
    size = decode_weight_grad_ref.shape[0]
    entries = picks_ref.shape[1]
    core = lax.axis_index("strip") % 2
    wanted = core if mine else 1 - core
    place = plan.place(wanted)

    def step(row_step, weighted_ref):
        return mm_tn(slab_ref[pl.ds(row_step * count, total)], weighted_ref[...])

    def fill(parts):
        piece, had = [], 0
        at = 0
        rest = plan.half_rows - sum(depth for depth, _ in parts)
        for depth, part in [*parts, (rest, lambda: jnp.zeros((rest, channels), wide))]:
            values = part() if depth else None
            start = 0
            while start < depth:
                some = min(depth - start, plan.piece_rows - had)
                piece.append(values[start : start + some].astype(low))
                start += some
                had += some
                if had == plan.piece_rows:
                    out_ref[at ^ place] = jnp.concatenate(piece, axis=0)
                    piece, had = [], 0
                    at += 1

    @pl.when(wanted == 0)
    def _():
        triple = 3 * channels
        fill([(triple, lambda: step(0, up_ref)), (triple, lambda: step(1, grad_ref))])

    @pl.when(wanted == 1)
    def _():
        sums = sums_ref[...]
        biases = [sums[0:1], sums[1:2], decode_bias_grad_ref[...], sums[2:3]]
        biases.append(jnp.zeros((tile_rows - len(biases), channels), wide))

        def picked():
            part = mm_tn(codes_ref[...], picks_ref[...])[size:]
            return jnp.concatenate([part[:, i : i + channels] for i in range(0, entries, channels)], axis=0)

        fill(
            [
                (3 * channels, lambda: step(2, down_ref)),
                (channels, lambda: mm_tn(second_ref[...], branch_grad_ref[...].reshape(total, channels))),
                (size, lambda: mm_tn(codes_ref[...], stream_ref[...])[:size]),
                (size * (entries // channels), picked),
                (size, lambda: decode_weight_grad_ref[...]),
                (tile_rows, lambda: jnp.concatenate(biases, axis=0)),
            ]
        )


def input_kernel(
    mine,
    masks_ref,
    latent_ref,
    grad_ref,
    mate_ref,
    other_ref,
    branch_grad_ref,
    conv_weight_ref,
    after_ref,
    *refs,
):
    latent_grad_ref, slab_ref, back_ref, out_ref, sems = refs[-5:]
    canvases, rows, across, channels = latent_ref.shape
    count = canvases * across
    places = Places(rows, count)
    steps = chunks(across)
    tape = Tape()

    def own(row, canvas):
        start = row * count + canvas * across
        return lambda at: grad_ref[pl.ds(start + at, tile_rows)].astype(wide)

    def beside(mate, canvas):
        def values(at):
            span = pl.ds(canvas * across + at, tile_rows)
            return jnp.where(mate, mate_ref[span], other_ref[span]).astype(wide)

        return values

    for row_step in range(3):
        for col_step in range(3):
            lanes = slice((2 - col_step) * channels, (3 - col_step) * channels)
            turned = conv_weight_ref[2 - row_step, lanes].T
            back_ref[row_step, col_step * channels : (col_step + 1) * channels] = turned

    slabs = {}

    def slab_of(row, canvas):
        if (row, canvas) not in slabs:
            if row < 0:
                values = beside(places.odd, canvas)
            elif row == rows:
                values = beside(jnp.logical_not(places.odd), canvas)
            else:
                values = own(row, canvas)
            near = min(max(row, 0), rows - 1)
            sides = [
                places.masks(masks_ref, plane, near, canvas, across)
                for plane in (left_plane, right_plane)
            ]
            start = (row + 1) * count + canvas * across
            slabs[row, canvas] = tape.add(
                "vpu", 0.07, [], lambda: store_slab(slab_ref, start, *sides, values)
            )
        return slabs[row, canvas]

    def tile(place, row, canvas):
        inside = canvas * across
        above, below = [
            places.masks(masks_ref, plane, row, canvas, across) for plane in (up_plane, down_plane)
        ]
        spreads = [None] * 3

        def spread(row_step):
            def run():
                span = pl.ds((row + row_step) * count + inside, across)
                spreads[row_step] = mm(slab_ref[span], back_ref[row_step])

            return run

        def finish():
            for start, _ in steps:
                some = slice(start, start + tile_rows)
                total = masked(spreads[0][some], above(start).astype(wide))
                total = total + masked(spreads[2][some], below(start).astype(wide))
                total = total + spreads[1][some]
                near = pl.ds(start, tile_rows)
                _, twice = silu_slopes(0.5 * latent_ref[canvas, row, near].astype(wide))
                stream = branch_grad_ref[row, pl.ds(inside + start, tile_rows)]
                out_ref[place, canvas, near] = (stream.astype(wide) + total * twice).astype(low)

        needs = [slab_of(near, canvas) for near in (row - 1, row, row + 1)]
        made = [tape.add("mxu", 0.063, needs, spread(row_step)) for row_step in range(3)]
        tape.add("vpu", 0.12, made, finish)

    for canvas in range(canvases):
        for place, row in enumerate(mine):
            tile(place, row, canvas)
    tape.play()
    copies = []
    for place, row in enumerate(mine):
        copies.append(
            pltpu.make_async_copy(out_ref.at[place], latent_grad_ref.at[:, row], sems.at[place])
        )
        copies[-1].start()
    for copy in copies:
        copy.wait()


class Plan:
    def __init__(self, sizes, half_rows):
        self.sizes = sizes
        bits = {axis: [(axis, b) for b in range(size.bit_length() - 1)] for axis, size in sizes.items()}
        strip, canvas = bits["strip"], bits["canvas"]
        near, far = [*canvas[:1], *strip[1:2]], strip[2:4][::-1]
        rest = [*strip[4:], *canvas[1:]]
        rest = [rest[i : i + 2] for i in range(0, len(rest), 2)]
        even, odd = [near, far, *rest], [far, near, *rest]
        if len(near) != len(far):
            odd = even
        self.stages = [tuple(zip(*pair, strict=True)) for pair in zip(even, odd, strict=True) if pair[0]]
        self.core = ((("strip", 0), ("strip", 0)),)
        self.half = sizes["strip"] * sizes["canvas"] // 2
        self.piece_rows = -(-half_rows // (self.half * tile_rows)) * tile_rows
        self.half_rows = self.half * self.piece_rows

    def place(self, core):
        number = 0
        for stage in self.stages:
            for spots in stage:
                even, odd = [(lax.axis_index(axis) // 2**bit) % 2 for axis, bit in spots]
                number = number * 2 + (even if spots[0] == spots[1] else jnp.where(core == 0, even, odd))
        return number

    def swap(self, values, stage, step):
        width = self.sizes["canvas"]
        pairs = []
        for strip in range(self.sizes["strip"]):
            change = {"strip": 0, "canvas": 0}
            for place, spots in enumerate(reversed(stage)):
                if step >> place & 1:
                    axis, bit = spots[strip % 2]
                    change[axis] |= 1 << bit
            for canvas in range(width):
                target = (strip ^ change["strip"]) * width + (canvas ^ change["canvas"])
                pairs.append((strip * width + canvas, target))
        return lax.ppermute(values, ("strip", "canvas"), pairs)


def add_kernel(count, after, *refs):
    ins, outs = refs[:count], refs[count + after :]
    depth = outs[0].shape[0]
    for place, out_ref in enumerate(outs):
        span = pl.ds(place * depth, depth)
        total = ins[0][span].astype(wide)
        for ref in ins[1:]:
            total = total + ref[span].astype(wide)
        out_ref[...] = total.astype(low)


def add_split(arrays, parts, after=()):
    depth, rows, channels = arrays[0].shape
    shape = jax.ShapeDtypeStruct((depth // parts, rows, channels), low)
    return pl.pallas_call(
        functools.partial(add_kernel, len(arrays), len(after)),
        in_specs=[in_vmem] * len(arrays) + [anywhere] * len(after),
        out_specs=[in_vmem] * parts,
        out_shape=[shape] * parts,
        compiler_params=pltpu.CompilerParams(vmem_limit_bytes=vmem_bytes),
    )(*arrays, *after)


def gate_kernel(*refs):
    pass


def gate(array, *after):
    return pl.pallas_call(
        gate_kernel,
        in_specs=[in_vmem] + [anywhere] * len(after),
        out_specs=in_vmem,
        out_shape=jax.ShapeDtypeStruct(array.shape, array.dtype),
        input_output_aliases={0: 0},
        compiler_params=pltpu.CompilerParams(vmem_limit_bytes=vmem_bytes),
    )(array, *after)


def join_kernel(count, *refs):
    at = 0
    for ref in refs[:count]:
        refs[-1][pl.ds(at, ref.shape[0])] = ref[...]
        at += ref.shape[0]


def join(arrays, *after):
    depth, rows, channels = arrays[0].shape
    return pl.pallas_call(
        functools.partial(join_kernel, len(arrays)),
        in_specs=[in_vmem] * len(arrays) + [anywhere] * len(after),
        out_specs=in_vmem,
        out_shape=jax.ShapeDtypeStruct((depth * len(arrays), rows, channels), low),
        compiler_params=pltpu.CompilerParams(vmem_limit_bytes=vmem_bytes),
    )(*arrays, *after)


def final_kernel(plan, count, sizes, *refs):
    ins, outs, gathered_ref = refs[:count], refs[count:-1], refs[-1]
    channels, size, entries = sizes
    core = lax.axis_index("strip") % 2
    at = 0
    for ref in ins:
        half = core if at < plan.half else 1 - core
        place = plan.place(half)
        for piece in range(ref.shape[0]):
            shard = half * plan.half + (place ^ at % plan.half)
            start = pl.multiple_of(shard * plan.piece_rows, plan.piece_rows)
            gathered_ref[pl.ds(start, plan.piece_rows)] = ref[piece]
            at += 1
    conv_ref, conv_bias_ref, mix_ref, mix_bias_ref, proj_ref, proj_bias_ref = outs[:6]
    codebook_ref, decode_ref, decode_bias_ref = outs[6:]
    triple = 3 * channels
    conv_ref[pl.ds(0, 2 * triple)] = gathered_ref[pl.ds(0, 2 * triple)].astype(wide)
    at = plan.half_rows
    conv_ref[pl.ds(2 * triple, triple)] = gathered_ref[pl.ds(at, triple)].astype(wide)
    at += triple
    mix_ref[...] = gathered_ref[pl.ds(at, channels)].astype(wide)
    at += channels
    proj_ref[...] = gathered_ref[pl.ds(at, size)].astype(wide)
    at += size
    for piece in range(entries // channels):
        part = gathered_ref[pl.ds(at, size)].astype(wide)
        codebook_ref[:, piece * channels : (piece + 1) * channels] = part
        at += size
    decode_ref[...] = gathered_ref[pl.ds(at, size)].astype(wide)
    at += size
    biases = gathered_ref[pl.ds(at, tile_rows)].astype(wide)
    conv_bias_ref[...] = biases[0:1]
    mix_bias_ref[...] = biases[1:2]
    decode_bias_ref[...] = biases[2:3]
    proj_bias_ref[...] = biases[3:4, :size]


def per_device(
    plan,
    latent_in,
    crop_code,
    code_index,
    conv_weight,
    conv_bias,
    mix_weight,
    mix_bias,
    proj_weight,
    proj_bias,
    codebook,
    decode_weight,
    decode_bias,
    out_grad,
):
    canvases, rows, across, channels = latent_in.shape
    entries, size = codebook.shape
    count = canvases * across
    total = rows * count
    strips = plan.sizes["strip"]
    struct = jax.ShapeDtypeStruct
    flat_weight = conv_weight.reshape(3, 3 * channels, channels)

    def far_away(*arrays):
        return [pltpu.with_memory_space_constraint(array, pltpu.HBM) for array in arrays]

    def call(kernel, ins, outs, shapes, scratch=(), flops=0, aliases=None):
        return pl.pallas_call(
            kernel,
            in_specs=list(ins),
            out_specs=list(outs),
            out_shape=list(shapes),
            scratch_shapes=list(scratch),
            input_output_aliases=aliases or {},
            compiler_params=pltpu.CompilerParams(vmem_limit_bytes=vmem_bytes),
            cost_estimate=pl.CostEstimate(flops=flops, bytes_accessed=0, transcendentals=0),
        )

    def trade(mate, other, split=True):
        near = [(i, i ^ 1) for i in range(strips)]
        far = [(i, i + 1) for i in range(1, strips - 1, 2)]
        far += [(target, source) for source, target in far]
        if not split:
            return lax.ppermute(mate, "strip", near), lax.ppermute(other, "strip", far)
        half = other.shape[0] // 2
        others = [lax.ppermute(part, "strip", far) for part in (other[:half], other[half:])]
        return (lax.ppermute(mate, "strip", near), *others)

    edge_shape = struct((canvases, across, channels), low)
    *edges, masks = call(
        edge_kernel,
        [in_hbm] * 2,
        [in_vmem] * 3,
        [edge_shape, edge_shape, struct((len(bits), total, 128), low)],
        [pltpu.VMEM(crop_code.shape, crop_code.dtype), pltpu.SemaphoreType.DMA((3,))],
    )(*far_away(latent_in, crop_code))
    mate, other = trade(*edges, split=False)
    outs = [
        struct((rows, count, 2 * size), wide),
        struct((total, entries), low),
        struct((size, channels), wide),
        struct((1, channels), wide),
        struct(latent_in.shape, low),
        struct(flat_weight.shape, low),
        struct(mix_weight.shape, low),
    ]
    held = [
        pltpu.VMEM(code_index.shape, code_index.dtype),
        pltpu.VMEM((size, entries), low),
        pltpu.VMEM((size, channels), low),
        pltpu.VMEM((rows, canvases, across, channels), low),
        pltpu.SemaphoreType.DMA((rows + 6,)),
    ]
    term, picks, decode_weight_grad, decode_bias_grad, latent, near_weight, near_mix = call(
        code_kernel,
        [in_hbm] * 7,
        [in_vmem] * 7,
        outs,
        held,
        flops=6 * total * channels * channels,
    )(
        *far_away(
            code_index,
            codebook.T,
            decode_weight,
            out_grad,
            latent_in,
            flat_weight,
            mix_weight,
        )
    )
    slab_shape = struct((total + 2 * count, 3 * channels), low)
    flat = struct((total, channels), low)
    kept = [slab_shape, flat, flat, flat, flat, flat, struct((total, 2 * size), low)]
    kept += [struct((rows, count, channels), low), struct((8, channels), wide)]
    edge_shape = struct((count, channels), low)
    inner, outer = tuple(range(1, rows - 1)), tuple(sorted({0, rows - 1}))
    shared = [masks, latent, term, near_weight, conv_bias, near_mix, mix_bias, proj_weight.T, proj_bias]

    def block_rows(beyond, halo, before):
        ins = [*shared, halo, *before]
        first = len(ins) - len(before)
        outs = call(
            functools.partial(rows_kernel, beyond),
            [in_vmem] * len(ins),
            [in_vmem] * (len(kept) + 1),
            [*kept, edge_shape],
            flops=20 * total * channels * channels,
            aliases={first + i: i for i in range(len(before))},
        )(*ins)
        return outs[:-1], outs[-1]

    before, edge_mate = block_rows("mate", mate, ())
    before, edge_other = block_rows("other", other, before)
    slab, grad, up, down, second, stream, codes, branch_grad, sums = before
    edges = (edge_mate, edge_other)

    def weight_half(mine, after):
        ins = [slab, grad, up, down, second, stream, codes, branch_grad, sums, picks]
        ins += [decode_weight_grad, decode_bias_grad]
        return call(
            functools.partial(weight_kernel, plan, mine),
            [in_vmem] * len(ins) + [anywhere],
            [in_vmem],
            [struct((plan.half, plan.piece_rows, channels), low)],
            flops=10 * total * channels * channels,
        )(*ins, after)[0]

    send = weight_half(False, edge_other)
    keep = weight_half(True, send)

    def input_rows(mine, halo, after, *before):
        return call(
            functools.partial(input_kernel, mine),
            [in_vmem] * 7 + [anywhere] + [in_hbm] * len(before),
            [in_hbm],
            [pltpu.HBM(latent_in.shape, low)],
            [
                pltpu.VMEM(slab_shape.shape, low),
                pltpu.VMEM(flat_weight.shape, low),
                pltpu.VMEM((len(mine), canvases, across, channels), low),
                pltpu.SemaphoreType.DMA((len(mine),)),
            ],
            flops=11 * total * channels * channels,
            aliases={8: 0} if before else {},
        )(masks, latent, grad, *halo, branch_grad, near_weight, after, *before)[0]

    arrays = [keep, plan.swap(send, plan.core, 1)]
    after = []
    for place, stage in enumerate(plan.stages):
        parts = add_split(arrays, 2 ** len(stage), after)
        arrays = [parts[0]]
        arrays += [plan.swap(parts[i], stage, i) for i in reversed(range(1, len(parts)))]
        after = []
        if place == 0:
            halo = trade(*[gate(edge, parts[0]) for edge in edges])
        elif place == 1:
            decoded = call(
                decoded_kernel,
                [in_vmem, in_vmem, in_vmem, anywhere],
                [pl.BlockSpec()],
                [pltpu.HBM(out_grad.shape, low)],
                flops=4 * total * channels * channels,
            )(term, decode_weight, decode_bias, parts[0])[0]
            after = [*far_away(decoded), *halo]
    halo = (halo[0], jnp.concatenate(halo[1:], axis=0))
    pieces = add_split(arrays, 1, after)
    latent_grad = input_rows(inner, edges, pieces[0])
    after = far_away(latent_grad)
    for stage in reversed(plan.stages):
        gathered = join(pieces, *after) if len(pieces) > 1 else pieces[0]
        others = [plan.swap(gathered, stage, i) for i in range(1, 2 ** len(stage))]
        pieces = [gathered, *others]
    latent_grad = input_rows(outer, halo, gathered, latent_grad)
    done = far_away(latent_grad)
    pieces = [pieces[0], *[gate(piece, *done) for piece in pieces[1:]]]
    arrays = [*pieces, *[plan.swap(piece, plan.core, 1) for piece in pieces]]

    results = call(
        functools.partial(final_kernel, plan, len(arrays), (channels, size, entries)),
        [in_vmem] * len(arrays),
        [pl.BlockSpec()] * 9,
        [
            struct((9 * channels, channels), wide),
            struct((1, channels), wide),
            struct((channels, channels), wide),
            struct((1, channels), wide),
            struct((size, channels), wide),
            struct((1, size), wide),
            struct((size, entries), wide),
            struct((size, channels), wide),
            struct((1, channels), wide),
        ],
        [pltpu.VMEM((2 * plan.half_rows, channels), low)],
    )(*arrays)
    return (
        decoded,
        latent_grad,
        results[0].reshape(3, 3, channels, channels),
        results[1].reshape(-1),
        results[2],
        results[3].reshape(-1),
        results[4].T,
        results[5].reshape(-1),
        results[6].T,
        results[7],
        results[8].reshape(-1),
    )


def solution(mesh):
    sizes = {axis: mesh.shape[axis] for axis in ("strip", "canvas")}
    shared = P("canvas", "strip", None, None)
    codes = P("canvas", "strip", None)

    def wrapped(*args):
        channels = args[0].shape[3]
        entries, size = args[9].shape
        others = 4 * channels + 2 * size + size * (entries // channels) + tile_rows
        plan = Plan(sizes, max(6 * channels, others))
        return jax.shard_map(
            functools.partial(per_device, plan),
            mesh=mesh,
            in_specs=(shared, codes, codes, *[P()] * 9, shared),
            out_specs=(shared, shared, *[P()] * 9),
            check_vma=False,
        )(*args)

    return wrapped
```

```python
import functools

import jax
import jax.numpy as jnp
from jax import lax
from jax.experimental import pallas as pl
from jax.experimental.pallas import tpu as pltpu
from jax.sharding import PartitionSpec as P

commit_weight = 0.25
low = jnp.bfloat16
wide = jnp.float32
bits = (1, 3, 4, 6)
up_plane, left_plane, right_plane, down_plane = range(4)
tile_rows = 16
vmem_bytes = 20 * 2**20
in_hbm = pl.BlockSpec(memory_space=pltpu.HBM)
anywhere = pl.BlockSpec(memory_space=pl.ANY)
in_vmem = pl.BlockSpec(memory_space=pltpu.VMEM)


def mm(lhs, rhs):
    return jnp.dot(lhs, rhs, preferred_element_type=wide)


def mm_nt(lhs, rhs):
    return lax.dot_general(lhs, rhs, (((1,), (1,)), ((), ())), preferred_element_type=wide)


def mm_tn(lhs, rhs):
    return lax.dot_general(lhs, rhs, (((0,), (0,)), ((), ())), preferred_element_type=wide)


def silu(values):
    half = 0.5 * values.astype(wide)
    return half * (1.0 + jnp.tanh(half))


def silu_slopes(half):
    turn = jnp.tanh(half)
    more = 1.0 + turn
    return half * more, more * (1.0 + half * (1.0 - turn))


def code_columns(code_ref):
    canvases, rows, across = code_ref.shape
    flat = code_ref[...].reshape(canvases * rows, across)
    extra = -across % 128
    if extra:
        flat = jnp.concatenate([flat, jnp.zeros((canvases * rows, extra), flat.dtype)], axis=1)
    return flat.T[:across]


def row_codes(columns, row, canvases, rows, lanes):
    pieces = [
        jnp.broadcast_to(
            columns[:, n * rows + row : n * rows + row + 1], (columns.shape[0], lanes)
        )
        for n in range(canvases)
    ]
    return jnp.concatenate(pieces, axis=0)


def chunks(count):
    return [(at, pl.ds(at, tile_rows)) for at in range(0, count, tile_rows)]


def masked(values, masks):
    return values * jnp.concatenate([masks] * (values.shape[1] // masks.shape[1]), axis=1)


def store_slab(slab_ref, at, left, right, values):
    channels = slab_ref.shape[1] // 3
    eight = tile_rows // 2
    place = lax.broadcasted_iota(jnp.int32, (eight, channels), 0)
    steps = chunks(left.count)

    def part(number):
        here = values(steps[number][0])
        halves = here[:eight], here[eight:]
        later = [pltpu.roll(half, 1, 0) for half in halves]
        sooner = [pltpu.roll(half, eight - 1, 0) for half in halves]
        return here, later, sooner

    now = part(0)
    before = now[1][1]
    for number, (start, _) in enumerate(steps):
        new = part(number + 1) if number + 1 < len(steps) else now
        here, later, sooner = now
        span = pl.ds(at + start, tile_rows)
        shifted = [
            jnp.where(place == 0, before, later[0]),
            jnp.where(place == 0, later[0], later[1]),
        ]
        shifted = jnp.concatenate(shifted, axis=0).astype(low)
        slab_ref[span, :channels] = masked(shifted, left(start))
        slab_ref[span, channels : 2 * channels] = here.astype(low)
        shifted = [
            jnp.where(place == eight - 1, sooner[1], sooner[0]),
            jnp.where(place == eight - 1, new[2][0], sooner[1]),
        ]
        shifted = jnp.concatenate(shifted, axis=0).astype(low)
        slab_ref[span, 2 * channels :] = masked(shifted, right(start))
        before = later[1]
        now = new


class Masks:
    def __init__(self, masks_ref, plane, at, count):
        self.masks_ref, self.plane, self.at, self.count = masks_ref, plane, at, count

    def __call__(self, start):
        at = self.at + start
        if not isinstance(at, int):
            at = pl.multiple_of(at, tile_rows)
        return self.masks_ref[self.plane, pl.ds(at, tile_rows)]


class Tape:
    def __init__(self):
        self.steps = []

    def add(self, unit, cost, after, step):
        self.steps.append((unit, cost, [a for a in after if a is not None], step))
        return len(self.steps) - 1

    def play(self):
        free = {"mxu": 0.0, "vpu": 0.0}
        lag = {"mxu": 0.1, "vpu": 0.02}
        ends = {}
        left = list(range(len(self.steps)))
        while left:
            best = None
            for number in left:
                unit, _, after, _ = self.steps[number]
                if all(a in ends for a in after):
                    start = max([free[unit], *[ends[a] for a in after]])
                    if best is None or (start, number) < best:
                        best = (start, number)
            start, number = best
            unit, cost, _, step = self.steps[number]
            free[unit] = start + cost
            ends[number] = start + cost + lag[unit]
            left.remove(number)
            step()


def edge_kernel(
    latent_hbm,
    crop_hbm,
    index_hbm,
    codebook_hbm,
    decode_weight_hbm,
    mate_ref,
    other_ref,
    crop_ref,
    index_ref,
    codebook_ref,
    decode_weight_ref,
    sems,
):
    rows = crop_ref.shape[1]
    odd = lax.axis_index("strip") % 2
    edge = (rows - 1) * (1 - odd)
    pairs = [
        (latent_hbm.at[:, rows - 1 - edge], other_ref),
        (latent_hbm.at[:, edge], mate_ref),
        (crop_hbm, crop_ref),
        (index_hbm, index_ref),
        (codebook_hbm, codebook_ref),
        (decode_weight_hbm, decode_weight_ref),
    ]
    copies = [
        pltpu.make_async_copy(source, target, sems.at[place])
        for place, (source, target) in enumerate(pairs)
    ]
    for copy in copies:
        copy.start()
    for copy in copies:
        copy.wait()


def code_kernel(
    crop_ref,
    index_ref,
    codebook_ref,
    decode_weight_ref,
    out_grad_hbm,
    latent_hbm,
    conv_weight_hbm,
    mix_weight_hbm,
    term_ref,
    picks_ref,
    masks_ref,
    bias_grad_ref,
    out_grad_ref,
    latent_ref,
    conv_weight_ref,
    mix_weight_ref,
    sems,
):
    canvases, rows, across = index_ref.shape
    size, entries = codebook_ref.shape
    channels = decode_weight_ref.shape[1]
    count = canvases * across
    pairs = [(out_grad_hbm.at[:, row], out_grad_ref.at[row]) for row in range(rows)]
    pairs += [
        (conv_weight_hbm, conv_weight_ref),
        (latent_hbm, latent_ref),
        (mix_weight_hbm, mix_weight_ref),
    ]
    copies = [
        pltpu.make_async_copy(source, target, sems.at[place])
        for place, (source, target) in enumerate(pairs)
    ]
    for copy in copies:
        copy.start()
    codebook = codebook_ref[...]
    both = jnp.concatenate([codebook * low(-0.5), codebook * low(2.0)], axis=0)
    weight = decode_weight_ref[...]
    weight = jnp.concatenate([weight, jnp.zeros_like(weight)], axis=0)
    table = jnp.concatenate([both, weight], axis=1).T
    lanes = lax.broadcasted_iota(jnp.int32, (tile_rows, 128), 1)
    index_columns, crop_columns = code_columns(index_ref), code_columns(crop_ref)
    terms = [None] * rows

    def make_picks(row):
        codes = row_codes(index_columns, row, canvases, rows, 128)
        for start, _ in chunks(count):
            near = codes[start : start + tile_rows]
            for at in range(0, entries, 128):
                chosen = lanes + at == near
                part = jnp.where(chosen, 1.0, 0.0).astype(low)
                picks_ref[pl.ds(row * count + start, tile_rows), at : at + 128] = part

    def make_masks(row):
        codes = row_codes(crop_columns, row, canvases, rows, 128)
        for start, _ in chunks(count):
            near = codes[start : start + tile_rows]
            span = pl.ds(row * count + start, tile_rows)
            for plane, bit in enumerate(bits):
                masks_ref[plane, span] = jnp.where((near & 2**bit) != 0, 1.0, 0.0).astype(low)

    def look_up(row):
        picks = picks_ref[pl.ds(row * count, count)]
        terms[row] = mm(jnp.concatenate([picks, grads(row)], axis=1), table)

    def grads(row):
        return out_grad_ref[row].reshape(count, channels)

    bias_sum = []
    make_picks(0)
    make_masks(0)
    if rows > 1:
        make_picks(1)
    for copy in copies[:rows]:
        copy.wait()
    for row in range(rows):
        look_up(row)
        if row + 2 < rows:
            make_picks(row + 2)
        if row + 1 < rows:
            make_masks(row + 1)
        for start, _ in chunks(count):
            part = grads(row)[start : start + tile_rows].astype(wide)
            part = part[:8] + part[8:]
            bias_sum = [bias_sum[0] + part] if bias_sum else [part]
        term_ref[row] = terms[row]
    bias_grad_ref[...] = jnp.sum(bias_sum[0], axis=0, keepdims=True)
    for copy in copies[rows:]:
        copy.wait()
    for row_step in range(3):
        for start, span in chunks(3 * channels):
            conv_weight_ref[row_step, span] = conv_weight_ref[row_step, span] * low(0.5)


def decoded_kernel(term_ref, decode_weight_ref, decode_bias_ref, after_ref, decoded_ref):
    canvases, rows, across, channels = decoded_ref.shape
    weight = decode_weight_ref[...] * low(0.5)
    weight = jnp.concatenate([jnp.zeros_like(weight), weight], axis=0)
    bias = decode_bias_ref[...].astype(wide).reshape(1, channels)
    for row in range(rows):
        decoded = (mm(term_ref[row].astype(low), weight) + bias).astype(low)
        decoded_ref[:, row] = decoded.reshape(canvases, across, channels)


class Places:
    mate, other = "mate", "other"

    def __init__(self, rows, count):
        self.rows, self.count = rows, count
        self.odd = lax.axis_index("strip") % 2 == 1
        self.inner = list(range(1, rows - 1))

    def row(self, unit):
        if unit == self.mate:
            return jnp.where(self.odd, 0, self.rows - 1)
        if unit == self.other:
            return jnp.where(self.odd, self.rows - 1, 0)
        return unit

    def toward(self, unit):
        return jnp.where(self.odd, *((0, 2) if unit == self.mate else (2, 0)))

    def halo(self, unit):
        first, last = 0, self.rows + 1
        return jnp.where(self.odd, *((first, last) if unit == self.mate else (last, first)))

    def span(self, number, at=0, size=None):
        start = number * self.count + at
        if not isinstance(start, int):
            start = pl.multiple_of(start, tile_rows)
        return pl.ds(start, size or self.count)

    def masks(self, masks_ref, plane, unit, canvas, across):
        return Masks(masks_ref, plane, self.row(unit) * self.count + canvas * across, across)


def rows_kernel(
    beyond,
    masks_ref,
    latent_ref,
    term_ref,
    conv_weight_ref,
    conv_bias_ref,
    mix_weight_ref,
    mix_bias_ref,
    proj_weight_ref,
    proj_bias_ref,
    halo_ref,
    also_ref,
    *refs,
):
    first = beyond == Places.mate
    outs = refs[-12:] if first else refs[-10:]
    slab_ref, grad_ref, up_ref, down_ref, second_ref, stream_ref, codes_ref = outs[:7]
    branch_grad_ref, sums_ref, edge_ref = outs[7:10]
    canvases, rows, across, channels = latent_ref.shape
    size = proj_weight_ref.shape[0]
    count = canvases * across
    places = Places(rows, count)
    units = [*places.inner, places.mate] if first else [places.other]

    def own(row, canvas):
        return lambda at: silu(latent_ref[canvas, row, pl.ds(at, tile_rows)])

    def halo(canvas):
        return lambda at: silu(halo_ref[canvas, pl.ds(at, tile_rows)])

    proj = proj_weight_ref[...]
    proj_both = jnp.concatenate([proj * low(2 * commit_weight), proj * low(-2.0)], axis=0).T
    mix_back = (mix_weight_ref[...] * low(0.5)).T
    proj_top = jnp.concatenate([proj, jnp.zeros_like(proj)], axis=0)
    conv_bias = 0.5 * conv_bias_ref[...].astype(wide).reshape(1, channels)
    mix_bias = mix_bias_ref[...].astype(wide).reshape(1, channels)
    proj_bias = proj_bias_ref[...].astype(wide).reshape(1, size)
    proj_bias = jnp.concatenate([2 * commit_weight * proj_bias, -2.0 * proj_bias], axis=1)
    sums = [None, None, None]
    steps = chunks(across)
    tape = Tape()
    slabs = {}

    def add_to(place, values):
        values = values[:8] + values[8:]
        sums[place] = values if sums[place] is None else sums[place] + values

    def slab_of(row, canvas):
        if row != beyond and (not first or row == places.other):
            return None
        if (row, canvas) not in slabs:
            if row == beyond:
                place, values = places.halo(beyond), halo(canvas)
            else:
                place, values = row + 1, own(row, canvas)
            sides = [
                places.masks(masks_ref, plane, row, canvas, across)
                for plane in (left_plane, right_plane)
            ]
            start = places.span(place, canvas * across).start
            slabs[row, canvas] = tape.add(
                "vpu", 0.08, [], lambda: store_slab(slab_ref, start, *sides, values)
            )
        return slabs[row, canvas]

    group = canvases if first else 1

    def tile(unit, canvas):
        inside = canvas * across
        there = places.row(unit)
        here = places.span(there, inside, group * across)
        above, below = [
            places.masks(masks_ref, plane, unit, canvas, across) for plane in (up_plane, down_plane)
        ]
        if unit == places.other:
            plane = jnp.where(places.odd, down_plane, up_plane)
            halo_masks = places.masks(masks_ref, plane, unit, canvas, across)
        conv, slope, made = [None] * 3, [], [None] * 4
        steps = chunks(group * across)

        def span(start):
            return places.span(there, inside + start, tile_rows)

        def multiply(place, step):
            def run():
                made[place] = step()

            return run

        def convolve(row_step):
            def run():
                rows_of = places.span(there + row_step, inside, group * across)
                conv[row_step] = mm(slab_ref[rows_of], conv_weight_ref[row_step])

            return run

        def convolve_halo():
            rows_of = places.span(places.halo(unit), inside, group * across)
            conv[0] = mm(slab_ref[rows_of], conv_weight_ref[places.toward(unit)])

        def activate():
            up, mid, down = conv
            for start, _ in steps:
                some = slice(start, start + tile_rows)
                if unit == places.other:
                    total = masked(up[some], halo_masks(start).astype(wide))
                    total = total + also_ref[pl.ds(inside + start, tile_rows)]
                else:
                    total = masked(up[some], above(start).astype(wide))
                    total = total + masked(down[some], below(start).astype(wide)) + mid[some]
                second, twice = silu_slopes(total + conv_bias)
                second_ref[span(start)] = second.astype(low)
                slope.append(twice)

        def add_latent():
            for start, _ in steps:
                latent = latent_ref[canvas + start // across, there, pl.ds(start % across, tile_rows)].astype(wide)
                part = latent + (made[0][start : start + tile_rows] + mix_bias)
                stream_ref[span(start)] = part.astype(low)

        def add_term():
            for start, _ in steps:
                part = made[1][start : start + tile_rows]
                part = part + (term_ref[there, pl.ds(inside + start, tile_rows)] + proj_bias)
                codes_ref[span(start)] = part.astype(low)
                add_to(2, part)

        def keep_branch():
            for start, _ in steps:
                part = made[2][start : start + tile_rows]
                branch_grad_ref[there, pl.ds(inside + start, tile_rows)] = part.astype(low)
                add_to(1, part)

        def keep_grad():
            for place, (start, _) in enumerate(steps):
                some = slice(start, start + tile_rows)
                part = made[3][some] * slope[place]
                rounded = part.astype(low)
                grad_ref[span(start)] = rounded
                up_ref[span(start)] = masked(rounded, above(start))
                down_ref[span(start)] = masked(rounded, below(start))
                if unit == beyond:
                    edge_ref[pl.ds(inside + start, tile_rows)] = rounded
                add_to(0, part)

        if unit == places.mate:
            needs = [*range(rows), unit]
        elif unit == places.other:
            needs = [unit]
        else:
            needs = [unit - 1, unit, unit + 1]
        needs = [slab_of(near, canvas + k) for near in needs for k in range(group)]
        if unit == places.other:
            last = [tape.add("mxu", 0.063 * group, needs, convolve_halo)]
        else:
            last = [tape.add("mxu", 0.063 * group, needs, convolve(row_step)) for row_step in range(3)]
        last = tape.add("vpu", 0.1 * group, last, activate)
        chain = [
            (0.021, lambda: mm(second_ref[here], mix_weight_ref[...]), 0.04, add_latent),
            (0.021, lambda: mm(stream_ref[here], proj_both), 0.03, add_term),
            (0.021, lambda: mm(codes_ref[here], proj_top), 0.03, keep_branch),
            (
                0.021,
                lambda: mm(branch_grad_ref[there, pl.ds(inside, group * across)], mix_back),
                0.07,
                keep_grad,
            ),
        ]
        for place, (cost, product, later, rest) in enumerate(chain):
            last = tape.add("mxu", cost * group, [last], multiply(place, product))
            last = tape.add("vpu", later * group, [last], rest)

    def weigh():
        box = [None]

        def product(row):
            def run():
                part = mm_tn(term_ref[row].astype(low), also_ref[row].reshape(count, channels))
                box[0] = part if box[0] is None else box[0] + part

            return run

        def store():
            refs[-2][...] = 0.5 * box[0][size:]

        made = [tape.add("mxu", 0.12, [], product(row)) for row in range(rows)]
        tape.add("vpu", 0.02, made, store)

    def convolve_last(canvas, some):
        there = places.row(places.other)
        inward = jnp.where(places.odd, -1, 1)
        plane = jnp.where(places.odd, up_plane, down_plane)
        masks = places.masks(masks_ref, plane, places.other, canvas, across)
        inside = canvas * across
        made = [None, None]

        def product(place, row, tap):
            def run():
                rows_of = places.span(row + 1, inside, some * across)
                made[place] = mm(slab_ref[rows_of], conv_weight_ref[tap])

            return run

        def store():
            for start, _ in chunks(some * across):
                near = slice(start, start + tile_rows)
                part = made[0][near] + masked(made[1][near], masks(start).astype(wide))
                refs[-1][pl.ds(inside + start, tile_rows)] = part

        needs = [slab_of(row, canvas + k) for row in range(rows) for k in range(some)]
        steps = [(there, 1), (there + inward, inward + 1)]
        needs = [
            tape.add("mxu", 0.063 * some, needs, product(place, *step))
            for place, step in enumerate(steps)
        ]
        tape.add("vpu", 0.04 * some, needs, store)

    if first:
        weigh()
    for unit in units:
        for canvas in range(0, canvases, group):
            tile(unit, canvas)
    if first:
        some = 2 if canvases % 2 == 0 else 1
        for canvas in range(0, canvases, some):
            convolve_last(canvas, some)
    tape.play()
    sums = [jnp.sum(values, axis=0, keepdims=True) for values in sums]
    sums[2] = jnp.concatenate([sums[2]] * (channels // sums[2].shape[1]), axis=1)
    blank = jnp.zeros((sums_ref.shape[0] - 3, channels), wide)
    sums = jnp.concatenate([*sums, blank], axis=0)
    sums_ref[...] = sums if first else sums + refs[8][...]


def weight_kernel(
    plan,
    mine,
    slab_ref,
    grad_ref,
    up_ref,
    down_ref,
    second_ref,
    stream_ref,
    codes_ref,
    branch_grad_ref,
    sums_ref,
    picks_ref,
    decode_weight_grad_ref,
    decode_bias_grad_ref,
    after_ref,
    out_ref,
):
    total, channels = grad_ref.shape
    rows, count, _ = branch_grad_ref.shape
    size = decode_weight_grad_ref.shape[0]
    entries = picks_ref.shape[1]
    core = lax.axis_index("strip") % 2
    wanted = core if mine else 1 - core
    place = plan.place(wanted)

    def step(row_step, weighted_ref):
        return mm_tn(slab_ref[pl.ds(row_step * count, total)], weighted_ref[...])

    def fill(parts):
        piece, had = [], 0
        at = 0
        rest = plan.half_rows - sum(depth for depth, _ in parts)
        for depth, part in [*parts, (rest, lambda: jnp.zeros((rest, channels), wide))]:
            values = part() if depth else None
            start = 0
            while start < depth:
                some = min(depth - start, plan.piece_rows - had)
                piece.append(values[start : start + some].astype(low))
                start += some
                had += some
                if had == plan.piece_rows:
                    out_ref[at ^ place] = jnp.concatenate(piece, axis=0)
                    piece, had = [], 0
                    at += 1

    @pl.when(wanted == 0)
    def _():
        triple = 3 * channels
        fill([(triple, lambda: step(0, up_ref)), (triple, lambda: step(1, grad_ref))])

    @pl.when(wanted == 1)
    def _():
        sums = sums_ref[...]
        biases = [sums[0:1], sums[1:2], decode_bias_grad_ref[...], sums[2:3]]
        biases.append(jnp.zeros((tile_rows - len(biases), channels), wide))

        def picked():
            part = mm_tn(codes_ref[...], picks_ref[...])[size:]
            return jnp.concatenate([part[:, i : i + channels] for i in range(0, entries, channels)], axis=0)

        fill(
            [
                (3 * channels, lambda: step(2, down_ref)),
                (channels, lambda: mm_tn(second_ref[...], branch_grad_ref[...].reshape(total, channels))),
                (size, lambda: mm_tn(codes_ref[...], stream_ref[...])[:size]),
                (size * (entries // channels), picked),
                (size, lambda: decode_weight_grad_ref[...]),
                (tile_rows, lambda: jnp.concatenate(biases, axis=0)),
            ]
        )


def input_kernel(
    mine,
    masks_ref,
    latent_ref,
    grad_ref,
    mate_ref,
    other_ref,
    branch_grad_ref,
    conv_weight_ref,
    after_ref,
    *refs,
):
    latent_grad_ref, slab_ref, back_ref, out_ref, sems = refs[-5:]
    canvases, rows, across, channels = latent_ref.shape
    count = canvases * across
    places = Places(rows, count)
    steps = chunks(across)
    tape = Tape()

    def own(row, canvas):
        start = row * count + canvas * across
        return lambda at: grad_ref[pl.ds(start + at, tile_rows)].astype(wide)

    def beside(mate, canvas):
        def values(at):
            span = pl.ds(canvas * across + at, tile_rows)
            return jnp.where(mate, mate_ref[span], other_ref[span]).astype(wide)

        return values

    for row_step in range(3):
        for col_step in range(3):
            lanes = slice((2 - col_step) * channels, (3 - col_step) * channels)
            turned = conv_weight_ref[2 - row_step, lanes].T
            back_ref[row_step, col_step * channels : (col_step + 1) * channels] = turned

    slabs = {}

    def slab_of(row, canvas):
        if (row, canvas) not in slabs:
            if row < 0:
                values = beside(places.odd, canvas)
            elif row == rows:
                values = beside(jnp.logical_not(places.odd), canvas)
            else:
                values = own(row, canvas)
            near = min(max(row, 0), rows - 1)
            sides = [
                places.masks(masks_ref, plane, near, canvas, across)
                for plane in (left_plane, right_plane)
            ]
            start = (row + 1) * count + canvas * across
            slabs[row, canvas] = tape.add(
                "vpu", 0.07, [], lambda: store_slab(slab_ref, start, *sides, values)
            )
        return slabs[row, canvas]

    def tile(place, row, canvas):
        inside = canvas * across
        above, below = [
            places.masks(masks_ref, plane, row, canvas, across) for plane in (up_plane, down_plane)
        ]
        spreads = [None] * 3

        def spread(row_step):
            def run():
                span = pl.ds((row + row_step) * count + inside, across)
                spreads[row_step] = mm(slab_ref[span], back_ref[row_step])

            return run

        def finish():
            for start, _ in steps:
                some = slice(start, start + tile_rows)
                total = masked(spreads[0][some], above(start).astype(wide))
                total = total + masked(spreads[2][some], below(start).astype(wide))
                total = total + spreads[1][some]
                near = pl.ds(start, tile_rows)
                _, twice = silu_slopes(0.5 * latent_ref[canvas, row, near].astype(wide))
                stream = branch_grad_ref[row, pl.ds(inside + start, tile_rows)]
                out_ref[place, canvas, near] = (stream.astype(wide) + total * twice).astype(low)

        needs = [slab_of(near, canvas) for near in (row - 1, row, row + 1)]
        made = [tape.add("mxu", 0.063, needs, spread(row_step)) for row_step in range(3)]
        tape.add("vpu", 0.12, made, finish)

    for canvas in range(canvases):
        for place, row in enumerate(mine):
            tile(place, row, canvas)
    tape.play()
    copies = []
    for place, row in enumerate(mine):
        copies.append(
            pltpu.make_async_copy(out_ref.at[place], latent_grad_ref.at[:, row], sems.at[place])
        )
        copies[-1].start()
    for copy in copies:
        copy.wait()


class Plan:
    def __init__(self, sizes, half_rows):
        self.sizes = sizes
        bits = {axis: [(axis, b) for b in range(size.bit_length() - 1)] for axis, size in sizes.items()}
        strip, canvas = bits["strip"], bits["canvas"]
        near, far = [*canvas[:1], *strip[1:2]], strip[2:4][::-1]
        rest = [*strip[4:], *canvas[1:]]
        rest = [rest[i : i + 2] for i in range(0, len(rest), 2)]
        even, odd = [near, far, *rest], [far, near, *rest]
        if len(near) != len(far):
            odd = even
        self.stages = [tuple(zip(*pair, strict=True)) for pair in zip(even, odd, strict=True) if pair[0]]
        self.core = ((("strip", 0), ("strip", 0)),)
        self.half = sizes["strip"] * sizes["canvas"] // 2
        self.piece_rows = -(-half_rows // (self.half * tile_rows)) * tile_rows
        self.half_rows = self.half * self.piece_rows

    def place(self, core):
        number = 0
        for stage in self.stages:
            for spots in stage:
                even, odd = [(lax.axis_index(axis) // 2**bit) % 2 for axis, bit in spots]
                number = number * 2 + (even if spots[0] == spots[1] else jnp.where(core == 0, even, odd))
        return number

    def swap(self, values, stage, step):
        width = self.sizes["canvas"]
        pairs = []
        for strip in range(self.sizes["strip"]):
            change = {"strip": 0, "canvas": 0}
            for place, spots in enumerate(reversed(stage)):
                if step >> place & 1:
                    axis, bit = spots[strip % 2]
                    change[axis] |= 1 << bit
            for canvas in range(width):
                target = (strip ^ change["strip"]) * width + (canvas ^ change["canvas"])
                pairs.append((strip * width + canvas, target))
        return lax.ppermute(values, ("strip", "canvas"), pairs)


def add_kernel(count, after, *refs):
    ins, outs = refs[:count], refs[count + after :]
    depth = outs[0].shape[0]
    for place, out_ref in enumerate(outs):
        span = pl.ds(place * depth, depth)
        total = ins[0][span].astype(wide)
        for ref in ins[1:]:
            total = total + ref[span].astype(wide)
        out_ref[...] = total.astype(low)


def add_split(arrays, parts, after=()):
    depth, rows, channels = arrays[0].shape
    shape = jax.ShapeDtypeStruct((depth // parts, rows, channels), low)
    return pl.pallas_call(
        functools.partial(add_kernel, len(arrays), len(after)),
        in_specs=[in_vmem] * len(arrays) + [anywhere] * len(after),
        out_specs=[in_vmem] * parts,
        out_shape=[shape] * parts,
        compiler_params=pltpu.CompilerParams(vmem_limit_bytes=vmem_bytes),
    )(*arrays, *after)


def gate_kernel(*refs):
    pass


def gate(array, *after):
    return pl.pallas_call(
        gate_kernel,
        in_specs=[in_vmem] + [anywhere] * len(after),
        out_specs=in_vmem,
        out_shape=jax.ShapeDtypeStruct(array.shape, array.dtype),
        input_output_aliases={0: 0},
        compiler_params=pltpu.CompilerParams(vmem_limit_bytes=vmem_bytes),
    )(array, *after)


def join_kernel(count, *refs):
    at = 0
    for ref in refs[:count]:
        refs[-1][pl.ds(at, ref.shape[0])] = ref[...]
        at += ref.shape[0]


def join(arrays, *after):
    depth, rows, channels = arrays[0].shape
    return pl.pallas_call(
        functools.partial(join_kernel, len(arrays)),
        in_specs=[in_vmem] * len(arrays) + [anywhere] * len(after),
        out_specs=in_vmem,
        out_shape=jax.ShapeDtypeStruct((depth * len(arrays), rows, channels), low),
        compiler_params=pltpu.CompilerParams(vmem_limit_bytes=vmem_bytes),
    )(*arrays, *after)


def final_kernel(plan, mine, count, sizes, *refs):
    ins, outs, scratch = refs[:count], refs[-15:-6], refs[-6:]
    gathered_ref, *line_refs, sems = scratch
    channels, size, entries = sizes
    core = lax.axis_index("strip") % 2
    half = core if mine else 1 - core
    place = plan.place(half)
    at = 0
    for ref in ins:
        for piece in range(ref.shape[0]):
            start = pl.multiple_of((place ^ at) * plan.piece_rows, plan.piece_rows)
            gathered_ref[pl.ds(start, plan.piece_rows)] = ref[piece].astype(wide)
            at += 1
    conv_ref, conv_bias_ref, mix_ref, mix_bias_ref, proj_ref, proj_bias_ref = outs[:6]
    codebook_ref, decode_ref, decode_bias_ref = outs[6:]
    triple = 3 * channels

    def copy_all(pairs):
        copies = [
            pltpu.make_async_copy(source, target, sems.at[number])
            for number, (source, target) in enumerate(pairs)
        ]
        for copy in copies:
            copy.start()
        for copy in copies:
            copy.wait()

    @pl.when(half == 0)
    def _():
        spans = [pl.ds(at, channels) for at in range(0, 2 * triple, channels)]
        copy_all([(gathered_ref.at[span], conv_ref.at[span]) for span in spans])

    @pl.when(half == 1)
    def _():
        pairs = []
        for at in range(0, triple, channels):
            span = pl.ds(2 * triple + at, channels)
            pairs.append((gathered_ref.at[pl.ds(at, channels)], conv_ref.at[span]))
        at = triple
        targets = [(mix_ref, channels), (proj_ref, size)]
        for piece in range(0, entries, channels):
            targets.append((codebook_ref.at[:, pl.ds(piece, channels)], size))
        targets.append((decode_ref, size))
        for target, depth in targets:
            pairs.append((gathered_ref.at[pl.ds(at, depth)], target))
            at += depth
        lines = gathered_ref[pl.ds(at, tile_rows)]
        targets = (conv_bias_ref, mix_bias_ref, decode_bias_ref, proj_bias_ref)
        for number, (line_ref, target) in enumerate(zip(line_refs, targets, strict=True)):
            line_ref[...] = lines[number : number + 1, : target.shape[1]]
            pairs.append((line_ref, target))
        copy_all(pairs)


def per_device(
    plan,
    latent_in,
    crop_code,
    code_index,
    conv_weight,
    conv_bias,
    mix_weight,
    mix_bias,
    proj_weight,
    proj_bias,
    codebook,
    decode_weight,
    decode_bias,
    out_grad,
):
    canvases, rows, across, channels = latent_in.shape
    entries, size = codebook.shape
    count = canvases * across
    total = rows * count
    strips = plan.sizes["strip"]
    struct = jax.ShapeDtypeStruct
    flat_weight = conv_weight.reshape(3, 3 * channels, channels)

    def far_away(*arrays):
        return [pltpu.with_memory_space_constraint(array, pltpu.HBM) for array in arrays]

    def call(kernel, ins, outs, shapes, scratch=(), flops=0, aliases=None):
        return pl.pallas_call(
            kernel,
            in_specs=list(ins),
            out_specs=list(outs),
            out_shape=list(shapes),
            scratch_shapes=list(scratch),
            input_output_aliases=aliases or {},
            compiler_params=pltpu.CompilerParams(vmem_limit_bytes=vmem_bytes),
            cost_estimate=pl.CostEstimate(flops=flops, bytes_accessed=0, transcendentals=0),
        )

    def trade(mate, other, split=True):
        near = [(i, i ^ 1) for i in range(strips)]
        far = [(i, i + 1) for i in range(1, strips - 1, 2)]
        far += [(target, source) for source, target in far]
        if not split:
            return lax.ppermute(mate, "strip", near), lax.ppermute(other, "strip", far)
        half = other.shape[0] // 2
        others = [lax.ppermute(part, "strip", far) for part in (other[:half], other[half:])]
        return (lax.ppermute(mate, "strip", near), *others)

    edge_shape = struct((canvases, across, channels), low)
    starts = [
        struct(crop_code.shape, crop_code.dtype),
        struct(code_index.shape, code_index.dtype),
        struct((size, entries), low),
        struct((size, channels), low),
    ]
    *edges, crop, index, near_codebook, near_decode = call(
        edge_kernel,
        [in_hbm] * 5,
        [in_vmem] * 6,
        [edge_shape, edge_shape, *starts],
        [pltpu.SemaphoreType.DMA((6,))],
    )(*far_away(latent_in, crop_code, code_index, codebook.T, decode_weight))
    mate, other = trade(*edges, split=False)
    outs = [
        struct((rows, count, 2 * size), wide),
        struct((total, entries), low),
        struct((len(bits), total, 128), low),
        struct((1, channels), wide),
        struct((rows, canvases, across, channels), low),
        struct(latent_in.shape, low),
        struct(flat_weight.shape, low),
        struct(mix_weight.shape, low),
    ]
    held = [pltpu.SemaphoreType.DMA((rows + 3,))]
    term, picks, masks, decode_bias_grad, near_grad, latent, near_weight, near_mix = call(
        code_kernel,
        [in_vmem] * 4 + [in_hbm] * 4,
        [in_vmem] * 8,
        outs,
        held,
        flops=6 * total * channels * channels,
    )(
        crop,
        index,
        near_codebook,
        near_decode,
        *far_away(out_grad, latent_in, flat_weight, mix_weight),
    )
    slab_shape = struct((total + 2 * count, 3 * channels), low)
    flat = struct((total, channels), low)
    kept = [slab_shape, flat, flat, flat, flat, flat, struct((total, 2 * size), low)]
    kept += [struct((rows, count, channels), low), struct((8, channels), wide)]
    edge_shape = struct((count, channels), low)
    inner, outer = tuple(range(1, rows - 1)), tuple(sorted({0, rows - 1}))
    shared = [masks, latent, term, near_weight, conv_bias, near_mix, mix_bias, proj_weight.T, proj_bias]

    def block_rows(beyond, halo, also, before, more):
        ins = [*shared, halo, also, *before]
        first = len(ins) - len(before)
        return call(
            functools.partial(rows_kernel, beyond),
            [in_vmem] * len(ins),
            [in_vmem] * (len(kept) + 1 + len(more)),
            [*kept, edge_shape, *more],
            flops=20 * total * channels * channels,
            aliases={first + i: i for i in range(len(before))},
        )(*ins)

    more = [struct((size, channels), wide), struct((count, channels), wide)]
    *before, edge_mate, decode_weight_grad, partial = block_rows("mate", mate, near_grad, (), more)
    *before, edge_other = block_rows("other", other, partial, before, ())
    slab, grad, up, down, second, stream, codes, branch_grad, sums = before
    edges = (edge_mate, edge_other)

    def weight_half(mine, after):
        ins = [slab, grad, up, down, second, stream, codes, branch_grad, sums, picks]
        ins += [decode_weight_grad, decode_bias_grad]
        return call(
            functools.partial(weight_kernel, plan, mine),
            [in_vmem] * len(ins) + [anywhere],
            [in_vmem],
            [struct((plan.half, plan.piece_rows, channels), low)],
            flops=10 * total * channels * channels,
        )(*ins, after)[0]

    send = weight_half(False, edge_other)
    keep = weight_half(True, send)

    def input_rows(mine, halo, after, *before):
        return call(
            functools.partial(input_kernel, mine),
            [in_vmem] * 7 + [anywhere] + [in_hbm] * len(before),
            [in_hbm],
            [pltpu.HBM(latent_in.shape, low)],
            [
                pltpu.VMEM(slab_shape.shape, low),
                pltpu.VMEM(flat_weight.shape, low),
                pltpu.VMEM((len(mine), canvases, across, channels), low),
                pltpu.SemaphoreType.DMA((len(mine),)),
            ],
            flops=11 * total * channels * channels,
            aliases={8: 0} if before else {},
        )(masks, latent, grad, *halo, branch_grad, near_weight, after, *before)[0]

    arrays = [keep, plan.swap(send, plan.core, 1)]
    after = []
    for place, stage in enumerate(plan.stages):
        parts = add_split(arrays, 2 ** len(stage), after)
        arrays = [parts[0]]
        arrays += [plan.swap(parts[i], stage, i) for i in reversed(range(1, len(parts)))]
        after = []
        if place == 0:
            halo = trade(*[gate(edge, parts[0]) for edge in edges])
        elif place == 1:
            decoded = call(
                decoded_kernel,
                [in_vmem, in_vmem, in_vmem, anywhere],
                [pl.BlockSpec()],
                [pltpu.HBM(out_grad.shape, low)],
                flops=4 * total * channels * channels,
            )(term, near_decode, decode_bias, parts[0])[0]
            after = [*far_away(decoded), *halo]
    halo = (halo[0], jnp.concatenate(halo[1:], axis=0))
    pieces = add_split(arrays, 1, after)
    latent_grad = input_rows(inner, edges, pieces[0])
    after = far_away(latent_grad)
    for stage in reversed(plan.stages):
        gathered = join(pieces, *after) if len(pieces) > 1 else pieces[0]
        others = [plan.swap(gathered, stage, i) for i in range(1, 2 ** len(stage))]
        pieces = [gathered, *others]
    latent_grad = input_rows(outer, halo, gathered, latent_grad)
    done = far_away(latent_grad)
    pieces = [pieces[0], *[gate(piece, *done) for piece in pieces[1:]]]
    swapped = [plan.swap(piece, plan.core, 1) for piece in pieces]
    shapes = [
        (9 * channels, channels),
        (1, channels),
        (channels, channels),
        (1, channels),
        (size, channels),
        (1, size),
        (size, entries),
        (size, channels),
        (1, channels),
    ]

    def finish(mine, arrays, *before):
        count = len(arrays)
        return call(
            functools.partial(final_kernel, plan, mine, count, (channels, size, entries)),
            [in_vmem] * count + [in_hbm] * len(before),
            [in_hbm] * len(shapes),
            [pltpu.HBM(shape, wide) for shape in shapes],
            [
                pltpu.VMEM((plan.half_rows, channels), wide),
                *[pltpu.VMEM((1, channels), wide)] * 3,
                pltpu.VMEM((1, size), wide),
                pltpu.SemaphoreType.DMA((16,)),
            ],
            aliases={count + i: i for i in range(len(before))},
        )(*arrays, *before)

    results = finish(True, pieces)
    results = finish(False, swapped, *results)
    return (
        decoded,
        latent_grad,
        results[0].reshape(3, 3, channels, channels),
        results[1].reshape(-1),
        results[2],
        results[3].reshape(-1),
        results[4].T,
        results[5].reshape(-1),
        results[6].T,
        results[7],
        results[8].reshape(-1),
    )


def solution(mesh):
    sizes = {axis: mesh.shape[axis] for axis in ("strip", "canvas")}
    shared = P("canvas", "strip", None, None)
    codes = P("canvas", "strip", None)

    def wrapped(*args):
        channels = args[0].shape[3]
        entries, size = args[9].shape
        others = 4 * channels + 2 * size + size * (entries // channels) + tile_rows
        plan = Plan(sizes, max(6 * channels, others))
        return jax.shard_map(
            functools.partial(per_device, plan),
            mesh=mesh,
            in_specs=(shared, codes, codes, *[P()] * 9, shared),
            out_specs=(shared, shared, *[P()] * 9),
            check_vma=False,
        )(*args)

    return wrapped
```

```python
import functools

import jax
import jax.numpy as jnp
from jax import lax
from jax.experimental import pallas as pl
from jax.experimental.pallas import tpu as pltpu
from jax.sharding import PartitionSpec as P

commit_weight = 0.25
low = jnp.bfloat16
wide = jnp.float32
bits = (1, 3, 4, 6)
up_plane, left_plane, right_plane, down_plane = range(4)
tile_rows = 16
vmem_bytes = 20 * 2**20
in_hbm = pl.BlockSpec(memory_space=pltpu.HBM)
anywhere = pl.BlockSpec(memory_space=pl.ANY)
in_vmem = pl.BlockSpec(memory_space=pltpu.VMEM)


def mm(lhs, rhs):
    return jnp.dot(lhs, rhs, preferred_element_type=wide)


def mm_nt(lhs, rhs):
    return lax.dot_general(lhs, rhs, (((1,), (1,)), ((), ())), preferred_element_type=wide)


def mm_tn(lhs, rhs):
    return lax.dot_general(lhs, rhs, (((0,), (0,)), ((), ())), preferred_element_type=wide)


def silu(values):
    half = 0.5 * values.astype(wide)
    return half * (1.0 + jnp.tanh(half))


def silu_slopes(half):
    turn = jnp.tanh(half)
    more = 1.0 + turn
    return half * more, more * (1.0 + half * (1.0 - turn))


def code_columns(code_ref):
    canvases, rows, across = code_ref.shape
    flat = code_ref[...].reshape(canvases * rows, across)
    extra = -across % 128
    if extra:
        flat = jnp.concatenate([flat, jnp.zeros((canvases * rows, extra), flat.dtype)], axis=1)
    return flat.T[:across]


def row_codes(columns, row, canvases, rows, lanes):
    pieces = [
        jnp.broadcast_to(
            columns[:, n * rows + row : n * rows + row + 1], (columns.shape[0], lanes)
        )
        for n in range(canvases)
    ]
    return jnp.concatenate(pieces, axis=0)


def chunks(count):
    return [(at, pl.ds(at, tile_rows)) for at in range(0, count, tile_rows)]


def masked(values, masks):
    return values * jnp.concatenate([masks] * (values.shape[1] // masks.shape[1]), axis=1)


def store_slab(slab_ref, at, left, right, values):
    channels = slab_ref.shape[1] // 3
    eight = tile_rows // 2
    place = lax.broadcasted_iota(jnp.int32, (eight, channels), 0)
    steps = chunks(left.count)

    def part(number):
        here = values(steps[number][0])
        halves = here[:eight], here[eight:]
        later = [pltpu.roll(half, 1, 0) for half in halves]
        sooner = [pltpu.roll(half, eight - 1, 0) for half in halves]
        return here, later, sooner

    now = part(0)
    before = now[1][1]
    for number, (start, _) in enumerate(steps):
        new = part(number + 1) if number + 1 < len(steps) else now
        here, later, sooner = now
        span = pl.ds(at + start, tile_rows)
        shifted = [
            jnp.where(place == 0, before, later[0]),
            jnp.where(place == 0, later[0], later[1]),
        ]
        shifted = jnp.concatenate(shifted, axis=0).astype(low)
        slab_ref[span, :channels] = masked(shifted, left(start))
        slab_ref[span, channels : 2 * channels] = here.astype(low)
        shifted = [
            jnp.where(place == eight - 1, sooner[1], sooner[0]),
            jnp.where(place == eight - 1, new[2][0], sooner[1]),
        ]
        shifted = jnp.concatenate(shifted, axis=0).astype(low)
        slab_ref[span, 2 * channels :] = masked(shifted, right(start))
        before = later[1]
        now = new


class Masks:
    def __init__(self, masks_ref, plane, at, count):
        self.masks_ref, self.plane, self.at, self.count = masks_ref, plane, at, count

    def __call__(self, start):
        at = self.at + start
        if not isinstance(at, int):
            at = pl.multiple_of(at, tile_rows)
        return self.masks_ref[self.plane, pl.ds(at, tile_rows)]


class Tape:
    def __init__(self):
        self.steps = []

    def add(self, unit, cost, after, step):
        self.steps.append((unit, cost, [a for a in after if a is not None], step))
        return len(self.steps) - 1

    def play(self):
        free = {"mxu": 0.0, "vpu": 0.0}
        lag = {"mxu": 0.1, "vpu": 0.02}
        ends = {}
        left = list(range(len(self.steps)))
        while left:
            best = None
            for number in left:
                unit, _, after, _ = self.steps[number]
                if all(a in ends for a in after):
                    start = max([free[unit], *[ends[a] for a in after]])
                    if best is None or (start, number) < best:
                        best = (start, number)
            start, number = best
            unit, cost, _, step = self.steps[number]
            free[unit] = start + cost
            ends[number] = start + cost + lag[unit]
            left.remove(number)
            step()


def edge_kernel(
    latent_hbm,
    crop_hbm,
    index_hbm,
    codebook_hbm,
    decode_weight_hbm,
    mate_ref,
    other_ref,
    crop_ref,
    index_ref,
    codebook_ref,
    decode_weight_ref,
    sems,
):
    rows = crop_ref.shape[1]
    odd = lax.axis_index("strip") % 2
    edge = (rows - 1) * (1 - odd)
    pairs = [
        (latent_hbm.at[:, rows - 1 - edge], other_ref),
        (latent_hbm.at[:, edge], mate_ref),
        (crop_hbm, crop_ref),
        (index_hbm, index_ref),
        (codebook_hbm, codebook_ref),
        (decode_weight_hbm, decode_weight_ref),
    ]
    copies = [
        pltpu.make_async_copy(source, target, sems.at[place])
        for place, (source, target) in enumerate(pairs)
    ]
    for copy in copies:
        copy.start()
    for copy in copies:
        copy.wait()


def code_kernel(
    crop_ref,
    index_ref,
    codebook_ref,
    decode_weight_ref,
    out_grad_hbm,
    latent_hbm,
    conv_weight_hbm,
    mix_weight_hbm,
    term_ref,
    picks_ref,
    masks_ref,
    bias_grad_ref,
    out_grad_ref,
    latent_ref,
    conv_weight_ref,
    mix_weight_ref,
    sems,
):
    canvases, rows, across = index_ref.shape
    size, entries = codebook_ref.shape
    channels = decode_weight_ref.shape[1]
    count = canvases * across
    pairs = [(out_grad_hbm.at[:, row], out_grad_ref.at[row]) for row in range(rows)]
    pairs += [
        (conv_weight_hbm, conv_weight_ref),
        (latent_hbm, latent_ref),
        (mix_weight_hbm, mix_weight_ref),
    ]
    copies = [
        pltpu.make_async_copy(source, target, sems.at[place])
        for place, (source, target) in enumerate(pairs)
    ]
    for copy in copies:
        copy.start()
    codebook = codebook_ref[...]
    both = jnp.concatenate([codebook * low(-0.5), codebook * low(2.0)], axis=0)
    weight = decode_weight_ref[...]
    weight = jnp.concatenate([weight, jnp.zeros_like(weight)], axis=0)
    table = jnp.concatenate([both, weight], axis=1).T
    lanes = lax.broadcasted_iota(jnp.int32, (tile_rows, 128), 1)
    index_columns, crop_columns = code_columns(index_ref), code_columns(crop_ref)
    terms = [None] * rows

    def make_picks(row):
        codes = row_codes(index_columns, row, canvases, rows, 128)
        for start, _ in chunks(count):
            near = codes[start : start + tile_rows]
            for at in range(0, entries, 128):
                chosen = lanes + at == near
                part = jnp.where(chosen, 1.0, 0.0).astype(low)
                picks_ref[pl.ds(row * count + start, tile_rows), at : at + 128] = part

    def make_masks(row):
        codes = row_codes(crop_columns, row, canvases, rows, 128)
        for start, _ in chunks(count):
            near = codes[start : start + tile_rows]
            span = pl.ds(row * count + start, tile_rows)
            for plane, bit in enumerate(bits):
                masks_ref[plane, span] = jnp.where((near & 2**bit) != 0, 1.0, 0.0).astype(low)

    def look_up(row):
        picks = picks_ref[pl.ds(row * count, count)]
        terms[row] = mm(jnp.concatenate([picks, grads(row)], axis=1), table)

    def grads(row):
        return out_grad_ref[row].reshape(count, channels)

    bias_sum = []
    make_picks(0)
    make_masks(0)
    if rows > 1:
        make_picks(1)
    for copy in copies[:rows]:
        copy.wait()
    for row in range(rows):
        look_up(row)
        if row + 2 < rows:
            make_picks(row + 2)
        if row + 1 < rows:
            make_masks(row + 1)
        for start, _ in chunks(count):
            part = grads(row)[start : start + tile_rows].astype(wide)
            part = part[:8] + part[8:]
            bias_sum = [bias_sum[0] + part] if bias_sum else [part]
        term_ref[row] = terms[row]
    bias_grad_ref[...] = jnp.sum(bias_sum[0], axis=0, keepdims=True)
    for copy in copies[rows:]:
        copy.wait()
    for row_step in range(3):
        for start, span in chunks(3 * channels):
            conv_weight_ref[row_step, span] = conv_weight_ref[row_step, span] * low(0.5)


def decoded_kernel(term_ref, decode_weight_ref, decode_bias_ref, after_ref, decoded_ref):
    canvases, rows, across, channels = decoded_ref.shape
    weight = decode_weight_ref[...] * low(0.5)
    weight = jnp.concatenate([jnp.zeros_like(weight), weight], axis=0)
    bias = decode_bias_ref[...].astype(wide).reshape(1, channels)
    for row in range(rows):
        decoded = (mm(term_ref[row].astype(low), weight) + bias).astype(low)
        decoded_ref[:, row] = decoded.reshape(canvases, across, channels)


class Places:
    mate, other = "mate", "other"

    def __init__(self, rows, count):
        self.rows, self.count = rows, count
        self.odd = lax.axis_index("strip") % 2 == 1
        self.inner = list(range(1, rows - 1))

    def row(self, unit):
        if unit == self.mate:
            return jnp.where(self.odd, 0, self.rows - 1)
        if unit == self.other:
            return jnp.where(self.odd, self.rows - 1, 0)
        return unit

    def toward(self, unit):
        return jnp.where(self.odd, *((0, 2) if unit == self.mate else (2, 0)))

    def halo(self, unit):
        first, last = 0, self.rows + 1
        return jnp.where(self.odd, *((first, last) if unit == self.mate else (last, first)))

    def span(self, number, at=0, size=None):
        start = number * self.count + at
        if not isinstance(start, int):
            start = pl.multiple_of(start, tile_rows)
        return pl.ds(start, size or self.count)

    def masks(self, masks_ref, plane, unit, canvas, across):
        return Masks(masks_ref, plane, self.row(unit) * self.count + canvas * across, across)


def rows_kernel(
    beyond,
    masks_ref,
    latent_ref,
    term_ref,
    conv_weight_ref,
    conv_bias_ref,
    mix_weight_ref,
    mix_bias_ref,
    proj_weight_ref,
    proj_bias_ref,
    halo_ref,
    also_ref,
    *refs,
):
    first = beyond == Places.mate
    outs = refs[-12:] if first else refs[-10:]
    slab_ref, grad_ref, up_ref, down_ref, second_ref, stream_ref, codes_ref = outs[:7]
    branch_grad_ref, sums_ref, edge_ref = outs[7:10]
    canvases, rows, across, channels = latent_ref.shape
    size = proj_weight_ref.shape[0]
    count = canvases * across
    places = Places(rows, count)
    units = [*places.inner, places.mate] if first else [places.other]

    def own(row, canvas):
        return lambda at: silu(latent_ref[canvas, row, pl.ds(at, tile_rows)])

    def halo(canvas):
        return lambda at: silu(halo_ref[canvas, pl.ds(at, tile_rows)])

    proj = proj_weight_ref[...]
    proj_both = jnp.concatenate([proj * low(2 * commit_weight), proj * low(-2.0)], axis=0).T
    mix_back = (mix_weight_ref[...] * low(0.5)).T
    proj_top = jnp.concatenate([proj, jnp.zeros_like(proj)], axis=0)
    conv_bias = 0.5 * conv_bias_ref[...].astype(wide).reshape(1, channels)
    mix_bias = mix_bias_ref[...].astype(wide).reshape(1, channels)
    proj_bias = proj_bias_ref[...].astype(wide).reshape(1, size)
    proj_bias = jnp.concatenate([2 * commit_weight * proj_bias, -2.0 * proj_bias], axis=1)
    sums = [None, None, None]
    steps = chunks(across)
    tape = Tape()
    slabs = {}

    def add_to(place, values):
        values = values[:8] + values[8:]
        sums[place] = values if sums[place] is None else sums[place] + values

    def slab_of(row, canvas):
        if row != beyond and (not first or row == places.other):
            return None
        if (row, canvas) not in slabs:
            if row == beyond:
                place, values = places.halo(beyond), halo(canvas)
            else:
                place, values = row + 1, own(row, canvas)
            sides = [
                places.masks(masks_ref, plane, row, canvas, across)
                for plane in (left_plane, right_plane)
            ]
            start = places.span(place, canvas * across).start
            slabs[row, canvas] = tape.add(
                "vpu", 0.08, [], lambda: store_slab(slab_ref, start, *sides, values)
            )
        return slabs[row, canvas]

    group = canvases if first else 1

    def tile(unit, canvas):
        inside = canvas * across
        there = places.row(unit)
        here = places.span(there, inside, group * across)
        above, below = [
            places.masks(masks_ref, plane, unit, canvas, across) for plane in (up_plane, down_plane)
        ]
        if unit == places.other:
            plane = jnp.where(places.odd, down_plane, up_plane)
            halo_masks = places.masks(masks_ref, plane, unit, canvas, across)
        conv, slope, made = [None] * 3, [], [None] * 4
        steps = chunks(group * across)

        def span(start):
            return places.span(there, inside + start, tile_rows)

        def multiply(place, step):
            def run():
                made[place] = step()

            return run

        def convolve(row_step):
            def run():
                rows_of = places.span(there + row_step, inside, group * across)
                conv[row_step] = mm(slab_ref[rows_of], conv_weight_ref[row_step])

            return run

        def convolve_halo():
            rows_of = places.span(places.halo(unit), inside, group * across)
            conv[0] = mm(slab_ref[rows_of], conv_weight_ref[places.toward(unit)])

        def activate():
            up, mid, down = conv
            for start, _ in steps:
                some = slice(start, start + tile_rows)
                if unit == places.other:
                    total = masked(up[some], halo_masks(start).astype(wide))
                    total = total + also_ref[pl.ds(inside + start, tile_rows)]
                else:
                    total = masked(up[some], above(start).astype(wide))
                    total = total + masked(down[some], below(start).astype(wide)) + mid[some]
                second, twice = silu_slopes(total + conv_bias)
                second_ref[span(start)] = second.astype(low)
                slope.append(twice)

        def add_latent():
            for start, _ in steps:
                latent = latent_ref[canvas + start // across, there, pl.ds(start % across, tile_rows)].astype(wide)
                part = latent + (made[0][start : start + tile_rows] + mix_bias)
                stream_ref[span(start)] = part.astype(low)

        def add_term():
            for start, _ in steps:
                part = made[1][start : start + tile_rows]
                part = part + (term_ref[there, pl.ds(inside + start, tile_rows)] + proj_bias)
                codes_ref[span(start)] = part.astype(low)
                add_to(2, part)

        def keep_branch():
            for start, _ in steps:
                part = made[2][start : start + tile_rows]
                branch_grad_ref[there, pl.ds(inside + start, tile_rows)] = part.astype(low)
                add_to(1, part)

        def keep_grad():
            for place, (start, _) in enumerate(steps):
                some = slice(start, start + tile_rows)
                part = made[3][some] * slope[place]
                rounded = part.astype(low)
                grad_ref[span(start)] = rounded
                up_ref[span(start)] = masked(rounded, above(start))
                down_ref[span(start)] = masked(rounded, below(start))
                if unit == beyond:
                    edge_ref[pl.ds(inside + start, tile_rows)] = rounded
                add_to(0, part)

        if unit == places.mate:
            needs = [*range(rows), unit]
        elif unit == places.other:
            needs = [unit]
        else:
            needs = [unit - 1, unit, unit + 1]
        needs = [slab_of(near, canvas + k) for near in needs for k in range(group)]
        if unit == places.other:
            last = [tape.add("mxu", 0.063 * group, needs, convolve_halo)]
        else:
            last = [tape.add("mxu", 0.063 * group, needs, convolve(row_step)) for row_step in range(3)]
        last = tape.add("vpu", 0.1 * group, last, activate)
        chain = [
            (0.021, lambda: mm(second_ref[here], mix_weight_ref[...]), 0.04, add_latent),
            (0.021, lambda: mm(stream_ref[here], proj_both), 0.03, add_term),
            (0.021, lambda: mm(codes_ref[here], proj_top), 0.03, keep_branch),
            (
                0.021,
                lambda: mm(branch_grad_ref[there, pl.ds(inside, group * across)], mix_back),
                0.07,
                keep_grad,
            ),
        ]
        for place, (cost, product, later, rest) in enumerate(chain):
            last = tape.add("mxu", cost * group, [last], multiply(place, product))
            last = tape.add("vpu", later * group, [last], rest)

    def weigh():
        box = [None]

        def product(row):
            def run():
                part = mm_tn(term_ref[row].astype(low), also_ref[row].reshape(count, channels))
                box[0] = part if box[0] is None else box[0] + part

            return run

        def store():
            refs[-2][...] = 0.5 * box[0][size:]

        made = [tape.add("mxu", 0.12, [], product(row)) for row in range(rows)]
        tape.add("vpu", 0.02, made, store)

    def convolve_last(canvas, some):
        there = places.row(places.other)
        inward = jnp.where(places.odd, -1, 1)
        plane = jnp.where(places.odd, up_plane, down_plane)
        masks = places.masks(masks_ref, plane, places.other, canvas, across)
        inside = canvas * across
        made = [None, None]

        def product(place, row, tap):
            def run():
                rows_of = places.span(row + 1, inside, some * across)
                made[place] = mm(slab_ref[rows_of], conv_weight_ref[tap])

            return run

        def store():
            for start, _ in chunks(some * across):
                near = slice(start, start + tile_rows)
                part = made[0][near] + masked(made[1][near], masks(start).astype(wide))
                refs[-1][pl.ds(inside + start, tile_rows)] = part

        needs = [slab_of(row, canvas + k) for row in range(rows) for k in range(some)]
        steps = [(there, 1), (there + inward, inward + 1)]
        needs = [
            tape.add("mxu", 0.063 * some, needs, product(place, *step))
            for place, step in enumerate(steps)
        ]
        tape.add("vpu", 0.04 * some, needs, store)

    if first:
        weigh()
    for unit in units:
        for canvas in range(0, canvases, group):
            tile(unit, canvas)
    if first:
        some = 2 if canvases % 2 == 0 else 1
        for canvas in range(0, canvases, some):
            convolve_last(canvas, some)
    tape.play()
    sums = [jnp.sum(values, axis=0, keepdims=True) for values in sums]
    sums[2] = jnp.concatenate([sums[2]] * (channels // sums[2].shape[1]), axis=1)
    blank = jnp.zeros((sums_ref.shape[0] - 3, channels), wide)
    sums = jnp.concatenate([*sums, blank], axis=0)
    sums_ref[...] = sums if first else sums + refs[8][...]


def weight_kernel(
    plan,
    mine,
    slab_ref,
    grad_ref,
    up_ref,
    down_ref,
    second_ref,
    stream_ref,
    codes_ref,
    branch_grad_ref,
    sums_ref,
    picks_ref,
    decode_weight_grad_ref,
    decode_bias_grad_ref,
    after_ref,
    out_ref,
):
    total, channels = grad_ref.shape
    rows, count, _ = branch_grad_ref.shape
    size = decode_weight_grad_ref.shape[0]
    entries = picks_ref.shape[1]
    core = lax.axis_index("strip") % 2
    wanted = core if mine else 1 - core
    place = plan.place(wanted)

    def step(row_step, weighted_ref):
        return mm_tn(slab_ref[pl.ds(row_step * count, total)], weighted_ref[...])

    def fill(parts):
        piece, had = [], 0
        at = 0
        rest = plan.half_rows - sum(depth for depth, _ in parts)
        for depth, part in [*parts, (rest, lambda: jnp.zeros((rest, channels), wide))]:
            values = part() if depth else None
            start = 0
            while start < depth:
                some = min(depth - start, plan.piece_rows - had)
                piece.append(values[start : start + some].astype(low))
                start += some
                had += some
                if had == plan.piece_rows:
                    out_ref[at ^ place] = jnp.concatenate(piece, axis=0)
                    piece, had = [], 0
                    at += 1

    @pl.when(wanted == 0)
    def _():
        triple = 3 * channels
        fill([(triple, lambda: step(0, up_ref)), (triple, lambda: step(1, grad_ref))])

    @pl.when(wanted == 1)
    def _():
        sums = sums_ref[...]
        biases = [sums[0:1], sums[1:2], decode_bias_grad_ref[...], sums[2:3]]
        biases.append(jnp.zeros((tile_rows - len(biases), channels), wide))

        def picked():
            part = mm_tn(codes_ref[...], picks_ref[...])[size:]
            return jnp.concatenate([part[:, i : i + channels] for i in range(0, entries, channels)], axis=0)

        fill(
            [
                (3 * channels, lambda: step(2, down_ref)),
                (channels, lambda: mm_tn(second_ref[...], branch_grad_ref[...].reshape(total, channels))),
                (size, lambda: mm_tn(codes_ref[...], stream_ref[...])[:size]),
                (size * (entries // channels), picked),
                (size, lambda: decode_weight_grad_ref[...]),
                (tile_rows, lambda: jnp.concatenate(biases, axis=0)),
            ]
        )


def input_kernel(
    mine,
    masks_ref,
    latent_ref,
    grad_ref,
    mate_ref,
    other_ref,
    branch_grad_ref,
    conv_weight_ref,
    after_ref,
    *refs,
):
    latent_grad_ref, slab_ref, back_ref, out_ref, sems = refs[-5:]
    canvases, rows, across, channels = latent_ref.shape
    count = canvases * across
    places = Places(rows, count)
    steps = chunks(across)
    tape = Tape()

    def own(row, canvas):
        start = row * count + canvas * across
        return lambda at: grad_ref[pl.ds(start + at, tile_rows)].astype(wide)

    def beside(mate, canvas):
        def values(at):
            span = pl.ds(canvas * across + at, tile_rows)
            return jnp.where(mate, mate_ref[span], other_ref[span]).astype(wide)

        return values

    for row_step in range(3):
        for col_step in range(3):
            lanes = slice((2 - col_step) * channels, (3 - col_step) * channels)
            turned = conv_weight_ref[2 - row_step, lanes].T
            back_ref[row_step, col_step * channels : (col_step + 1) * channels] = turned

    slabs = {}

    def slab_of(row, canvas):
        if (row, canvas) not in slabs:
            if row < 0:
                values = beside(places.odd, canvas)
            elif row == rows:
                values = beside(jnp.logical_not(places.odd), canvas)
            else:
                values = own(row, canvas)
            near = min(max(row, 0), rows - 1)
            sides = [
                places.masks(masks_ref, plane, near, canvas, across)
                for plane in (left_plane, right_plane)
            ]
            start = (row + 1) * count + canvas * across
            slabs[row, canvas] = tape.add(
                "vpu", 0.07, [], lambda: store_slab(slab_ref, start, *sides, values)
            )
        return slabs[row, canvas]

    def tile(place, row, canvas):
        inside = canvas * across
        above, below = [
            places.masks(masks_ref, plane, row, canvas, across) for plane in (up_plane, down_plane)
        ]
        spreads = [None] * 3

        def spread(row_step):
            def run():
                span = pl.ds((row + row_step) * count + inside, across)
                spreads[row_step] = mm(slab_ref[span], back_ref[row_step])

            return run

        def finish():
            for start, _ in steps:
                some = slice(start, start + tile_rows)
                total = masked(spreads[0][some], above(start).astype(wide))
                total = total + masked(spreads[2][some], below(start).astype(wide))
                total = total + spreads[1][some]
                near = pl.ds(start, tile_rows)
                _, twice = silu_slopes(0.5 * latent_ref[canvas, row, near].astype(wide))
                stream = branch_grad_ref[row, pl.ds(inside + start, tile_rows)]
                out_ref[place, canvas, near] = (stream.astype(wide) + total * twice).astype(low)

        needs = [slab_of(near, canvas) for near in (row - 1, row, row + 1)]
        made = [tape.add("mxu", 0.063, needs, spread(row_step)) for row_step in range(3)]
        tape.add("vpu", 0.12, made, finish)

    for canvas in range(canvases):
        for place, row in enumerate(mine):
            tile(place, row, canvas)
    tape.play()
    copies = []
    for place, row in enumerate(mine):
        copies.append(
            pltpu.make_async_copy(out_ref.at[place], latent_grad_ref.at[:, row], sems.at[place])
        )
        copies[-1].start()
    for copy in copies:
        copy.wait()


class Plan:
    def __init__(self, sizes, half_rows):
        self.sizes = sizes
        bits = {axis: [(axis, b) for b in range(size.bit_length() - 1)] for axis, size in sizes.items()}
        strip, canvas = bits["strip"], bits["canvas"]
        near, far = [*canvas[:1], *strip[1:2]], strip[2:4][::-1]
        rest = [*strip[4:], *canvas[1:]]
        rest = [rest[i : i + 2] for i in range(0, len(rest), 2)]
        even, odd = [near, far, *rest], [far, near, *rest]
        stages = [tuple(zip(*pair, strict=True)) for pair in zip(even, odd, strict=True) if pair[0]]
        self.split, self.whole = stages[0], stages[1:]
        self.core = ((("strip", 0), ("strip", 0)),)
        self.half = 2 ** len(self.split)
        self.piece_rows = -(-half_rows // (self.half * tile_rows)) * tile_rows
        self.half_rows = self.half * self.piece_rows

    def place(self, core):
        number = 0
        for spots in self.split:
            even, odd = [(lax.axis_index(axis) // 2**bit) % 2 for axis, bit in spots]
            number = number * 2 + jnp.where(core == 0, even, odd)
        return number

    def swap(self, values, stage, step):
        width = self.sizes["canvas"]
        pairs = []
        for strip in range(self.sizes["strip"]):
            change = {"strip": 0, "canvas": 0}
            for place, spots in enumerate(reversed(stage)):
                if step >> place & 1:
                    axis, bit = spots[strip % 2]
                    change[axis] |= 1 << bit
            for canvas in range(width):
                target = (strip ^ change["strip"]) * width + (canvas ^ change["canvas"])
                pairs.append((strip * width + canvas, target))
        return lax.ppermute(values, ("strip", "canvas"), pairs)


def add_kernel(count, after, *refs):
    ins, outs = refs[:count], refs[count + after :]
    depth = outs[0].shape[0]
    for place, out_ref in enumerate(outs):
        span = pl.ds(place * depth, depth)
        terms = [ref[span].astype(wide) for ref in ins]
        while len(terms) > 1:
            terms = [sum(terms[i + 1 : i + 2], terms[i]) for i in range(0, len(terms), 2)]
        out_ref[...] = terms[0].astype(low)


def add_split(arrays, parts, after=()):
    depth, rows, channels = arrays[0].shape
    shape = jax.ShapeDtypeStruct((depth // parts, rows, channels), low)
    return pl.pallas_call(
        functools.partial(add_kernel, len(arrays), len(after)),
        in_specs=[in_vmem] * len(arrays) + [anywhere] * len(after),
        out_specs=[in_vmem] * parts,
        out_shape=[shape] * parts,
        compiler_params=pltpu.CompilerParams(vmem_limit_bytes=vmem_bytes),
    )(*arrays, *after)


def gate_kernel(*refs):
    pass


def gate(array, *after):
    return pl.pallas_call(
        gate_kernel,
        in_specs=[in_vmem] + [anywhere] * len(after),
        out_specs=in_vmem,
        out_shape=jax.ShapeDtypeStruct(array.shape, array.dtype),
        input_output_aliases={0: 0},
        compiler_params=pltpu.CompilerParams(vmem_limit_bytes=vmem_bytes),
    )(array, *after)


def final_kernel(plan, mine, count, sizes, *refs):
    ins, outs, scratch = refs[:count], refs[-15:-6], refs[-6:]
    gathered_ref, *line_refs, sems = scratch
    channels, size, entries = sizes
    core = lax.axis_index("strip") % 2
    half = core if mine else 1 - core
    place = plan.place(half)
    at = 0
    for ref in ins:
        for piece in range(ref.shape[0]):
            start = pl.multiple_of((place ^ at) * plan.piece_rows, plan.piece_rows)
            gathered_ref[pl.ds(start, plan.piece_rows)] = ref[piece].astype(wide)
            at += 1
    conv_ref, conv_bias_ref, mix_ref, mix_bias_ref, proj_ref, proj_bias_ref = outs[:6]
    codebook_ref, decode_ref, decode_bias_ref = outs[6:]
    triple = 3 * channels

    def copy_all(pairs):
        copies = [
            pltpu.make_async_copy(source, target, sems.at[number])
            for number, (source, target) in enumerate(pairs)
        ]
        for copy in copies:
            copy.start()
        for copy in copies:
            copy.wait()

    @pl.when(half == 0)
    def _():
        spans = [pl.ds(at, channels) for at in range(0, 2 * triple, channels)]
        copy_all([(gathered_ref.at[span], conv_ref.at[span]) for span in spans])

    @pl.when(half == 1)
    def _():
        pairs = []
        for at in range(0, triple, channels):
            span = pl.ds(2 * triple + at, channels)
            pairs.append((gathered_ref.at[pl.ds(at, channels)], conv_ref.at[span]))
        at = triple
        targets = [(mix_ref, channels), (proj_ref, size)]
        for piece in range(0, entries, channels):
            targets.append((codebook_ref.at[:, pl.ds(piece, channels)], size))
        targets.append((decode_ref, size))
        for target, depth in targets:
            pairs.append((gathered_ref.at[pl.ds(at, depth)], target))
            at += depth
        lines = gathered_ref[pl.ds(at, tile_rows)]
        targets = (conv_bias_ref, mix_bias_ref, decode_bias_ref, proj_bias_ref)
        for number, (line_ref, target) in enumerate(zip(line_refs, targets, strict=True)):
            line_ref[...] = lines[number : number + 1, : target.shape[1]]
            pairs.append((line_ref, target))
        copy_all(pairs)


def per_device(
    plan,
    latent_in,
    crop_code,
    code_index,
    conv_weight,
    conv_bias,
    mix_weight,
    mix_bias,
    proj_weight,
    proj_bias,
    codebook,
    decode_weight,
    decode_bias,
    out_grad,
):
    canvases, rows, across, channels = latent_in.shape
    entries, size = codebook.shape
    count = canvases * across
    total = rows * count
    strips = plan.sizes["strip"]
    struct = jax.ShapeDtypeStruct
    flat_weight = conv_weight.reshape(3, 3 * channels, channels)

    def far_away(*arrays):
        return [pltpu.with_memory_space_constraint(array, pltpu.HBM) for array in arrays]

    def call(kernel, ins, outs, shapes, scratch=(), flops=0, aliases=None):
        return pl.pallas_call(
            kernel,
            in_specs=list(ins),
            out_specs=list(outs),
            out_shape=list(shapes),
            scratch_shapes=list(scratch),
            input_output_aliases=aliases or {},
            compiler_params=pltpu.CompilerParams(vmem_limit_bytes=vmem_bytes),
            cost_estimate=pl.CostEstimate(flops=flops, bytes_accessed=0, transcendentals=0),
        )

    def trade(mate, other, split=True):
        near = [(i, i ^ 1) for i in range(strips)]
        far = [(i, i + 1) for i in range(1, strips - 1, 2)]
        far += [(target, source) for source, target in far]
        if not split:
            return lax.ppermute(mate, "strip", near), lax.ppermute(other, "strip", far)
        half = other.shape[0] // 2
        others = [lax.ppermute(part, "strip", far) for part in (other[:half], other[half:])]
        return (lax.ppermute(mate, "strip", near), *others)

    edge_shape = struct((canvases, across, channels), low)
    starts = [
        struct(crop_code.shape, crop_code.dtype),
        struct(code_index.shape, code_index.dtype),
        struct((size, entries), low),
        struct((size, channels), low),
    ]
    *edges, crop, index, near_codebook, near_decode = call(
        edge_kernel,
        [in_hbm] * 5,
        [in_vmem] * 6,
        [edge_shape, edge_shape, *starts],
        [pltpu.SemaphoreType.DMA((6,))],
    )(*far_away(latent_in, crop_code, code_index, codebook.T, decode_weight))
    mate, other = trade(*edges, split=False)
    outs = [
        struct((rows, count, 2 * size), wide),
        struct((total, entries), low),
        struct((len(bits), total, 128), low),
        struct((1, channels), wide),
        struct((rows, canvases, across, channels), low),
        struct(latent_in.shape, low),
        struct(flat_weight.shape, low),
        struct(mix_weight.shape, low),
    ]
    held = [pltpu.SemaphoreType.DMA((rows + 3,))]
    term, picks, masks, decode_bias_grad, near_grad, latent, near_weight, near_mix = call(
        code_kernel,
        [in_vmem] * 4 + [in_hbm] * 4,
        [in_vmem] * 8,
        outs,
        held,
        flops=6 * total * channels * channels,
    )(
        crop,
        index,
        near_codebook,
        near_decode,
        *far_away(out_grad, latent_in, flat_weight, mix_weight),
    )
    slab_shape = struct((total + 2 * count, 3 * channels), low)
    flat = struct((total, channels), low)
    kept = [slab_shape, flat, flat, flat, flat, flat, struct((total, 2 * size), low)]
    kept += [struct((rows, count, channels), low), struct((8, channels), wide)]
    edge_shape = struct((count, channels), low)
    inner, outer = tuple(range(1, rows - 1)), tuple(sorted({0, rows - 1}))
    shared = [masks, latent, term, near_weight, conv_bias, near_mix, mix_bias, proj_weight.T, proj_bias]

    def block_rows(beyond, halo, also, before, more):
        ins = [*shared, halo, also, *before]
        first = len(ins) - len(before)
        return call(
            functools.partial(rows_kernel, beyond),
            [in_vmem] * len(ins),
            [in_vmem] * (len(kept) + 1 + len(more)),
            [*kept, edge_shape, *more],
            flops=20 * total * channels * channels,
            aliases={first + i: i for i in range(len(before))},
        )(*ins)

    more = [struct((size, channels), wide), struct((count, channels), wide)]
    *before, edge_mate, decode_weight_grad, partial = block_rows("mate", mate, near_grad, (), more)
    *before, edge_other = block_rows("other", other, partial, before, ())
    slab, grad, up, down, second, stream, codes, branch_grad, sums = before
    edges = (edge_mate, edge_other)

    def weight_half(mine, after):
        ins = [slab, grad, up, down, second, stream, codes, branch_grad, sums, picks]
        ins += [decode_weight_grad, decode_bias_grad]
        return call(
            functools.partial(weight_kernel, plan, mine),
            [in_vmem] * len(ins) + [anywhere],
            [in_vmem],
            [struct((plan.half, plan.piece_rows, channels), low)],
            flops=10 * total * channels * channels,
        )(*ins, after)[0]

    send = weight_half(False, edge_other)
    keep = weight_half(True, send)

    def input_rows(mine, halo, after, *before):
        return call(
            functools.partial(input_kernel, mine),
            [in_vmem] * 7 + [anywhere] + [in_hbm] * len(before),
            [in_hbm],
            [pltpu.HBM(latent_in.shape, low)],
            [
                pltpu.VMEM(slab_shape.shape, low),
                pltpu.VMEM(flat_weight.shape, low),
                pltpu.VMEM((len(mine), canvases, across, channels), low),
                pltpu.SemaphoreType.DMA((len(mine),)),
            ],
            flops=11 * total * channels * channels,
            aliases={8: 0} if before else {},
        )(masks, latent, grad, *halo, branch_grad, near_weight, after, *before)[0]

    parts = add_split([keep, plan.swap(send, plan.core, 1)], plan.half)
    halo = trade(*edges, split=False)
    swaps = [plan.swap(parts[i], plan.split, i) for i in reversed(range(1, plan.half))]
    latent_grad = input_rows(inner, edges, parts[0])
    after = far_away(latent_grad)
    piece = add_split([parts[0], *swaps], 1, after)[0]
    decoded = call(
        decoded_kernel,
        [in_vmem, in_vmem, in_vmem, anywhere],
        [pl.BlockSpec()],
        [pltpu.HBM(out_grad.shape, low)],
        flops=4 * total * channels * channels,
    )(term, near_decode, decode_bias, piece)[0]
    after = far_away(decoded)
    for stage in plan.whole:
        swaps = [plan.swap(piece, stage, i) for i in range(1, 2 ** len(stage))]
        piece = add_split([piece, *swaps], 1, after)[0]
        after = []
    others = [plan.swap(piece, plan.split, i) for i in range(1, plan.half)]
    latent_grad = input_rows(outer, halo, piece, latent_grad)
    done = far_away(latent_grad)
    pieces = [piece, *[gate(other, *done) for other in others]]
    swapped = [plan.swap(piece, plan.core, 1) for piece in pieces]
    shapes = [
        (9 * channels, channels),
        (1, channels),
        (channels, channels),
        (1, channels),
        (size, channels),
        (1, size),
        (size, entries),
        (size, channels),
        (1, channels),
    ]

    def finish(mine, arrays, *before):
        count = len(arrays)
        return call(
            functools.partial(final_kernel, plan, mine, count, (channels, size, entries)),
            [in_vmem] * count + [in_hbm] * len(before),
            [in_hbm] * len(shapes),
            [pltpu.HBM(shape, wide) for shape in shapes],
            [
                pltpu.VMEM((plan.half_rows, channels), wide),
                *[pltpu.VMEM((1, channels), wide)] * 3,
                pltpu.VMEM((1, size), wide),
                pltpu.SemaphoreType.DMA((16,)),
            ],
            aliases={count + i: i for i in range(len(before))},
        )(*arrays, *before)

    results = finish(True, pieces)
    results = finish(False, swapped, *results)
    return (
        decoded,
        latent_grad,
        results[0].reshape(3, 3, channels, channels),
        results[1].reshape(-1),
        results[2],
        results[3].reshape(-1),
        results[4].T,
        results[5].reshape(-1),
        results[6].T,
        results[7],
        results[8].reshape(-1),
    )


def solution(mesh):
    sizes = {axis: mesh.shape[axis] for axis in ("strip", "canvas")}
    shared = P("canvas", "strip", None, None)
    codes = P("canvas", "strip", None)

    def wrapped(*args):
        channels = args[0].shape[3]
        entries, size = args[9].shape
        others = 4 * channels + 2 * size + size * (entries // channels) + tile_rows
        plan = Plan(sizes, max(6 * channels, others))
        return jax.shard_map(
            functools.partial(per_device, plan),
            mesh=mesh,
            in_specs=(shared, codes, codes, *[P()] * 9, shared),
            out_specs=(shared, shared, *[P()] * 9),
            check_vma=False,
        )(*args)

    return wrapped
```

```python
import functools

import jax
import jax.numpy as jnp
from jax import lax
from jax.experimental import pallas as pl
from jax.experimental.pallas import tpu as pltpu
from jax.sharding import PartitionSpec as P

commit_weight = 0.25
low = jnp.bfloat16
wide = jnp.float32
bits = (1, 3, 4, 6)
up_plane, left_plane, right_plane, down_plane = range(4)
tile_rows = 16
half_tile = 8
vmem_bytes = 20 * 2**20
in_hbm = pl.BlockSpec(memory_space=pltpu.HBM)
anywhere = pl.BlockSpec(memory_space=pl.ANY)
in_vmem = pl.BlockSpec(memory_space=pltpu.VMEM)


def mm(lhs, rhs):
    return jnp.dot(lhs, rhs, preferred_element_type=wide)


def mm_nt(lhs, rhs):
    return lax.dot_general(lhs, rhs, (((1,), (1,)), ((), ())), preferred_element_type=wide)


def mm_tn(lhs, rhs):
    return lax.dot_general(lhs, rhs, (((0,), (0,)), ((), ())), preferred_element_type=wide)


def silu(values):
    half = 0.5 * values.astype(wide)
    return half * (1.0 + jnp.tanh(half))


def silu_slopes(half):
    turn = jnp.tanh(half)
    more = 1.0 + turn
    return half * more, more * (1.0 + half * (1.0 - turn))


def code_columns(code_ref):
    canvases, rows, across = code_ref.shape
    flat = code_ref[...].reshape(canvases * rows, across)
    extra = -across % 128
    if extra:
        flat = jnp.concatenate([flat, jnp.zeros((canvases * rows, extra), flat.dtype)], axis=1)
    return flat.T[:across]


def row_codes(columns, row, canvases, rows, lanes):
    pieces = [
        jnp.broadcast_to(
            columns[:, n * rows + row : n * rows + row + 1], (columns.shape[0], lanes)
        )
        for n in range(canvases)
    ]
    return jnp.concatenate(pieces, axis=0)


def chunks(count):
    return [(at, pl.ds(at, tile_rows)) for at in range(0, count, tile_rows)]


def masked(values, masks):
    return values * jnp.concatenate([masks] * (values.shape[1] // masks.shape[1]), axis=1)


def store_slab(slab_ref, at, left, right, values):
    channels = slab_ref.shape[1] // 3
    eight = tile_rows // 2
    place = lax.broadcasted_iota(jnp.int32, (eight, channels), 0)
    steps = chunks(left.count)

    def part(number):
        here = values(steps[number][0])
        halves = here[:eight], here[eight:]
        later = [pltpu.roll(half, 1, 0) for half in halves]
        sooner = [pltpu.roll(half, eight - 1, 0) for half in halves]
        return here, later, sooner

    now = part(0)
    before = now[1][1]
    for number, (start, _) in enumerate(steps):
        new = part(number + 1) if number + 1 < len(steps) else now
        here, later, sooner = now
        span = pl.ds(at + start, tile_rows)
        shifted = [
            jnp.where(place == 0, before, later[0]),
            jnp.where(place == 0, later[0], later[1]),
        ]
        shifted = jnp.concatenate(shifted, axis=0).astype(low)
        slab_ref[span, :channels] = masked(shifted, left(start))
        slab_ref[span, channels : 2 * channels] = here.astype(low)
        shifted = [
            jnp.where(place == eight - 1, sooner[1], sooner[0]),
            jnp.where(place == eight - 1, new[2][0], sooner[1]),
        ]
        shifted = jnp.concatenate(shifted, axis=0).astype(low)
        slab_ref[span, 2 * channels :] = masked(shifted, right(start))
        before = later[1]
        now = new


class Masks:
    def __init__(self, masks_ref, plane, at, count):
        self.masks_ref, self.plane, self.at, self.count = masks_ref, plane, at, count

    def __call__(self, start):
        at = self.at + start
        if not isinstance(at, int):
            at = pl.multiple_of(at, tile_rows)
        return self.masks_ref[self.plane, pl.ds(at, tile_rows)]


class Tape:
    def __init__(self):
        self.steps = []

    def add(self, unit, cost, after, step):
        self.steps.append((unit, cost, [a for a in after if a is not None], step))
        return len(self.steps) - 1

    def play(self):
        free = {"mxu": 0.0, "vpu": 0.0}
        lag = {"mxu": 0.1, "vpu": 0.02}
        ends = {}
        left = list(range(len(self.steps)))
        while left:
            best = None
            for number in left:
                unit, _, after, _ = self.steps[number]
                if all(a in ends for a in after):
                    start = max([free[unit], *[ends[a] for a in after]])
                    if best is None or (start, number) < best:
                        best = (start, number)
            start, number = best
            unit, cost, _, step = self.steps[number]
            free[unit] = start + cost
            ends[number] = start + cost + lag[unit]
            left.remove(number)
            step()


def edge_kernel(
    latent_hbm,
    crop_hbm,
    index_hbm,
    codebook_hbm,
    decode_weight_hbm,
    mate_ref,
    other_ref,
    crop_ref,
    index_ref,
    codebook_ref,
    decode_weight_ref,
    sems,
):
    rows = crop_ref.shape[1]
    odd = lax.axis_index("strip") % 2
    edge = (rows - 1) * (1 - odd)
    pairs = [
        (latent_hbm.at[:, rows - 1 - edge], other_ref),
        (latent_hbm.at[:, edge], mate_ref),
        (crop_hbm, crop_ref),
        (index_hbm, index_ref),
        (codebook_hbm, codebook_ref),
        (decode_weight_hbm, decode_weight_ref),
    ]
    copies = [
        pltpu.make_async_copy(source, target, sems.at[place])
        for place, (source, target) in enumerate(pairs)
    ]
    for copy in copies:
        copy.start()
    for copy in copies:
        copy.wait()


def code_kernel(
    crop_ref,
    index_ref,
    codebook_ref,
    decode_weight_ref,
    out_grad_hbm,
    latent_hbm,
    conv_weight_hbm,
    mix_weight_hbm,
    term_ref,
    picks_ref,
    masks_ref,
    bias_grad_ref,
    out_grad_ref,
    latent_ref,
    conv_weight_ref,
    mix_weight_ref,
    sems,
):
    canvases, rows, across = index_ref.shape
    size, entries = codebook_ref.shape
    channels = decode_weight_ref.shape[1]
    count = canvases * across
    pairs = [(out_grad_hbm.at[:, row], out_grad_ref.at[row]) for row in range(rows)]
    pairs += [
        (conv_weight_hbm, conv_weight_ref),
        (latent_hbm, latent_ref),
        (mix_weight_hbm, mix_weight_ref),
    ]
    copies = [
        pltpu.make_async_copy(source, target, sems.at[place])
        for place, (source, target) in enumerate(pairs)
    ]
    for copy in copies:
        copy.start()
    codebook = codebook_ref[...]
    both = jnp.concatenate([codebook * low(-0.5), codebook * low(2.0)], axis=0)
    weight = decode_weight_ref[...]
    weight = jnp.concatenate([weight, jnp.zeros_like(weight)], axis=0)
    table = jnp.concatenate([both, weight], axis=1).T
    lanes = lax.broadcasted_iota(jnp.int32, (tile_rows, 128), 1)
    index_columns, crop_columns = code_columns(index_ref), code_columns(crop_ref)
    terms = [None] * rows

    def make_picks(row):
        codes = row_codes(index_columns, row, canvases, rows, 128)
        for start, _ in chunks(count):
            near = codes[start : start + tile_rows]
            for at in range(0, entries, 128):
                chosen = lanes + at == near
                part = jnp.where(chosen, 1.0, 0.0).astype(low)
                picks_ref[pl.ds(row * count + start, tile_rows), at : at + 128] = part

    def make_masks(row):
        codes = row_codes(crop_columns, row, canvases, rows, 128)
        for start, _ in chunks(count):
            near = codes[start : start + tile_rows]
            span = pl.ds(row * count + start, tile_rows)
            for plane, bit in enumerate(bits):
                masks_ref[plane, span] = jnp.where((near & 2**bit) != 0, 1.0, 0.0).astype(low)

    def look_up(row):
        picks = picks_ref[pl.ds(row * count, count)]
        terms[row] = mm(jnp.concatenate([picks, grads(row)], axis=1), table)

    def grads(row):
        return out_grad_ref[row].reshape(count, channels)

    bias_sum = []
    make_picks(0)
    make_masks(0)
    if rows > 1:
        make_picks(1)
    for copy in copies[:rows]:
        copy.wait()
    for row in range(rows):
        look_up(row)
        if row + 2 < rows:
            make_picks(row + 2)
        if row + 1 < rows:
            make_masks(row + 1)
        for start, _ in chunks(count):
            part = grads(row)[start : start + tile_rows].astype(wide)
            part = part[:8] + part[8:]
            bias_sum = [bias_sum[0] + part] if bias_sum else [part]
        term_ref[row] = terms[row]
    bias_grad_ref[...] = jnp.sum(bias_sum[0], axis=0, keepdims=True)
    for copy in copies[rows:]:
        copy.wait()
    for row_step in range(3):
        for start, span in chunks(3 * channels):
            conv_weight_ref[row_step, span] = conv_weight_ref[row_step, span] * low(0.5)


def decoded_kernel(term_ref, decode_weight_ref, decode_bias_ref, after_ref, decoded_ref):
    canvases, rows, across, channels = decoded_ref.shape
    weight = decode_weight_ref[...] * low(0.5)
    weight = jnp.concatenate([jnp.zeros_like(weight), weight], axis=0)
    bias = decode_bias_ref[...].astype(wide).reshape(1, channels)
    for row in range(rows):
        decoded = (mm(term_ref[row].astype(low), weight) + bias).astype(low)
        decoded_ref[:, row] = decoded.reshape(canvases, across, channels)


class Places:
    mate, other = "mate", "other"

    def __init__(self, rows, count):
        self.rows, self.count = rows, count
        self.odd = lax.axis_index("strip") % 2 == 1
        self.inner = list(range(1, rows - 1))

    def row(self, unit):
        if unit == self.mate:
            return jnp.where(self.odd, 0, self.rows - 1)
        if unit == self.other:
            return jnp.where(self.odd, self.rows - 1, 0)
        return unit

    def toward(self, unit):
        return jnp.where(self.odd, *((0, 2) if unit == self.mate else (2, 0)))

    def halo(self, unit):
        first, last = 0, self.rows + 1
        return jnp.where(self.odd, *((first, last) if unit == self.mate else (last, first)))

    def span(self, number, at=0, size=None):
        start = number * self.count + at
        if not isinstance(start, int):
            start = pl.multiple_of(start, tile_rows)
        return pl.ds(start, size or self.count)

    def masks(self, masks_ref, plane, unit, canvas, across):
        return Masks(masks_ref, plane, self.row(unit) * self.count + canvas * across, across)


def rows_kernel(
    beyond,
    masks_ref,
    latent_ref,
    term_ref,
    conv_weight_ref,
    conv_bias_ref,
    mix_weight_ref,
    mix_bias_ref,
    proj_weight_ref,
    proj_bias_ref,
    halo_ref,
    also_ref,
    *refs,
):
    first = beyond == Places.mate
    outs = refs[-12:] if first else refs[-10:]
    slab_ref, grad_ref, up_ref, down_ref, second_ref, stream_ref, codes_ref = outs[:7]
    branch_grad_ref, sums_ref, edge_ref = outs[7:10]
    canvases, rows, across, channels = latent_ref.shape
    size = proj_weight_ref.shape[0]
    count = canvases * across
    places = Places(rows, count)
    units = [*places.inner, places.mate] if first else [places.other]

    def own(row, canvas):
        return lambda at: silu(latent_ref[canvas, row, pl.ds(at, tile_rows)])

    def halo(canvas):
        return lambda at: silu(halo_ref[canvas, pl.ds(at, tile_rows)])

    proj = proj_weight_ref[...]
    proj_both = jnp.concatenate([proj * low(2 * commit_weight), proj * low(-2.0)], axis=0).T
    mix_back = (mix_weight_ref[...] * low(0.5)).T
    proj_top = jnp.concatenate([proj, jnp.zeros_like(proj)], axis=0)
    conv_bias = 0.5 * conv_bias_ref[...].astype(wide).reshape(1, channels)
    mix_bias = mix_bias_ref[...].astype(wide).reshape(1, channels)
    proj_bias = proj_bias_ref[...].astype(wide).reshape(1, size)
    proj_bias = jnp.concatenate([2 * commit_weight * proj_bias, -2.0 * proj_bias], axis=1)
    sums = [None, None, None]
    steps = chunks(across)
    tape = Tape()
    slabs = {}

    def add_to(place, values):
        values = values[:8] + values[8:]
        sums[place] = values if sums[place] is None else sums[place] + values

    def slab_of(row, canvas):
        if row != beyond and (not first or row == places.other):
            return None
        if (row, canvas) not in slabs:
            if row == beyond:
                place, values = places.halo(beyond), halo(canvas)
            else:
                place, values = row + 1, own(row, canvas)
            sides = [
                places.masks(masks_ref, plane, row, canvas, across)
                for plane in (left_plane, right_plane)
            ]
            start = places.span(place, canvas * across).start
            slabs[row, canvas] = tape.add(
                "vpu", 0.08, [], lambda: store_slab(slab_ref, start, *sides, values)
            )
        return slabs[row, canvas]

    group = canvases if first else 1

    def tile(unit, canvas):
        inside = canvas * across
        there = places.row(unit)
        here = places.span(there, inside, group * across)
        above, below = [
            places.masks(masks_ref, plane, unit, canvas, across) for plane in (up_plane, down_plane)
        ]
        if unit == places.other:
            plane = jnp.where(places.odd, down_plane, up_plane)
            halo_masks = places.masks(masks_ref, plane, unit, canvas, across)
        conv, slope, made = [None] * 3, [], [None] * 4
        steps = chunks(group * across)

        def span(start):
            return places.span(there, inside + start, tile_rows)

        def multiply(place, step):
            def run():
                made[place] = step()

            return run

        def convolve(row_step):
            def run():
                rows_of = places.span(there + row_step, inside, group * across)
                conv[row_step] = mm(slab_ref[rows_of], conv_weight_ref[row_step])

            return run

        def convolve_halo():
            rows_of = places.span(places.halo(unit), inside, group * across)
            conv[0] = mm(slab_ref[rows_of], conv_weight_ref[places.toward(unit)])

        def activate():
            up, mid, down = conv
            for start, _ in steps:
                some = slice(start, start + tile_rows)
                if unit == places.other:
                    total = masked(up[some], halo_masks(start).astype(wide))
                    total = total + also_ref[pl.ds(inside + start, tile_rows)]
                else:
                    total = masked(up[some], above(start).astype(wide))
                    total = total + masked(down[some], below(start).astype(wide)) + mid[some]
                second, twice = silu_slopes(total + conv_bias)
                second_ref[span(start)] = second.astype(low)
                slope.append(twice)

        def add_latent():
            for start, _ in steps:
                latent = latent_ref[canvas + start // across, there, pl.ds(start % across, tile_rows)].astype(wide)
                part = latent + (made[0][start : start + tile_rows] + mix_bias)
                stream_ref[span(start)] = part.astype(low)

        def add_term():
            for start, _ in steps:
                part = made[1][start : start + tile_rows]
                part = part + (term_ref[there, pl.ds(inside + start, tile_rows)] + proj_bias)
                codes_ref[span(start)] = part.astype(low)
                add_to(2, part)

        def keep_branch():
            for start, _ in steps:
                part = made[2][start : start + tile_rows]
                branch_grad_ref[there, pl.ds(inside + start, tile_rows)] = part.astype(low)
                add_to(1, part)

        def keep_grad():
            for place, (start, _) in enumerate(steps):
                some = slice(start, start + tile_rows)
                part = made[3][some] * slope[place]
                rounded = part.astype(low)
                grad_ref[span(start)] = rounded
                up_ref[span(start)] = masked(rounded, above(start))
                down_ref[span(start)] = masked(rounded, below(start))
                if unit == beyond:
                    edge_ref[pl.ds(inside + start, tile_rows)] = rounded
                add_to(0, part)

        if unit == places.mate:
            needs = [*range(rows), unit]
        elif unit == places.other:
            needs = [unit]
        else:
            needs = [unit - 1, unit, unit + 1]
        needs = [slab_of(near, canvas + k) for near in needs for k in range(group)]
        if unit == places.other:
            last = [tape.add("mxu", 0.063 * group, needs, convolve_halo)]
        else:
            last = [tape.add("mxu", 0.063 * group, needs, convolve(row_step)) for row_step in range(3)]
        last = tape.add("vpu", 0.1 * group, last, activate)
        chain = [
            (0.021, lambda: mm(second_ref[here], mix_weight_ref[...]), 0.04, add_latent),
            (0.021, lambda: mm(stream_ref[here], proj_both), 0.03, add_term),
            (0.021, lambda: mm(codes_ref[here], proj_top), 0.03, keep_branch),
            (
                0.021,
                lambda: mm(branch_grad_ref[there, pl.ds(inside, group * across)], mix_back),
                0.07,
                keep_grad,
            ),
        ]
        for place, (cost, product, later, rest) in enumerate(chain):
            last = tape.add("mxu", cost * group, [last], multiply(place, product))
            last = tape.add("vpu", later * group, [last], rest)

    def weigh():
        box = [None]

        def product(row):
            def run():
                part = mm_tn(term_ref[row].astype(low), also_ref[row].reshape(count, channels))
                box[0] = part if box[0] is None else box[0] + part

            return run

        def store():
            refs[-2][...] = 0.5 * box[0][size:]

        made = [tape.add("mxu", 0.12, [], product(row)) for row in range(rows)]
        tape.add("vpu", 0.02, made, store)

    def convolve_last(canvas, some):
        there = places.row(places.other)
        inward = jnp.where(places.odd, -1, 1)
        plane = jnp.where(places.odd, up_plane, down_plane)
        masks = places.masks(masks_ref, plane, places.other, canvas, across)
        inside = canvas * across
        made = [None, None]

        def product(place, row, tap):
            def run():
                rows_of = places.span(row + 1, inside, some * across)
                made[place] = mm(slab_ref[rows_of], conv_weight_ref[tap])

            return run

        def store():
            for start, _ in chunks(some * across):
                near = slice(start, start + tile_rows)
                part = made[0][near] + masked(made[1][near], masks(start).astype(wide))
                refs[-1][pl.ds(inside + start, tile_rows)] = part

        needs = [slab_of(row, canvas + k) for row in range(rows) for k in range(some)]
        steps = [(there, 1), (there + inward, inward + 1)]
        needs = [
            tape.add("mxu", 0.063 * some, needs, product(place, *step))
            for place, step in enumerate(steps)
        ]
        tape.add("vpu", 0.04 * some, needs, store)

    if first:
        weigh()
    for unit in units:
        for canvas in range(0, canvases, group):
            tile(unit, canvas)
    if first:
        some = 2 if canvases % 2 == 0 else 1
        for canvas in range(0, canvases, some):
            convolve_last(canvas, some)
    tape.play()
    sums = [jnp.sum(values, axis=0, keepdims=True) for values in sums]
    sums[2] = jnp.concatenate([sums[2]] * (channels // sums[2].shape[1]), axis=1)
    blank = jnp.zeros((sums_ref.shape[0] - 3, channels), wide)
    sums = jnp.concatenate([*sums, blank], axis=0)
    sums_ref[...] = sums if first else sums + refs[8][...]


def weight_kernel(
    plan,
    mine,
    slab_ref,
    grad_ref,
    up_ref,
    down_ref,
    second_ref,
    stream_ref,
    codes_ref,
    branch_grad_ref,
    sums_ref,
    picks_ref,
    decode_weight_grad_ref,
    decode_bias_grad_ref,
    after_ref,
    out_ref,
):
    total, channels = grad_ref.shape
    rows, count, _ = branch_grad_ref.shape
    size = decode_weight_grad_ref.shape[0]
    entries = picks_ref.shape[1]
    core = lax.axis_index("strip") % 2
    wanted = core if mine else 1 - core
    place = plan.place(wanted)

    def step(row_step, weighted_ref, first, last):
        span, lanes = pl.ds(row_step * count, total), pl.ds(first * channels, (last - first) * channels)
        return (last - first) * channels, lambda: mm_tn(slab_ref[span, lanes], weighted_ref[...])

    def fill(parts):
        piece, had = [], 0
        at = 0
        rest = plan.half_rows - sum(depth for depth, _ in parts)
        for depth, part in [*parts, (rest, lambda: jnp.zeros((rest, channels), wide))]:
            values = part() if depth else None
            start = 0
            while start < depth:
                some = min(depth - start, plan.piece_rows - had)
                piece.append(values[start : start + some])
                start += some
                had += some
                if had == plan.piece_rows:
                    out_ref[at ^ place] = jnp.concatenate(piece, axis=0).astype(low)
                    piece, had = [], 0
                    at += 1

    @pl.when(wanted == 0)
    def _():
        fill(
            [
                step(0, up_ref, 0, 3),
                step(1, grad_ref, 0, 2),
                (size, lambda: mm_tn(codes_ref[...], stream_ref[...])[:size]),
                (size, lambda: decode_weight_grad_ref[...]),
            ]
        )

    @pl.when(wanted == 1)
    def _():
        sums = sums_ref[...]
        biases = [sums[0:1], sums[1:2], decode_bias_grad_ref[...], sums[2:3]]
        biases.append(jnp.zeros((tile_rows - len(biases), channels), wide))

        def picked():
            part = mm_tn(codes_ref[...], picks_ref[...])[size:]
            return jnp.concatenate([part[:, i : i + channels] for i in range(0, entries, channels)], axis=0)

        fill(
            [
                step(1, grad_ref, 2, 3),
                step(2, down_ref, 0, 3),
                (channels, lambda: mm_tn(second_ref[...], branch_grad_ref[...].reshape(total, channels))),
                (size * (entries // channels), picked),
                (tile_rows, lambda: jnp.concatenate(biases, axis=0)),
            ]
        )


def input_kernel(
    mine,
    masks_ref,
    latent_ref,
    grad_ref,
    mate_ref,
    other_ref,
    branch_grad_ref,
    conv_weight_ref,
    after_ref,
    *refs,
):
    latent_grad_ref, slab_ref, back_ref, out_ref, sems = refs[-5:]
    canvases, rows, across, channels = latent_ref.shape
    count = canvases * across
    places = Places(rows, count)
    steps = chunks(across)
    tape = Tape()

    def own(row, canvas):
        start = row * count + canvas * across
        return lambda at: grad_ref[pl.ds(start + at, tile_rows)].astype(wide)

    def beside(mate, canvas):
        def values(at):
            span = pl.ds(canvas * across + at, tile_rows)
            return jnp.where(mate, mate_ref[span], other_ref[span]).astype(wide)

        return values

    for row_step in range(3):
        for col_step in range(3):
            lanes = slice((2 - col_step) * channels, (3 - col_step) * channels)
            turned = conv_weight_ref[2 - row_step, lanes].T
            back_ref[row_step, col_step * channels : (col_step + 1) * channels] = turned

    slabs = {}

    def slab_of(row, canvas):
        if (row, canvas) not in slabs:
            if row < 0:
                values = beside(places.odd, canvas)
            elif row == rows:
                values = beside(jnp.logical_not(places.odd), canvas)
            else:
                values = own(row, canvas)
            near = min(max(row, 0), rows - 1)
            sides = [
                places.masks(masks_ref, plane, near, canvas, across)
                for plane in (left_plane, right_plane)
            ]
            start = (row + 1) * count + canvas * across
            slabs[row, canvas] = tape.add(
                "vpu", 0.07, [], lambda: store_slab(slab_ref, start, *sides, values)
            )
        return slabs[row, canvas]

    def tile(place, row, canvas):
        inside = canvas * across
        above, below = [
            places.masks(masks_ref, plane, row, canvas, across) for plane in (up_plane, down_plane)
        ]
        spreads = [None] * 3

        def spread(row_step):
            def run():
                span = pl.ds((row + row_step) * count + inside, across)
                spreads[row_step] = mm(slab_ref[span], back_ref[row_step])

            return run

        def finish():
            for start, _ in steps:
                some = slice(start, start + tile_rows)
                total = masked(spreads[0][some], above(start).astype(wide))
                total = total + masked(spreads[2][some], below(start).astype(wide))
                total = total + spreads[1][some]
                near = pl.ds(start, tile_rows)
                _, twice = silu_slopes(0.5 * latent_ref[canvas, row, near].astype(wide))
                stream = branch_grad_ref[row, pl.ds(inside + start, tile_rows)]
                out_ref[place, canvas, near] = (stream.astype(wide) + total * twice).astype(low)

        needs = [slab_of(near, canvas) for near in (row - 1, row, row + 1)]
        made = [tape.add("mxu", 0.063, needs, spread(row_step)) for row_step in range(3)]
        tape.add("vpu", 0.12, made, finish)

    for canvas in range(canvases):
        for place, row in enumerate(mine):
            tile(place, row, canvas)
    tape.play()
    copies = []
    for place, row in enumerate(mine):
        copies.append(
            pltpu.make_async_copy(out_ref.at[place], latent_grad_ref.at[:, row], sems.at[place])
        )
        copies[-1].start()
    for copy in copies:
        copy.wait()


class Plan:
    def __init__(self, sizes, half_rows):
        self.sizes = sizes
        bits = {axis: [(axis, b) for b in range(size.bit_length() - 1)] for axis, size in sizes.items()}
        strip, canvas = bits["strip"], bits["canvas"]
        near, far = [*canvas[:1], *strip[1:2]], strip[2:4][::-1]
        rest = [*strip[4:], *canvas[1:]]
        rest = [rest[i : i + 2] for i in range(0, len(rest), 2)]
        even, odd = [near, far, *rest], [far, near, *rest]
        stages = [tuple(zip(*pair, strict=True)) for pair in zip(even, odd, strict=True) if pair[0]]
        self.split, self.whole = stages[0], stages[1:]
        self.core = ((("strip", 0), ("strip", 0)),)
        self.half = 2 ** len(self.split)
        self.piece_rows = -(-half_rows // (self.half * half_tile)) * half_tile
        self.half_rows = self.half * self.piece_rows

    def place(self, core):
        number = 0
        for spots in self.split:
            even, odd = [(lax.axis_index(axis) // 2**bit) % 2 for axis, bit in spots]
            number = number * 2 + jnp.where(core == 0, even, odd)
        return number

    def swap(self, values, stage, step):
        width = self.sizes["canvas"]
        pairs = []
        for strip in range(self.sizes["strip"]):
            change = {"strip": 0, "canvas": 0}
            for place, spots in enumerate(reversed(stage)):
                if step >> place & 1:
                    axis, bit = spots[strip % 2]
                    change[axis] |= 1 << bit
            for canvas in range(width):
                target = (strip ^ change["strip"]) * width + (canvas ^ change["canvas"])
                pairs.append((strip * width + canvas, target))
        return lax.ppermute(values, ("strip", "canvas"), pairs)


def add_kernel(count, after, *refs):
    ins, outs = refs[:count], refs[count + after :]
    depth = outs[0].shape[0]
    for place, out_ref in enumerate(outs):
        span = pl.ds(place * depth, depth)
        terms = [ref[span].astype(wide) for ref in ins]
        while len(terms) > 1:
            terms = [sum(terms[i + 1 : i + 2], terms[i]) for i in range(0, len(terms), 2)]
        out_ref[...] = terms[0].astype(low)


def add_split(arrays, parts, after=()):
    depth, rows, channels = arrays[0].shape
    shape = jax.ShapeDtypeStruct((depth // parts, rows, channels), low)
    return pl.pallas_call(
        functools.partial(add_kernel, len(arrays), len(after)),
        in_specs=[in_vmem] * len(arrays) + [anywhere] * len(after),
        out_specs=[in_vmem] * parts,
        out_shape=[shape] * parts,
        compiler_params=pltpu.CompilerParams(vmem_limit_bytes=vmem_bytes),
    )(*arrays, *after)


def gate_kernel(*refs):
    pass


def gate(array, *after):
    return pl.pallas_call(
        gate_kernel,
        in_specs=[in_vmem] + [anywhere] * len(after),
        out_specs=in_vmem,
        out_shape=jax.ShapeDtypeStruct(array.shape, array.dtype),
        input_output_aliases={0: 0},
        compiler_params=pltpu.CompilerParams(vmem_limit_bytes=vmem_bytes),
    )(array, *after)


def final_kernel(plan, mine, count, sizes, *refs):
    ins, outs, scratch = refs[:count], refs[-15:-6], refs[-6:]
    gathered_ref, *line_refs, sems = scratch
    channels, size, entries = sizes
    core = lax.axis_index("strip") % 2
    half = core if mine else 1 - core
    place = plan.place(half)
    at = 0
    for ref in ins:
        for piece in range(ref.shape[0]):
            start = pl.multiple_of((place ^ at) * plan.piece_rows, plan.piece_rows)
            gathered_ref[pl.ds(start, plan.piece_rows)] = ref[piece].astype(wide)
            at += 1
    conv_ref, conv_bias_ref, mix_ref, mix_bias_ref, proj_ref, proj_bias_ref = outs[:6]
    codebook_ref, decode_ref, decode_bias_ref = outs[6:]
    conv_rows = 5 * channels

    def copy_all(pairs):
        copies = [
            pltpu.make_async_copy(source, target, sems.at[number])
            for number, (source, target) in enumerate(pairs)
        ]
        for copy in copies:
            copy.start()
        for copy in copies:
            copy.wait()

    def place_all(first, last, targets):
        pairs = []
        for start in range(first, last, channels):
            span = pl.ds(start, channels)
            pairs.append((gathered_ref.at[pl.ds(start - first, channels)], conv_ref.at[span]))
        at = last - first
        for target, depth in targets:
            pairs.append((gathered_ref.at[pl.ds(at, depth)], target))
            at += depth
        return pairs, at

    @pl.when(half == 0)
    def _():
        copy_all(place_all(0, conv_rows, [(proj_ref, size), (decode_ref, size)])[0])

    @pl.when(half == 1)
    def _():
        targets = [(mix_ref, channels)]
        for piece in range(0, entries, channels):
            targets.append((codebook_ref.at[:, pl.ds(piece, channels)], size))
        pairs, at = place_all(conv_rows, 9 * channels, targets)
        lines = gathered_ref[pl.ds(at, tile_rows)]
        targets = (conv_bias_ref, mix_bias_ref, decode_bias_ref, proj_bias_ref)
        for number, (line_ref, target) in enumerate(zip(line_refs, targets, strict=True)):
            line_ref[...] = lines[number : number + 1, : target.shape[1]]
            pairs.append((line_ref, target))
        copy_all(pairs)


def per_device(
    plan,
    latent_in,
    crop_code,
    code_index,
    conv_weight,
    conv_bias,
    mix_weight,
    mix_bias,
    proj_weight,
    proj_bias,
    codebook,
    decode_weight,
    decode_bias,
    out_grad,
):
    canvases, rows, across, channels = latent_in.shape
    entries, size = codebook.shape
    count = canvases * across
    total = rows * count
    strips = plan.sizes["strip"]
    struct = jax.ShapeDtypeStruct
    flat_weight = conv_weight.reshape(3, 3 * channels, channels)

    def far_away(*arrays):
        return [pltpu.with_memory_space_constraint(array, pltpu.HBM) for array in arrays]

    def call(kernel, ins, outs, shapes, scratch=(), flops=0, aliases=None):
        return pl.pallas_call(
            kernel,
            in_specs=list(ins),
            out_specs=list(outs),
            out_shape=list(shapes),
            scratch_shapes=list(scratch),
            input_output_aliases=aliases or {},
            compiler_params=pltpu.CompilerParams(vmem_limit_bytes=vmem_bytes),
            cost_estimate=pl.CostEstimate(flops=flops, bytes_accessed=0, transcendentals=0),
        )

    def trade(mate, other, split=True):
        near = [(i, i ^ 1) for i in range(strips)]
        far = [(i, i + 1) for i in range(1, strips - 1, 2)]
        far += [(target, source) for source, target in far]
        if not split:
            return lax.ppermute(mate, "strip", near), lax.ppermute(other, "strip", far)
        half = other.shape[0] // 2
        others = [lax.ppermute(part, "strip", far) for part in (other[:half], other[half:])]
        return (lax.ppermute(mate, "strip", near), *others)

    edge_shape = struct((canvases, across, channels), low)
    starts = [
        struct(crop_code.shape, crop_code.dtype),
        struct(code_index.shape, code_index.dtype),
        struct((size, entries), low),
        struct((size, channels), low),
    ]
    *edges, crop, index, near_codebook, near_decode = call(
        edge_kernel,
        [in_hbm] * 5,
        [in_vmem] * 6,
        [edge_shape, edge_shape, *starts],
        [pltpu.SemaphoreType.DMA((6,))],
    )(*far_away(latent_in, crop_code, code_index, codebook.T, decode_weight))
    mate, other = trade(*edges, split=False)
    outs = [
        struct((rows, count, 2 * size), wide),
        struct((total, entries), low),
        struct((len(bits), total, 128), low),
        struct((1, channels), wide),
        struct((rows, canvases, across, channels), low),
        struct(latent_in.shape, low),
        struct(flat_weight.shape, low),
        struct(mix_weight.shape, low),
    ]
    held = [pltpu.SemaphoreType.DMA((rows + 3,))]
    term, picks, masks, decode_bias_grad, near_grad, latent, near_weight, near_mix = call(
        code_kernel,
        [in_vmem] * 4 + [in_hbm] * 4,
        [in_vmem] * 8,
        outs,
        held,
        flops=6 * total * channels * channels,
    )(
        crop,
        index,
        near_codebook,
        near_decode,
        *far_away(out_grad, latent_in, flat_weight, mix_weight),
    )
    slab_shape = struct((total + 2 * count, 3 * channels), low)
    flat = struct((total, channels), low)
    kept = [slab_shape, flat, flat, flat, flat, flat, struct((total, 2 * size), low)]
    kept += [struct((rows, count, channels), low), struct((8, channels), wide)]
    edge_shape = struct((count, channels), low)
    inner, outer = tuple(range(1, rows - 1)), tuple(sorted({0, rows - 1}))
    shared = [masks, latent, term, near_weight, conv_bias, near_mix, mix_bias, proj_weight.T, proj_bias]

    def block_rows(beyond, halo, also, before, more):
        ins = [*shared, halo, also, *before]
        first = len(ins) - len(before)
        return call(
            functools.partial(rows_kernel, beyond),
            [in_vmem] * len(ins),
            [in_vmem] * (len(kept) + 1 + len(more)),
            [*kept, edge_shape, *more],
            flops=20 * total * channels * channels,
            aliases={first + i: i for i in range(len(before))},
        )(*ins)

    more = [struct((size, channels), wide), struct((count, channels), wide)]
    *before, edge_mate, decode_weight_grad, partial = block_rows("mate", mate, near_grad, (), more)
    *before, edge_other = block_rows("other", other, partial, before, ())
    slab, grad, up, down, second, stream, codes, branch_grad, sums = before
    edges = (edge_mate, edge_other)

    def weight_half(mine, after):
        ins = [slab, grad, up, down, second, stream, codes, branch_grad, sums, picks]
        ins += [decode_weight_grad, decode_bias_grad]
        return call(
            functools.partial(weight_kernel, plan, mine),
            [in_vmem] * len(ins) + [anywhere],
            [in_vmem],
            [struct((plan.half, plan.piece_rows, channels), low)],
            flops=10 * total * channels * channels,
        )(*ins, after)[0]

    send = weight_half(False, edge_other)
    keep = weight_half(True, send)

    def input_rows(mine, halo, after, *before):
        return call(
            functools.partial(input_kernel, mine),
            [in_vmem] * 7 + [anywhere] + [in_hbm] * len(before),
            [in_hbm],
            [pltpu.HBM(latent_in.shape, low)],
            [
                pltpu.VMEM(slab_shape.shape, low),
                pltpu.VMEM(flat_weight.shape, low),
                pltpu.VMEM((len(mine), canvases, across, channels), low),
                pltpu.SemaphoreType.DMA((len(mine),)),
            ],
            flops=11 * total * channels * channels,
            aliases={8: 0} if before else {},
        )(masks, latent, grad, *halo, branch_grad, near_weight, after, *before)[0]

    parts = add_split([keep, plan.swap(send, plan.core, 1)], plan.half)
    halo = trade(*edges, split=False)
    swaps = [plan.swap(parts[i], plan.split, i) for i in reversed(range(1, plan.half))]
    piece = add_split([parts[0], *swaps], 1)[0]
    latent_grad = input_rows(inner, edges, piece)
    decoded = call(
        decoded_kernel,
        [in_vmem, in_vmem, in_vmem, anywhere],
        [pl.BlockSpec()],
        [pltpu.HBM(out_grad.shape, low)],
        flops=4 * total * channels * channels,
    )(term, near_decode, decode_bias, piece)[0]
    after = far_away(decoded, latent_grad)
    for stage in plan.whole:
        swaps = [plan.swap(piece, stage, i) for i in range(1, 2 ** len(stage))]
        piece = add_split([piece, *swaps], 1, after)[0]
        after = []
    others = [plan.swap(piece, plan.split, i) for i in range(1, plan.half)]
    latent_grad = input_rows(outer, halo, piece, latent_grad)
    done = far_away(latent_grad)
    pieces = [piece, *[gate(other, *done) for other in others]]
    swapped = [plan.swap(piece, plan.core, 1) for piece in pieces]
    shapes = [
        (9 * channels, channels),
        (1, channels),
        (channels, channels),
        (1, channels),
        (size, channels),
        (1, size),
        (size, entries),
        (size, channels),
        (1, channels),
    ]

    def finish(mine, arrays, *before):
        count = len(arrays)
        return call(
            functools.partial(final_kernel, plan, mine, count, (channels, size, entries)),
            [in_vmem] * count + [in_hbm] * len(before),
            [in_hbm] * len(shapes),
            [pltpu.HBM(shape, wide) for shape in shapes],
            [
                pltpu.VMEM((plan.half_rows, channels), wide),
                *[pltpu.VMEM((1, channels), wide)] * 3,
                pltpu.VMEM((1, size), wide),
                pltpu.SemaphoreType.DMA((16,)),
            ],
            aliases={count + i: i for i in range(len(before))},
        )(*arrays, *before)

    results = finish(True, pieces)
    results = finish(False, swapped, *results)
    return (
        decoded,
        latent_grad,
        results[0].reshape(3, 3, channels, channels),
        results[1].reshape(-1),
        results[2],
        results[3].reshape(-1),
        results[4].T,
        results[5].reshape(-1),
        results[6].T,
        results[7],
        results[8].reshape(-1),
    )


def solution(mesh):
    sizes = {axis: mesh.shape[axis] for axis in ("strip", "canvas")}
    shared = P("canvas", "strip", None, None)
    codes = P("canvas", "strip", None)

    def wrapped(*args):
        channels = args[0].shape[3]
        entries, size = args[9].shape
        others = 5 * channels + size * (entries // channels) + tile_rows
        plan = Plan(sizes, max(5 * channels + 2 * size, others))
        return jax.shard_map(
            functools.partial(per_device, plan),
            mesh=mesh,
            in_specs=(shared, codes, codes, *[P()] * 9, shared),
            out_specs=(shared, shared, *[P()] * 9),
            check_vma=False,
        )(*args)

    return wrapped
```

```python
import functools

import jax
import jax.numpy as jnp
from jax import lax
from jax.experimental import pallas as pl
from jax.experimental.pallas import tpu as pltpu
from jax.sharding import PartitionSpec as P

commit_weight = 0.25
low = jnp.bfloat16
wide = jnp.float32
bits = (1, 3, 4, 6)
up_plane, left_plane, right_plane, down_plane = range(4)
tile_rows = 16
half_tile = 16
vmem_bytes = 20 * 2**20
in_hbm = pl.BlockSpec(memory_space=pltpu.HBM)
anywhere = pl.BlockSpec(memory_space=pl.ANY)
in_vmem = pl.BlockSpec(memory_space=pltpu.VMEM)


def mm(lhs, rhs):
    return jnp.dot(lhs, rhs, preferred_element_type=wide)


def mm_nt(lhs, rhs):
    return lax.dot_general(lhs, rhs, (((1,), (1,)), ((), ())), preferred_element_type=wide)


def mm_tn(lhs, rhs):
    return lax.dot_general(lhs, rhs, (((0,), (0,)), ((), ())), preferred_element_type=wide)


def silu(values):
    half = 0.5 * values.astype(wide)
    return half * (1.0 + jnp.tanh(half))


def silu_slopes(half):
    turn = jnp.tanh(half)
    more = 1.0 + turn
    return half * more, more * (1.0 + half * (1.0 - turn))


def code_columns(code_ref):
    canvases, rows, across = code_ref.shape
    flat = code_ref[...].reshape(canvases * rows, across)
    extra = -across % 128
    if extra:
        flat = jnp.concatenate([flat, jnp.zeros((canvases * rows, extra), flat.dtype)], axis=1)
    return flat.T[:across]


def row_codes(columns, row, canvases, rows, lanes):
    pieces = [
        jnp.broadcast_to(
            columns[:, n * rows + row : n * rows + row + 1], (columns.shape[0], lanes)
        )
        for n in range(canvases)
    ]
    return jnp.concatenate(pieces, axis=0)


def chunks(count):
    return [(at, pl.ds(at, tile_rows)) for at in range(0, count, tile_rows)]


def masked(values, masks):
    return values * jnp.concatenate([masks] * (values.shape[1] // masks.shape[1]), axis=1)


def store_slab(slab_ref, at, left, right, values):
    channels = slab_ref.shape[1] // 3
    eight = tile_rows // 2
    place = lax.broadcasted_iota(jnp.int32, (eight, channels), 0)
    steps = chunks(left.count)

    def part(number):
        here = values(steps[number][0])
        halves = here[:eight], here[eight:]
        later = [pltpu.roll(half, 1, 0) for half in halves]
        sooner = [pltpu.roll(half, eight - 1, 0) for half in halves]
        return here, later, sooner

    now = part(0)
    before = now[1][1]
    for number, (start, _) in enumerate(steps):
        new = part(number + 1) if number + 1 < len(steps) else now
        here, later, sooner = now
        span = pl.ds(at + start, tile_rows)
        shifted = [
            jnp.where(place == 0, before, later[0]),
            jnp.where(place == 0, later[0], later[1]),
        ]
        shifted = jnp.concatenate(shifted, axis=0).astype(low)
        slab_ref[span, :channels] = masked(shifted, left(start))
        slab_ref[span, channels : 2 * channels] = here.astype(low)
        shifted = [
            jnp.where(place == eight - 1, sooner[1], sooner[0]),
            jnp.where(place == eight - 1, new[2][0], sooner[1]),
        ]
        shifted = jnp.concatenate(shifted, axis=0).astype(low)
        slab_ref[span, 2 * channels :] = masked(shifted, right(start))
        before = later[1]
        now = new


class Masks:
    def __init__(self, masks_ref, plane, at, count):
        self.masks_ref, self.plane, self.at, self.count = masks_ref, plane, at, count

    def __call__(self, start):
        at = self.at + start
        if not isinstance(at, int):
            at = pl.multiple_of(at, tile_rows)
        return self.masks_ref[self.plane, pl.ds(at, tile_rows)]


class Tape:
    def __init__(self):
        self.steps = []

    def add(self, unit, cost, after, step):
        self.steps.append((unit, cost, [a for a in after if a is not None], step))
        return len(self.steps) - 1

    def play(self):
        free = {"mxu": 0.0, "vpu": 0.0}
        lag = {"mxu": 0.1, "vpu": 0.02}
        ends = {}
        left = list(range(len(self.steps)))
        while left:
            best = None
            for number in left:
                unit, _, after, _ = self.steps[number]
                if all(a in ends for a in after):
                    start = max([free[unit], *[ends[a] for a in after]])
                    if best is None or (start, number) < best:
                        best = (start, number)
            start, number = best
            unit, cost, _, step = self.steps[number]
            free[unit] = start + cost
            ends[number] = start + cost + lag[unit]
            left.remove(number)
            step()


def edge_kernel(
    latent_hbm,
    crop_hbm,
    index_hbm,
    codebook_hbm,
    decode_weight_hbm,
    mate_ref,
    other_ref,
    crop_ref,
    index_ref,
    codebook_ref,
    decode_weight_ref,
    sems,
):
    rows = crop_ref.shape[1]
    odd = lax.axis_index("strip") % 2
    edge = (rows - 1) * (1 - odd)
    pairs = [
        (latent_hbm.at[:, rows - 1 - edge], other_ref),
        (latent_hbm.at[:, edge], mate_ref),
        (crop_hbm, crop_ref),
        (index_hbm, index_ref),
        (codebook_hbm, codebook_ref),
        (decode_weight_hbm, decode_weight_ref),
    ]
    copies = [
        pltpu.make_async_copy(source, target, sems.at[place])
        for place, (source, target) in enumerate(pairs)
    ]
    for copy in copies:
        copy.start()
    for copy in copies:
        copy.wait()


def code_kernel(
    crop_ref,
    index_ref,
    codebook_ref,
    decode_weight_ref,
    out_grad_hbm,
    latent_hbm,
    conv_weight_hbm,
    mix_weight_hbm,
    term_ref,
    picks_ref,
    masks_ref,
    bias_grad_ref,
    out_grad_ref,
    latent_ref,
    conv_weight_ref,
    mix_weight_ref,
    sems,
):
    canvases, rows, across = index_ref.shape
    size, entries = codebook_ref.shape
    channels = decode_weight_ref.shape[1]
    count = canvases * across
    pairs = [(out_grad_hbm.at[:, row], out_grad_ref.at[row]) for row in range(rows)]
    pairs += [
        (conv_weight_hbm, conv_weight_ref),
        (latent_hbm, latent_ref),
        (mix_weight_hbm, mix_weight_ref),
    ]
    copies = [
        pltpu.make_async_copy(source, target, sems.at[place])
        for place, (source, target) in enumerate(pairs)
    ]
    for copy in copies:
        copy.start()
    codebook = codebook_ref[...]
    both = jnp.concatenate([codebook * low(-0.5), codebook * low(2.0)], axis=0)
    weight = decode_weight_ref[...]
    weight = jnp.concatenate([weight, jnp.zeros_like(weight)], axis=0)
    table = jnp.concatenate([both, weight], axis=1).T
    lanes = lax.broadcasted_iota(jnp.int32, (tile_rows, 128), 1)
    index_columns, crop_columns = code_columns(index_ref), code_columns(crop_ref)
    terms = [None] * rows

    def make_picks(row):
        codes = row_codes(index_columns, row, canvases, rows, 128)
        for start, _ in chunks(count):
            near = codes[start : start + tile_rows]
            for at in range(0, entries, 128):
                chosen = lanes + at == near
                part = jnp.where(chosen, 1.0, 0.0).astype(low)
                picks_ref[pl.ds(row * count + start, tile_rows), at : at + 128] = part

    def make_masks(row):
        codes = row_codes(crop_columns, row, canvases, rows, 128)
        for start, _ in chunks(count):
            near = codes[start : start + tile_rows]
            span = pl.ds(row * count + start, tile_rows)
            for plane, bit in enumerate(bits):
                masks_ref[plane, span] = jnp.where((near & 2**bit) != 0, 1.0, 0.0).astype(low)

    def look_up(row):
        picks = picks_ref[pl.ds(row * count, count)]
        terms[row] = mm(jnp.concatenate([picks, grads(row)], axis=1), table)

    def grads(row):
        return out_grad_ref[row].reshape(count, channels)

    bias_sum = []
    make_picks(0)
    make_masks(0)
    if rows > 1:
        make_picks(1)
    for copy in copies[:rows]:
        copy.wait()
    for row in range(rows):
        look_up(row)
        if row + 2 < rows:
            make_picks(row + 2)
        if row + 1 < rows:
            make_masks(row + 1)
        for start, _ in chunks(count):
            part = grads(row)[start : start + tile_rows].astype(wide)
            part = part[:8] + part[8:]
            bias_sum = [bias_sum[0] + part] if bias_sum else [part]
        term_ref[row] = terms[row]
    bias_grad_ref[...] = jnp.sum(bias_sum[0], axis=0, keepdims=True)
    for copy in copies[rows:]:
        copy.wait()
    for row_step in range(3):
        for start, span in chunks(3 * channels):
            conv_weight_ref[row_step, span] = conv_weight_ref[row_step, span] * low(0.5)


def decoded_kernel(term_ref, decode_weight_ref, decode_bias_ref, after_ref, decoded_ref):
    canvases, rows, across, channels = decoded_ref.shape
    weight = decode_weight_ref[...] * low(0.5)
    weight = jnp.concatenate([jnp.zeros_like(weight), weight], axis=0)
    bias = decode_bias_ref[...].astype(wide).reshape(1, channels)
    for row in range(rows):
        decoded = (mm(term_ref[row].astype(low), weight) + bias).astype(low)
        decoded_ref[:, row] = decoded.reshape(canvases, across, channels)


class Places:
    mate, other = "mate", "other"

    def __init__(self, rows, count):
        self.rows, self.count = rows, count
        self.odd = lax.axis_index("strip") % 2 == 1
        self.inner = list(range(1, rows - 1))

    def row(self, unit):
        if unit == self.mate:
            return jnp.where(self.odd, 0, self.rows - 1)
        if unit == self.other:
            return jnp.where(self.odd, self.rows - 1, 0)
        return unit

    def toward(self, unit):
        return jnp.where(self.odd, *((0, 2) if unit == self.mate else (2, 0)))

    def halo(self, unit):
        first, last = 0, self.rows + 1
        return jnp.where(self.odd, *((first, last) if unit == self.mate else (last, first)))

    def span(self, number, at=0, size=None):
        start = number * self.count + at
        if not isinstance(start, int):
            start = pl.multiple_of(start, tile_rows)
        return pl.ds(start, size or self.count)

    def masks(self, masks_ref, plane, unit, canvas, across):
        return Masks(masks_ref, plane, self.row(unit) * self.count + canvas * across, across)


def rows_kernel(
    beyond,
    masks_ref,
    latent_ref,
    term_ref,
    conv_weight_ref,
    conv_bias_ref,
    mix_weight_ref,
    mix_bias_ref,
    proj_weight_ref,
    proj_bias_ref,
    halo_ref,
    also_ref,
    *refs,
):
    first = beyond == Places.mate
    outs = refs[-12:] if first else refs[-10:]
    slab_ref, grad_ref, up_ref, down_ref, second_ref, stream_ref, codes_ref = outs[:7]
    branch_grad_ref, sums_ref, edge_ref = outs[7:10]
    canvases, rows, across, channels = latent_ref.shape
    size = proj_weight_ref.shape[0]
    count = canvases * across
    places = Places(rows, count)
    units = [*places.inner, places.mate] if first else [places.other]

    def own(row, canvas):
        return lambda at: silu(latent_ref[canvas, row, pl.ds(at, tile_rows)])

    def halo(canvas):
        return lambda at: silu(halo_ref[canvas, pl.ds(at, tile_rows)])

    proj = proj_weight_ref[...]
    proj_both = jnp.concatenate([proj * low(2 * commit_weight), proj * low(-2.0)], axis=0).T
    mix_back = (mix_weight_ref[...] * low(0.5)).T
    proj_top = jnp.concatenate([proj, jnp.zeros_like(proj)], axis=0)
    conv_bias = 0.5 * conv_bias_ref[...].astype(wide).reshape(1, channels)
    mix_bias = mix_bias_ref[...].astype(wide).reshape(1, channels)
    proj_bias = proj_bias_ref[...].astype(wide).reshape(1, size)
    proj_bias = jnp.concatenate([2 * commit_weight * proj_bias, -2.0 * proj_bias], axis=1)
    sums = [None, None, None]
    steps = chunks(across)
    tape = Tape()
    slabs = {}

    def add_to(place, values):
        values = values[:8] + values[8:]
        sums[place] = values if sums[place] is None else sums[place] + values

    def slab_of(row, canvas):
        if row != beyond and (not first or row == places.other):
            return None
        if (row, canvas) not in slabs:
            if row == beyond:
                place, values = places.halo(beyond), halo(canvas)
            else:
                place, values = row + 1, own(row, canvas)
            sides = [
                places.masks(masks_ref, plane, row, canvas, across)
                for plane in (left_plane, right_plane)
            ]
            start = places.span(place, canvas * across).start
            slabs[row, canvas] = tape.add(
                "vpu", 0.08, [], lambda: store_slab(slab_ref, start, *sides, values)
            )
        return slabs[row, canvas]

    group = canvases if first else 1

    def tile(unit, canvas):
        inside = canvas * across
        there = places.row(unit)
        here = places.span(there, inside, group * across)
        above, below = [
            places.masks(masks_ref, plane, unit, canvas, across) for plane in (up_plane, down_plane)
        ]
        if unit == places.other:
            plane = jnp.where(places.odd, down_plane, up_plane)
            halo_masks = places.masks(masks_ref, plane, unit, canvas, across)
        conv, slope, made = [None] * 3, [], [None] * 4
        steps = chunks(group * across)

        def span(start):
            return places.span(there, inside + start, tile_rows)

        def multiply(place, step):
            def run():
                made[place] = step()

            return run

        def convolve(row_step):
            def run():
                rows_of = places.span(there + row_step, inside, group * across)
                conv[row_step] = mm(slab_ref[rows_of], conv_weight_ref[row_step])

            return run

        def convolve_halo():
            rows_of = places.span(places.halo(unit), inside, group * across)
            conv[0] = mm(slab_ref[rows_of], conv_weight_ref[places.toward(unit)])

        def activate():
            up, mid, down = conv
            for start, _ in steps:
                some = slice(start, start + tile_rows)
                if unit == places.other:
                    total = masked(up[some], halo_masks(start).astype(wide))
                    total = total + also_ref[pl.ds(inside + start, tile_rows)]
                else:
                    total = masked(up[some], above(start).astype(wide))
                    total = total + masked(down[some], below(start).astype(wide)) + mid[some]
                second, twice = silu_slopes(total + conv_bias)
                second_ref[span(start)] = second.astype(low)
                slope.append(twice)

        def add_latent():
            for start, _ in steps:
                latent = latent_ref[canvas + start // across, there, pl.ds(start % across, tile_rows)].astype(wide)
                part = latent + (made[0][start : start + tile_rows] + mix_bias)
                stream_ref[span(start)] = part.astype(low)

        def add_term():
            for start, _ in steps:
                part = made[1][start : start + tile_rows]
                part = part + (term_ref[there, pl.ds(inside + start, tile_rows)] + proj_bias)
                codes_ref[span(start)] = part.astype(low)
                add_to(2, part)

        def keep_branch():
            for start, _ in steps:
                part = made[2][start : start + tile_rows]
                branch_grad_ref[there, pl.ds(inside + start, tile_rows)] = part.astype(low)
                add_to(1, part)

        def keep_grad():
            for place, (start, _) in enumerate(steps):
                some = slice(start, start + tile_rows)
                part = made[3][some] * slope[place]
                rounded = part.astype(low)
                grad_ref[span(start)] = rounded
                up_ref[span(start)] = masked(rounded, above(start))
                down_ref[span(start)] = masked(rounded, below(start))
                if unit == beyond:
                    edge_ref[pl.ds(inside + start, tile_rows)] = rounded
                add_to(0, part)

        if unit == places.mate:
            needs = [*range(rows), unit]
        elif unit == places.other:
            needs = [unit]
        else:
            needs = [unit - 1, unit, unit + 1]
        needs = [slab_of(near, canvas + k) for near in needs for k in range(group)]
        if unit == places.other:
            last = [tape.add("mxu", 0.063 * group, needs, convolve_halo)]
        else:
            last = [tape.add("mxu", 0.063 * group, needs, convolve(row_step)) for row_step in range(3)]
        last = tape.add("vpu", 0.1 * group, last, activate)
        chain = [
            (0.021, lambda: mm(second_ref[here], mix_weight_ref[...]), 0.04, add_latent),
            (0.021, lambda: mm(stream_ref[here], proj_both), 0.03, add_term),
            (0.021, lambda: mm(codes_ref[here], proj_top), 0.03, keep_branch),
            (
                0.021,
                lambda: mm(branch_grad_ref[there, pl.ds(inside, group * across)], mix_back),
                0.07,
                keep_grad,
            ),
        ]
        for place, (cost, product, later, rest) in enumerate(chain):
            last = tape.add("mxu", cost * group, [last], multiply(place, product))
            last = tape.add("vpu", later * group, [last], rest)

    def weigh():
        box = [None]

        def product(row):
            def run():
                part = mm_tn(term_ref[row].astype(low), also_ref[row].reshape(count, channels))
                box[0] = part if box[0] is None else box[0] + part

            return run

        def store():
            refs[-2][...] = 0.5 * box[0][size:]

        made = [tape.add("mxu", 0.12, [], product(row)) for row in range(rows)]
        tape.add("vpu", 0.02, made, store)

    def convolve_last(canvas, some):
        there = places.row(places.other)
        inward = jnp.where(places.odd, -1, 1)
        plane = jnp.where(places.odd, up_plane, down_plane)
        masks = places.masks(masks_ref, plane, places.other, canvas, across)
        inside = canvas * across
        made = [None, None]

        def product(place, row, tap):
            def run():
                rows_of = places.span(row + 1, inside, some * across)
                made[place] = mm(slab_ref[rows_of], conv_weight_ref[tap])

            return run

        def store():
            for start, _ in chunks(some * across):
                near = slice(start, start + tile_rows)
                part = made[0][near] + masked(made[1][near], masks(start).astype(wide))
                refs[-1][pl.ds(inside + start, tile_rows)] = part

        needs = [slab_of(row, canvas + k) for row in range(rows) for k in range(some)]
        steps = [(there, 1), (there + inward, inward + 1)]
        needs = [
            tape.add("mxu", 0.063 * some, needs, product(place, *step))
            for place, step in enumerate(steps)
        ]
        tape.add("vpu", 0.04 * some, needs, store)

    if first:
        weigh()
    for unit in units:
        for canvas in range(0, canvases, group):
            tile(unit, canvas)
    if first:
        some = 2 if canvases % 2 == 0 else 1
        for canvas in range(0, canvases, some):
            convolve_last(canvas, some)
    tape.play()
    sums = [jnp.sum(values, axis=0, keepdims=True) for values in sums]
    sums[2] = jnp.concatenate([sums[2]] * (channels // sums[2].shape[1]), axis=1)
    blank = jnp.zeros((sums_ref.shape[0] - 3, channels), wide)
    sums = jnp.concatenate([*sums, blank], axis=0)
    sums_ref[...] = sums if first else sums + refs[8][...]


def weight_kernel(
    plan,
    mine,
    slab_ref,
    grad_ref,
    up_ref,
    down_ref,
    second_ref,
    stream_ref,
    codes_ref,
    branch_grad_ref,
    sums_ref,
    picks_ref,
    decode_weight_grad_ref,
    decode_bias_grad_ref,
    after_ref,
    out_ref,
):
    total, channels = grad_ref.shape
    rows, count, _ = branch_grad_ref.shape
    size = decode_weight_grad_ref.shape[0]
    entries = picks_ref.shape[1]
    core = lax.axis_index("strip") % 2
    wanted = core if mine else 1 - core
    place = plan.place(wanted)

    def step(row_step, weighted_ref, first, last):
        span, lanes = pl.ds(row_step * count, total), pl.ds(first * channels, (last - first) * channels)
        return (last - first) * channels, lambda: mm_tn(slab_ref[span, lanes], weighted_ref[...])

    def fill(parts):
        piece, had = [], 0
        at = 0
        rest = plan.half_rows - sum(depth for depth, _ in parts)
        for depth, part in [*parts, (rest, lambda: jnp.zeros((rest, channels), wide))]:
            values = part() if depth else None
            start = 0
            while start < depth:
                some = min(depth - start, plan.piece_rows - had)
                piece.append(values[start : start + some])
                start += some
                had += some
                if had == plan.piece_rows:
                    out_ref[at ^ place] = jnp.concatenate(piece, axis=0).astype(low)
                    piece, had = [], 0
                    at += 1

    @pl.when(wanted == 0)
    def _():
        fill(
            [
                step(0, up_ref, 0, 3),
                step(1, grad_ref, 0, 2),
                (size, lambda: mm_tn(codes_ref[...], stream_ref[...])[:size]),
                (size, lambda: decode_weight_grad_ref[...]),
            ]
        )

    @pl.when(wanted == 1)
    def _():
        sums = sums_ref[...]
        biases = [sums[0:1], sums[1:2], decode_bias_grad_ref[...], sums[2:3]]
        biases.append(jnp.zeros((tile_rows - len(biases), channels), wide))

        def picked():
            part = mm_tn(codes_ref[...], picks_ref[...])[size:]
            return jnp.concatenate([part[:, i : i + channels] for i in range(0, entries, channels)], axis=0)

        fill(
            [
                step(1, grad_ref, 2, 3),
                step(2, down_ref, 0, 3),
                (channels, lambda: mm_tn(second_ref[...], branch_grad_ref[...].reshape(total, channels))),
                (size * (entries // channels), picked),
                (tile_rows, lambda: jnp.concatenate(biases, axis=0)),
            ]
        )


def input_kernel(
    mine,
    masks_ref,
    latent_ref,
    grad_ref,
    mate_ref,
    other_ref,
    branch_grad_ref,
    conv_weight_ref,
    after_ref,
    *refs,
):
    latent_grad_ref, slab_ref, back_ref, out_ref, sems = refs[-5:]
    canvases, rows, across, channels = latent_ref.shape
    count = canvases * across
    places = Places(rows, count)
    steps = chunks(across)
    tape = Tape()

    def own(row, canvas):
        start = row * count + canvas * across
        return lambda at: grad_ref[pl.ds(start + at, tile_rows)].astype(wide)

    def beside(mate, canvas):
        def values(at):
            span = pl.ds(canvas * across + at, tile_rows)
            return jnp.where(mate, mate_ref[span], other_ref[span]).astype(wide)

        return values

    for row_step in range(3):
        for col_step in range(3):
            lanes = slice((2 - col_step) * channels, (3 - col_step) * channels)
            turned = conv_weight_ref[2 - row_step, lanes].T
            back_ref[row_step, col_step * channels : (col_step + 1) * channels] = turned

    slabs = {}

    def slab_of(row, canvas):
        if (row, canvas) not in slabs:
            if row < 0:
                values = beside(places.odd, canvas)
            elif row == rows:
                values = beside(jnp.logical_not(places.odd), canvas)
            else:
                values = own(row, canvas)
            near = min(max(row, 0), rows - 1)
            sides = [
                places.masks(masks_ref, plane, near, canvas, across)
                for plane in (left_plane, right_plane)
            ]
            start = (row + 1) * count + canvas * across
            slabs[row, canvas] = tape.add(
                "vpu", 0.07, [], lambda: store_slab(slab_ref, start, *sides, values)
            )
        return slabs[row, canvas]

    def tile(place, row, canvas):
        inside = canvas * across
        above, below = [
            places.masks(masks_ref, plane, row, canvas, across) for plane in (up_plane, down_plane)
        ]
        spreads = [None] * 3

        def spread(row_step):
            def run():
                span = pl.ds((row + row_step) * count + inside, across)
                spreads[row_step] = mm(slab_ref[span], back_ref[row_step])

            return run

        def finish():
            for start, _ in steps:
                some = slice(start, start + tile_rows)
                total = masked(spreads[0][some], above(start).astype(wide))
                total = total + masked(spreads[2][some], below(start).astype(wide))
                total = total + spreads[1][some]
                near = pl.ds(start, tile_rows)
                _, twice = silu_slopes(0.5 * latent_ref[canvas, row, near].astype(wide))
                stream = branch_grad_ref[row, pl.ds(inside + start, tile_rows)]
                out_ref[place, canvas, near] = (stream.astype(wide) + total * twice).astype(low)

        needs = [slab_of(near, canvas) for near in (row - 1, row, row + 1)]
        made = [tape.add("mxu", 0.063, needs, spread(row_step)) for row_step in range(3)]
        tape.add("vpu", 0.12, made, finish)

    for canvas in range(canvases):
        for place, row in enumerate(mine):
            tile(place, row, canvas)
    tape.play()
    copies = []
    for place, row in enumerate(mine):
        copies.append(
            pltpu.make_async_copy(out_ref.at[place], latent_grad_ref.at[:, row], sems.at[place])
        )
        copies[-1].start()
    for copy in copies:
        copy.wait()


class Plan:
    def __init__(self, sizes, half_rows):
        self.sizes = sizes
        bits = {axis: [(axis, b) for b in range(size.bit_length() - 1)] for axis, size in sizes.items()}
        strip, canvas = bits["strip"], bits["canvas"]
        near, far = [*canvas[:1], *strip[1:2]], strip[2:4][::-1]
        rest = [*strip[4:], *canvas[1:]]
        rest = [rest[i : i + 2] for i in range(0, len(rest), 2)]
        even, odd = [near, far, *rest], [far, near, *rest]
        stages = [tuple(zip(*pair, strict=True)) for pair in zip(even, odd, strict=True) if pair[0]]
        self.split, self.whole = stages[0], stages[1:]
        self.core = ((("strip", 0), ("strip", 0)),)
        self.half = 2 ** len(self.split)
        self.piece_rows = -(-half_rows // (self.half * half_tile)) * half_tile
        self.half_rows = self.half * self.piece_rows

    def place(self, core):
        number = 0
        for spots in self.split:
            even, odd = [(lax.axis_index(axis) // 2**bit) % 2 for axis, bit in spots]
            number = number * 2 + jnp.where(core == 0, even, odd)
        return number

    def swap(self, values, stage, step):
        width = self.sizes["canvas"]
        pairs = []
        for strip in range(self.sizes["strip"]):
            change = {"strip": 0, "canvas": 0}
            for place, spots in enumerate(reversed(stage)):
                if step >> place & 1:
                    axis, bit = spots[strip % 2]
                    change[axis] |= 1 << bit
            for canvas in range(width):
                target = (strip ^ change["strip"]) * width + (canvas ^ change["canvas"])
                pairs.append((strip * width + canvas, target))
        return lax.ppermute(values, ("strip", "canvas"), pairs)


def add_kernel(count, after, *refs):
    ins, outs = refs[:count], refs[count + after :]
    depth = outs[0].shape[0]
    for place, out_ref in enumerate(outs):
        span = pl.ds(place * depth, depth)
        terms = [ref[span].astype(wide) for ref in ins]
        while len(terms) > 1:
            terms = [sum(terms[i + 1 : i + 2], terms[i]) for i in range(0, len(terms), 2)]
        out_ref[...] = terms[0].astype(low)


def add_split(arrays, parts, after=()):
    depth, rows, channels = arrays[0].shape
    shape = jax.ShapeDtypeStruct((depth // parts, rows, channels), low)
    return pl.pallas_call(
        functools.partial(add_kernel, len(arrays), len(after)),
        in_specs=[in_vmem] * len(arrays) + [anywhere] * len(after),
        out_specs=[in_vmem] * parts,
        out_shape=[shape] * parts,
        compiler_params=pltpu.CompilerParams(vmem_limit_bytes=vmem_bytes),
    )(*arrays, *after)


def gate_kernel(*refs):
    pass


def gate(array, *after):
    return pl.pallas_call(
        gate_kernel,
        in_specs=[in_vmem] + [anywhere] * len(after),
        out_specs=in_vmem,
        out_shape=jax.ShapeDtypeStruct(array.shape, array.dtype),
        input_output_aliases={0: 0},
        compiler_params=pltpu.CompilerParams(vmem_limit_bytes=vmem_bytes),
    )(array, *after)


def final_kernel(plan, mine, count, sizes, *refs):
    ins, outs, scratch = refs[:count], refs[-15:-6], refs[-6:]
    gathered_ref, *line_refs, sems = scratch
    channels, size, entries = sizes
    core = lax.axis_index("strip") % 2
    half = core if mine else 1 - core
    place = plan.place(half)
    at = 0
    for ref in ins:
        for piece in range(ref.shape[0]):
            start = pl.multiple_of((place ^ at) * plan.piece_rows, plan.piece_rows)
            gathered_ref[pl.ds(start, plan.piece_rows)] = ref[piece].astype(wide)
            at += 1
    conv_ref, conv_bias_ref, mix_ref, mix_bias_ref, proj_ref, proj_bias_ref = outs[:6]
    codebook_ref, decode_ref, decode_bias_ref = outs[6:]
    conv_rows = 5 * channels

    def copy_all(pairs):
        copies = [
            pltpu.make_async_copy(source, target, sems.at[number])
            for number, (source, target) in enumerate(pairs)
        ]
        for copy in copies:
            copy.start()
        for copy in copies:
            copy.wait()

    def place_all(first, last, targets):
        pairs = []
        for start in range(first, last, channels):
            span = pl.ds(start, channels)
            pairs.append((gathered_ref.at[pl.ds(start - first, channels)], conv_ref.at[span]))
        at = last - first
        for target, depth in targets:
            pairs.append((gathered_ref.at[pl.ds(at, depth)], target))
            at += depth
        return pairs, at

    @pl.when(half == 0)
    def _():
        copy_all(place_all(0, conv_rows, [(proj_ref, size), (decode_ref, size)])[0])

    @pl.when(half == 1)
    def _():
        targets = [(mix_ref, channels)]
        for piece in range(0, entries, channels):
            targets.append((codebook_ref.at[:, pl.ds(piece, channels)], size))
        pairs, at = place_all(conv_rows, 9 * channels, targets)
        lines = gathered_ref[pl.ds(at, tile_rows)]
        targets = (conv_bias_ref, mix_bias_ref, decode_bias_ref, proj_bias_ref)
        for number, (line_ref, target) in enumerate(zip(line_refs, targets, strict=True)):
            line_ref[...] = lines[number : number + 1, : target.shape[1]]
            pairs.append((line_ref, target))
        copy_all(pairs)


def per_device(
    plan,
    latent_in,
    crop_code,
    code_index,
    conv_weight,
    conv_bias,
    mix_weight,
    mix_bias,
    proj_weight,
    proj_bias,
    codebook,
    decode_weight,
    decode_bias,
    out_grad,
):
    canvases, rows, across, channels = latent_in.shape
    entries, size = codebook.shape
    count = canvases * across
    total = rows * count
    strips = plan.sizes["strip"]
    struct = jax.ShapeDtypeStruct
    flat_weight = conv_weight.reshape(3, 3 * channels, channels)

    def far_away(*arrays):
        return [pltpu.with_memory_space_constraint(array, pltpu.HBM) for array in arrays]

    def call(kernel, ins, outs, shapes, scratch=(), flops=0, aliases=None):
        return pl.pallas_call(
            kernel,
            in_specs=list(ins),
            out_specs=list(outs),
            out_shape=list(shapes),
            scratch_shapes=list(scratch),
            input_output_aliases=aliases or {},
            compiler_params=pltpu.CompilerParams(vmem_limit_bytes=vmem_bytes),
            cost_estimate=pl.CostEstimate(flops=flops, bytes_accessed=0, transcendentals=0),
        )

    def trade(mate, other, split=True):
        near = [(i, i ^ 1) for i in range(strips)]
        far = [(i, i + 1) for i in range(1, strips - 1, 2)]
        far += [(target, source) for source, target in far]
        if not split:
            return lax.ppermute(mate, "strip", near), lax.ppermute(other, "strip", far)
        half = other.shape[0] // 2
        others = [lax.ppermute(part, "strip", far) for part in (other[:half], other[half:])]
        return (lax.ppermute(mate, "strip", near), *others)

    edge_shape = struct((canvases, across, channels), low)
    starts = [
        struct(crop_code.shape, crop_code.dtype),
        struct(code_index.shape, code_index.dtype),
        struct((size, entries), low),
        struct((size, channels), low),
    ]
    *edges, crop, index, near_codebook, near_decode = call(
        edge_kernel,
        [in_hbm] * 5,
        [in_vmem] * 6,
        [edge_shape, edge_shape, *starts],
        [pltpu.SemaphoreType.DMA((6,))],
    )(*far_away(latent_in, crop_code, code_index, codebook.T, decode_weight))
    mate, other = trade(*edges, split=False)
    outs = [
        struct((rows, count, 2 * size), wide),
        struct((total, entries), low),
        struct((len(bits), total, 128), low),
        struct((1, channels), wide),
        struct((rows, canvases, across, channels), low),
        struct(latent_in.shape, low),
        struct(flat_weight.shape, low),
        struct(mix_weight.shape, low),
    ]
    held = [pltpu.SemaphoreType.DMA((rows + 3,))]
    term, picks, masks, decode_bias_grad, near_grad, latent, near_weight, near_mix = call(
        code_kernel,
        [in_vmem] * 4 + [in_hbm] * 4,
        [in_vmem] * 8,
        outs,
        held,
        flops=6 * total * channels * channels,
    )(
        crop,
        index,
        near_codebook,
        near_decode,
        *far_away(out_grad, latent_in, flat_weight, mix_weight),
    )
    slab_shape = struct((total + 2 * count, 3 * channels), low)
    flat = struct((total, channels), low)
    kept = [slab_shape, flat, flat, flat, flat, flat, struct((total, 2 * size), low)]
    kept += [struct((rows, count, channels), low), struct((8, channels), wide)]
    edge_shape = struct((count, channels), low)
    inner, outer = tuple(range(1, rows - 1)), tuple(sorted({0, rows - 1}))
    shared = [masks, latent, term, near_weight, conv_bias, near_mix, mix_bias, proj_weight.T, proj_bias]

    def block_rows(beyond, halo, also, before, more):
        ins = [*shared, halo, also, *before]
        first = len(ins) - len(before)
        return call(
            functools.partial(rows_kernel, beyond),
            [in_vmem] * len(ins),
            [in_vmem] * (len(kept) + 1 + len(more)),
            [*kept, edge_shape, *more],
            flops=20 * total * channels * channels,
            aliases={first + i: i for i in range(len(before))},
        )(*ins)

    more = [struct((size, channels), wide), struct((count, channels), wide)]
    *before, edge_mate, decode_weight_grad, partial = block_rows("mate", mate, near_grad, (), more)
    *before, edge_other = block_rows("other", other, partial, before, ())
    slab, grad, up, down, second, stream, codes, branch_grad, sums = before
    edges = (edge_mate, edge_other)

    def weight_half(mine, after):
        ins = [slab, grad, up, down, second, stream, codes, branch_grad, sums, picks]
        ins += [decode_weight_grad, decode_bias_grad]
        return call(
            functools.partial(weight_kernel, plan, mine),
            [in_vmem] * len(ins) + [anywhere],
            [in_vmem],
            [struct((plan.half, plan.piece_rows, channels), low)],
            flops=10 * total * channels * channels,
        )(*ins, after)[0]

    send = weight_half(False, edge_other)
    keep = weight_half(True, send)

    def input_rows(mine, halo, after, *before):
        return call(
            functools.partial(input_kernel, mine),
            [in_vmem] * 7 + [anywhere] + [in_hbm] * len(before),
            [in_hbm],
            [pltpu.HBM(latent_in.shape, low)],
            [
                pltpu.VMEM(slab_shape.shape, low),
                pltpu.VMEM(flat_weight.shape, low),
                pltpu.VMEM((len(mine), canvases, across, channels), low),
                pltpu.SemaphoreType.DMA((len(mine),)),
            ],
            flops=11 * total * channels * channels,
            aliases={8: 0} if before else {},
        )(masks, latent, grad, *halo, branch_grad, near_weight, after, *before)[0]

    parts = add_split([keep, plan.swap(send, plan.core, 1)], plan.half)
    halo = trade(*edges, split=False)
    swaps = [plan.swap(parts[i], plan.split, i) for i in reversed(range(1, plan.half))]
    piece = add_split([parts[0], *swaps], 1)[0]
    latent_grad = input_rows(inner, edges, piece)
    decoded = call(
        decoded_kernel,
        [in_vmem, in_vmem, in_vmem, anywhere],
        [pl.BlockSpec()],
        [pltpu.HBM(out_grad.shape, low)],
        flops=4 * total * channels * channels,
    )(term, near_decode, decode_bias, piece)[0]
    after = far_away(decoded, latent_grad)
    for stage in plan.whole:
        swaps = [plan.swap(piece, stage, i) for i in range(1, 2 ** len(stage))]
        piece = add_split([piece, *swaps], 1, after)[0]
        after = []
    others = [plan.swap(piece, plan.split, i) for i in range(1, plan.half)]
    latent_grad = input_rows(outer, halo, piece, latent_grad)
    done = far_away(latent_grad)
    pieces = [piece, *[gate(other, *done) for other in others]]
    swapped = [plan.swap(piece, plan.core, 1) for piece in pieces]
    shapes = [
        (9 * channels, channels),
        (1, channels),
        (channels, channels),
        (1, channels),
        (size, channels),
        (1, size),
        (size, entries),
        (size, channels),
        (1, channels),
    ]

    def finish(mine, arrays, *before):
        count = len(arrays)
        return call(
            functools.partial(final_kernel, plan, mine, count, (channels, size, entries)),
            [in_vmem] * count + [in_hbm] * len(before),
            [in_hbm] * len(shapes),
            [pltpu.HBM(shape, wide) for shape in shapes],
            [
                pltpu.VMEM((plan.half_rows, channels), wide),
                *[pltpu.VMEM((1, channels), wide)] * 3,
                pltpu.VMEM((1, size), wide),
                pltpu.SemaphoreType.DMA((16,)),
            ],
            aliases={count + i: i for i in range(len(before))},
        )(*arrays, *before)

    results = finish(True, pieces)
    results = finish(False, swapped, *results)
    return (
        decoded,
        latent_grad,
        results[0].reshape(3, 3, channels, channels),
        results[1].reshape(-1),
        results[2],
        results[3].reshape(-1),
        results[4].T,
        results[5].reshape(-1),
        results[6].T,
        results[7],
        results[8].reshape(-1),
    )


def solution(mesh):
    sizes = {axis: mesh.shape[axis] for axis in ("strip", "canvas")}
    shared = P("canvas", "strip", None, None)
    codes = P("canvas", "strip", None)

    def wrapped(*args):
        channels = args[0].shape[3]
        entries, size = args[9].shape
        others = 5 * channels + size * (entries // channels) + tile_rows
        plan = Plan(sizes, max(5 * channels + 2 * size, others))
        return jax.shard_map(
            functools.partial(per_device, plan),
            mesh=mesh,
            in_specs=(shared, codes, codes, *[P()] * 9, shared),
            out_specs=(shared, shared, *[P()] * 9),
            check_vma=False,
        )(*args)

    return wrapped
```

```python
import functools

import jax
import jax.numpy as jnp
from jax import lax
from jax.experimental import pallas as pl
from jax.experimental.pallas import tpu as pltpu
from jax.sharding import PartitionSpec as P

commit_weight = 0.25
low = jnp.bfloat16
wide = jnp.float32
bits = (1, 3, 4, 6)
up_plane, left_plane, right_plane, down_plane = range(4)
tile_rows = 16
half_tile = 16
vmem_bytes = 20 * 2**20
in_hbm = pl.BlockSpec(memory_space=pltpu.HBM)
anywhere = pl.BlockSpec(memory_space=pl.ANY)
in_vmem = pl.BlockSpec(memory_space=pltpu.VMEM)


def mm(lhs, rhs):
    return jnp.dot(lhs, rhs, preferred_element_type=wide)


def mm_nt(lhs, rhs):
    return lax.dot_general(lhs, rhs, (((1,), (1,)), ((), ())), preferred_element_type=wide)


def mm_tn(lhs, rhs):
    return lax.dot_general(lhs, rhs, (((0,), (0,)), ((), ())), preferred_element_type=wide)


def silu(values):
    half = 0.5 * values.astype(wide)
    return half * (1.0 + jnp.tanh(half))


def silu_slopes(half):
    turn = jnp.tanh(half)
    more = 1.0 + turn
    return half * more, more * (1.0 + half * (1.0 - turn))


def code_columns(code_ref):
    canvases, rows, across = code_ref.shape
    flat = code_ref[...].reshape(canvases * rows, across)
    extra = -across % 128
    if extra:
        flat = jnp.concatenate([flat, jnp.zeros((canvases * rows, extra), flat.dtype)], axis=1)
    return flat.T[:across]


def row_codes(columns, row, canvases, rows, lanes):
    pieces = [
        jnp.broadcast_to(
            columns[:, n * rows + row : n * rows + row + 1], (columns.shape[0], lanes)
        )
        for n in range(canvases)
    ]
    return jnp.concatenate(pieces, axis=0)


def chunks(count):
    return [(at, pl.ds(at, tile_rows)) for at in range(0, count, tile_rows)]


def masked(values, masks):
    return values * jnp.concatenate([masks] * (values.shape[1] // masks.shape[1]), axis=1)


def store_slab(slab_ref, at, left, right, values):
    channels = slab_ref.shape[1] // 3
    eight = tile_rows // 2
    place = lax.broadcasted_iota(jnp.int32, (eight, channels), 0)
    steps = chunks(left.count)

    def part(number):
        here = values(steps[number][0])
        halves = here[:eight], here[eight:]
        later = [pltpu.roll(half, 1, 0) for half in halves]
        sooner = [pltpu.roll(half, eight - 1, 0) for half in halves]
        return here, later, sooner

    now = part(0)
    before = now[1][1]
    for number, (start, _) in enumerate(steps):
        new = part(number + 1) if number + 1 < len(steps) else now
        here, later, sooner = now
        span = pl.ds(at + start, tile_rows)
        shifted = [
            jnp.where(place == 0, before, later[0]),
            jnp.where(place == 0, later[0], later[1]),
        ]
        shifted = jnp.concatenate(shifted, axis=0).astype(low)
        slab_ref[span, :channels] = masked(shifted, left(start))
        slab_ref[span, channels : 2 * channels] = here.astype(low)
        shifted = [
            jnp.where(place == eight - 1, sooner[1], sooner[0]),
            jnp.where(place == eight - 1, new[2][0], sooner[1]),
        ]
        shifted = jnp.concatenate(shifted, axis=0).astype(low)
        slab_ref[span, 2 * channels :] = masked(shifted, right(start))
        before = later[1]
        now = new


class Masks:
    def __init__(self, masks_ref, plane, at, count):
        self.masks_ref, self.plane, self.at, self.count = masks_ref, plane, at, count

    def __call__(self, start):
        at = self.at + start
        if not isinstance(at, int):
            at = pl.multiple_of(at, tile_rows)
        return self.masks_ref[self.plane, pl.ds(at, tile_rows)]


class Tape:
    def __init__(self):
        self.steps = []

    def add(self, unit, cost, after, step):
        self.steps.append((unit, cost, [a for a in after if a is not None], step))
        return len(self.steps) - 1

    def play(self):
        free = {"mxu": 0.0, "vpu": 0.0}
        lag = {"mxu": 0.1, "vpu": 0.02}
        ends = {}
        left = list(range(len(self.steps)))
        while left:
            best = None
            for number in left:
                unit, _, after, _ = self.steps[number]
                if all(a in ends for a in after):
                    start = max([free[unit], *[ends[a] for a in after]])
                    if best is None or (start, number) < best:
                        best = (start, number)
            start, number = best
            unit, cost, _, step = self.steps[number]
            free[unit] = start + cost
            ends[number] = start + cost + lag[unit]
            left.remove(number)
            step()


def edge_kernel(
    latent_hbm,
    crop_hbm,
    index_hbm,
    codebook_hbm,
    decode_weight_hbm,
    mate_ref,
    other_ref,
    crop_ref,
    index_ref,
    codebook_ref,
    decode_weight_ref,
    sems,
):
    rows = crop_ref.shape[1]
    odd = lax.axis_index("strip") % 2
    edge = (rows - 1) * (1 - odd)
    pairs = [
        (latent_hbm.at[:, rows - 1 - edge], other_ref),
        (latent_hbm.at[:, edge], mate_ref),
        (crop_hbm, crop_ref),
        (index_hbm, index_ref),
        (codebook_hbm, codebook_ref),
        (decode_weight_hbm, decode_weight_ref),
    ]
    copies = [
        pltpu.make_async_copy(source, target, sems.at[place])
        for place, (source, target) in enumerate(pairs)
    ]
    for copy in copies:
        copy.start()
    for copy in copies:
        copy.wait()


def code_kernel(
    crop_ref,
    index_ref,
    codebook_ref,
    decode_weight_ref,
    out_grad_hbm,
    latent_hbm,
    conv_weight_hbm,
    mix_weight_hbm,
    term_ref,
    picks_ref,
    masks_ref,
    bias_grad_ref,
    out_grad_ref,
    latent_ref,
    conv_weight_ref,
    mix_weight_ref,
    sems,
):
    canvases, rows, across = index_ref.shape
    size, entries = codebook_ref.shape
    channels = decode_weight_ref.shape[1]
    count = canvases * across
    pairs = [(out_grad_hbm.at[:, row], out_grad_ref.at[row]) for row in range(rows)]
    pairs += [
        (conv_weight_hbm, conv_weight_ref),
        (latent_hbm, latent_ref),
        (mix_weight_hbm, mix_weight_ref),
    ]
    copies = [
        pltpu.make_async_copy(source, target, sems.at[place])
        for place, (source, target) in enumerate(pairs)
    ]
    for copy in copies:
        copy.start()
    codebook = codebook_ref[...]
    both = jnp.concatenate([codebook * low(-0.5), codebook * low(2.0)], axis=0)
    weight = decode_weight_ref[...]
    weight = jnp.concatenate([weight, jnp.zeros_like(weight)], axis=0)
    table = jnp.concatenate([both, weight], axis=1).T
    lanes = lax.broadcasted_iota(jnp.int32, (tile_rows, 128), 1)
    index_columns, crop_columns = code_columns(index_ref), code_columns(crop_ref)
    terms = [None] * rows

    def make_picks(row):
        codes = row_codes(index_columns, row, canvases, rows, 128)
        for start, _ in chunks(count):
            near = codes[start : start + tile_rows]
            for at in range(0, entries, 128):
                chosen = lanes + at == near
                part = jnp.where(chosen, 1.0, 0.0).astype(low)
                picks_ref[pl.ds(row * count + start, tile_rows), at : at + 128] = part

    def make_masks(row):
        codes = row_codes(crop_columns, row, canvases, rows, 128)
        for start, _ in chunks(count):
            near = codes[start : start + tile_rows]
            span = pl.ds(row * count + start, tile_rows)
            for plane, bit in enumerate(bits):
                masks_ref[plane, span] = jnp.where((near & 2**bit) != 0, 1.0, 0.0).astype(low)

    def look_up(row):
        picks = picks_ref[pl.ds(row * count, count)]
        terms[row] = mm(jnp.concatenate([picks, grads(row)], axis=1), table)

    def grads(row):
        return out_grad_ref[row].reshape(count, channels)

    bias_sum = []
    make_picks(0)
    make_masks(0)
    if rows > 1:
        make_picks(1)
    for copy in copies[:rows]:
        copy.wait()
    for row in range(rows):
        look_up(row)
        if row + 2 < rows:
            make_picks(row + 2)
        if row + 1 < rows:
            make_masks(row + 1)
        for start, _ in chunks(count):
            part = grads(row)[start : start + tile_rows].astype(wide)
            part = part[:8] + part[8:]
            bias_sum = [bias_sum[0] + part] if bias_sum else [part]
        term_ref[row] = terms[row]
    bias_grad_ref[...] = jnp.sum(bias_sum[0], axis=0, keepdims=True)
    for copy in copies[rows:]:
        copy.wait()
    for row_step in range(3):
        for start, span in chunks(3 * channels):
            conv_weight_ref[row_step, span] = conv_weight_ref[row_step, span] * low(0.5)


def decoded_kernel(term_ref, decode_weight_ref, decode_bias_ref, after_ref, decoded_ref):
    canvases, rows, across, channels = decoded_ref.shape
    weight = decode_weight_ref[...] * low(0.5)
    weight = jnp.concatenate([jnp.zeros_like(weight), weight], axis=0)
    bias = decode_bias_ref[...].astype(wide).reshape(1, channels)
    for row in range(rows):
        decoded = (mm(term_ref[row].astype(low), weight) + bias).astype(low)
        decoded_ref[:, row] = decoded.reshape(canvases, across, channels)


class Places:
    mate, other = "mate", "other"

    def __init__(self, rows, count):
        self.rows, self.count = rows, count
        self.odd = lax.axis_index("strip") % 2 == 1
        self.inner = list(range(1, rows - 1))

    def row(self, unit):
        if unit == self.mate:
            return jnp.where(self.odd, 0, self.rows - 1)
        if unit == self.other:
            return jnp.where(self.odd, self.rows - 1, 0)
        return unit

    def toward(self, unit):
        return jnp.where(self.odd, *((0, 2) if unit == self.mate else (2, 0)))

    def halo(self, unit):
        first, last = 0, self.rows + 1
        return jnp.where(self.odd, *((first, last) if unit == self.mate else (last, first)))

    def span(self, number, at=0, size=None):
        start = number * self.count + at
        if not isinstance(start, int):
            start = pl.multiple_of(start, tile_rows)
        return pl.ds(start, size or self.count)

    def masks(self, masks_ref, plane, unit, canvas, across):
        return Masks(masks_ref, plane, self.row(unit) * self.count + canvas * across, across)


def rows_kernel(
    beyond,
    masks_ref,
    latent_ref,
    term_ref,
    conv_weight_ref,
    conv_bias_ref,
    mix_weight_ref,
    mix_bias_ref,
    proj_weight_ref,
    proj_bias_ref,
    halo_ref,
    also_ref,
    *refs,
):
    first = beyond == Places.mate
    outs = refs[-12:] if first else refs[-10:]
    slab_ref, grad_ref, up_ref, down_ref, second_ref, stream_ref, codes_ref = outs[:7]
    branch_grad_ref, sums_ref, edge_ref = outs[7:10]
    canvases, rows, across, channels = latent_ref.shape
    size = proj_weight_ref.shape[0]
    count = canvases * across
    places = Places(rows, count)
    units = [*places.inner, places.mate] if first else [places.other]

    def own(row, canvas):
        return lambda at: silu(latent_ref[canvas, row, pl.ds(at, tile_rows)])

    def halo(canvas):
        return lambda at: silu(halo_ref[canvas, pl.ds(at, tile_rows)])

    proj = proj_weight_ref[...]
    proj_both = jnp.concatenate([proj * low(2 * commit_weight), proj * low(-2.0)], axis=0).T
    mix_back = (mix_weight_ref[...] * low(0.5)).T
    proj_top = jnp.concatenate([proj, jnp.zeros_like(proj)], axis=0)
    conv_bias = 0.5 * conv_bias_ref[...].astype(wide).reshape(1, channels)
    mix_bias = mix_bias_ref[...].astype(wide).reshape(1, channels)
    proj_bias = proj_bias_ref[...].astype(wide).reshape(1, size)
    proj_bias = jnp.concatenate([2 * commit_weight * proj_bias, -2.0 * proj_bias], axis=1)
    sums = [None, None, None]
    steps = chunks(across)
    tape = Tape()
    slabs = {}

    def add_to(place, values):
        values = values[:8] + values[8:]
        sums[place] = values if sums[place] is None else sums[place] + values

    def slab_of(row, canvas):
        if row != beyond and (not first or row == places.other):
            return None
        if (row, canvas) not in slabs:
            if row == beyond:
                place, values = places.halo(beyond), halo(canvas)
            else:
                place, values = row + 1, own(row, canvas)
            sides = [
                places.masks(masks_ref, plane, row, canvas, across)
                for plane in (left_plane, right_plane)
            ]
            start = places.span(place, canvas * across).start
            slabs[row, canvas] = tape.add(
                "vpu", 0.08, [], lambda: store_slab(slab_ref, start, *sides, values)
            )
        return slabs[row, canvas]

    group = canvases if first else 1

    def tile(unit, canvas):
        inside = canvas * across
        there = places.row(unit)
        here = places.span(there, inside, group * across)
        above, below = [
            places.masks(masks_ref, plane, unit, canvas, across) for plane in (up_plane, down_plane)
        ]
        if unit == places.other:
            plane = jnp.where(places.odd, down_plane, up_plane)
            halo_masks = places.masks(masks_ref, plane, unit, canvas, across)
        conv, slope, made = [None] * 3, [], [None] * 4
        steps = chunks(group * across)

        def span(start):
            return places.span(there, inside + start, tile_rows)

        def multiply(place, step):
            def run():
                made[place] = step()

            return run

        def convolve(row_step):
            def run():
                rows_of = places.span(there + row_step, inside, group * across)
                conv[row_step] = mm(slab_ref[rows_of], conv_weight_ref[row_step])

            return run

        def convolve_halo():
            rows_of = places.span(places.halo(unit), inside, group * across)
            conv[0] = mm(slab_ref[rows_of], conv_weight_ref[places.toward(unit)])

        def activate():
            up, mid, down = conv
            for start, _ in steps:
                some = slice(start, start + tile_rows)
                if unit == places.other:
                    total = masked(up[some], halo_masks(start).astype(wide))
                    total = total + also_ref[pl.ds(inside + start, tile_rows)]
                else:
                    total = masked(up[some], above(start).astype(wide))
                    total = total + masked(down[some], below(start).astype(wide)) + mid[some]
                second, twice = silu_slopes(total + conv_bias)
                second_ref[span(start)] = second.astype(low)
                slope.append(twice)

        def add_latent():
            for start, _ in steps:
                latent = latent_ref[canvas + start // across, there, pl.ds(start % across, tile_rows)].astype(wide)
                part = latent + (made[0][start : start + tile_rows] + mix_bias)
                stream_ref[span(start)] = part.astype(low)

        def add_term():
            for start, _ in steps:
                part = made[1][start : start + tile_rows]
                part = part + (term_ref[there, pl.ds(inside + start, tile_rows)] + proj_bias)
                codes_ref[span(start)] = part.astype(low)
                add_to(2, part)

        def keep_branch():
            for start, _ in steps:
                part = made[2][start : start + tile_rows]
                branch_grad_ref[there, pl.ds(inside + start, tile_rows)] = part.astype(low)
                add_to(1, part)

        def keep_grad():
            for place, (start, _) in enumerate(steps):
                some = slice(start, start + tile_rows)
                part = made[3][some] * slope[place]
                rounded = part.astype(low)
                grad_ref[span(start)] = rounded
                up_ref[span(start)] = masked(rounded, above(start))
                down_ref[span(start)] = masked(rounded, below(start))
                if unit == beyond:
                    edge_ref[pl.ds(inside + start, tile_rows)] = rounded
                add_to(0, part)

        if unit == places.mate:
            needs = [*range(rows), unit]
        elif unit == places.other:
            needs = [unit]
        else:
            needs = [unit - 1, unit, unit + 1]
        needs = [slab_of(near, canvas + k) for near in needs for k in range(group)]
        if unit == places.other:
            last = [tape.add("mxu", 0.063 * group, needs, convolve_halo)]
        else:
            last = [tape.add("mxu", 0.063 * group, needs, convolve(row_step)) for row_step in range(3)]
        last = tape.add("vpu", 0.1 * group, last, activate)
        chain = [
            (0.021, lambda: mm(second_ref[here], mix_weight_ref[...]), 0.04, add_latent),
            (0.021, lambda: mm(stream_ref[here], proj_both), 0.03, add_term),
            (0.021, lambda: mm(codes_ref[here], proj_top), 0.03, keep_branch),
            (
                0.021,
                lambda: mm(branch_grad_ref[there, pl.ds(inside, group * across)], mix_back),
                0.07,
                keep_grad,
            ),
        ]
        for place, (cost, product, later, rest) in enumerate(chain):
            last = tape.add("mxu", cost * group, [last], multiply(place, product))
            last = tape.add("vpu", later * group, [last], rest)

    def weigh():
        box = [None]

        def product(row):
            def run():
                part = mm_tn(term_ref[row].astype(low), also_ref[row].reshape(count, channels))
                box[0] = part if box[0] is None else box[0] + part

            return run

        def store():
            refs[-2][...] = 0.5 * box[0][size:]

        made = [tape.add("mxu", 0.12, [], product(row)) for row in range(rows)]
        tape.add("vpu", 0.02, made, store)

    def convolve_last(canvas, some):
        there = places.row(places.other)
        inward = jnp.where(places.odd, -1, 1)
        plane = jnp.where(places.odd, up_plane, down_plane)
        masks = places.masks(masks_ref, plane, places.other, canvas, across)
        inside = canvas * across
        made = [None, None]

        def product(place, row, tap):
            def run():
                rows_of = places.span(row + 1, inside, some * across)
                made[place] = mm(slab_ref[rows_of], conv_weight_ref[tap])

            return run

        def store():
            for start, _ in chunks(some * across):
                near = slice(start, start + tile_rows)
                part = made[0][near] + masked(made[1][near], masks(start).astype(wide))
                refs[-1][pl.ds(inside + start, tile_rows)] = part

        needs = [slab_of(row, canvas + k) for row in range(rows) for k in range(some)]
        steps = [(there, 1), (there + inward, inward + 1)]
        needs = [
            tape.add("mxu", 0.063 * some, needs, product(place, *step))
            for place, step in enumerate(steps)
        ]
        tape.add("vpu", 0.04 * some, needs, store)

    if first:
        weigh()
    for unit in units:
        for canvas in range(0, canvases, group):
            tile(unit, canvas)
    if first:
        some = 2 if canvases % 2 == 0 else 1
        for canvas in range(0, canvases, some):
            convolve_last(canvas, some)
    tape.play()
    sums = [jnp.sum(values, axis=0, keepdims=True) for values in sums]
    sums[2] = jnp.concatenate([sums[2]] * (channels // sums[2].shape[1]), axis=1)
    blank = jnp.zeros((sums_ref.shape[0] - 3, channels), wide)
    sums = jnp.concatenate([*sums, blank], axis=0)
    sums_ref[...] = sums if first else sums + refs[8][...]


def weight_kernel(
    plan,
    mine,
    slab_ref,
    grad_ref,
    up_ref,
    down_ref,
    second_ref,
    stream_ref,
    codes_ref,
    branch_grad_ref,
    sums_ref,
    picks_ref,
    decode_weight_grad_ref,
    decode_bias_grad_ref,
    after_ref,
    out_ref,
):
    total, channels = grad_ref.shape
    rows, count, _ = branch_grad_ref.shape
    size = decode_weight_grad_ref.shape[0]
    entries = picks_ref.shape[1]
    core = lax.axis_index("strip") % 2
    wanted = core if mine else 1 - core
    place = plan.place(wanted)

    def step(row_step, weighted_ref, first, last):
        span, lanes = pl.ds(row_step * count, total), pl.ds(first * channels, (last - first) * channels)
        return (last - first) * channels, lambda: mm_tn(slab_ref[span, lanes], weighted_ref[...])

    def fill(parts):
        piece, had = [], 0
        at = 0
        rest = plan.half_rows - sum(depth for depth, _ in parts)
        for depth, part in [*parts, (rest, lambda: jnp.zeros((rest, channels), wide))]:
            values = part() if depth else None
            start = 0
            while start < depth:
                some = min(depth - start, plan.piece_rows - had)
                piece.append(values[start : start + some])
                start += some
                had += some
                if had == plan.piece_rows:
                    out_ref[at ^ place] = jnp.concatenate(piece, axis=0).astype(low)
                    piece, had = [], 0
                    at += 1

    @pl.when(wanted == 0)
    def _():
        fill(
            [
                step(0, up_ref, 0, 3),
                step(1, grad_ref, 0, 2),
                (size, lambda: mm_tn(codes_ref[...], stream_ref[...])[:size]),
                (size, lambda: decode_weight_grad_ref[...]),
            ]
        )

    @pl.when(wanted == 1)
    def _():
        sums = sums_ref[...]
        biases = [sums[0:1], sums[1:2], decode_bias_grad_ref[...], sums[2:3]]
        biases.append(jnp.zeros((tile_rows - len(biases), channels), wide))

        def picked():
            part = mm_tn(codes_ref[...], picks_ref[...])[size:]
            return jnp.concatenate([part[:, i : i + channels] for i in range(0, entries, channels)], axis=0)

        fill(
            [
                step(1, grad_ref, 2, 3),
                step(2, down_ref, 0, 3),
                (channels, lambda: mm_tn(second_ref[...], branch_grad_ref[...].reshape(total, channels))),
                (size * (entries // channels), picked),
                (tile_rows, lambda: jnp.concatenate(biases, axis=0)),
            ]
        )


def input_kernel(
    mine,
    masks_ref,
    latent_ref,
    grad_ref,
    mate_ref,
    other_ref,
    branch_grad_ref,
    conv_weight_ref,
    after_ref,
    *refs,
):
    latent_grad_ref, slab_ref, back_ref, out_ref, sems = refs[-5:]
    canvases, rows, across, channels = latent_ref.shape
    count = canvases * across
    places = Places(rows, count)
    steps = chunks(across)
    tape = Tape()

    def own(row, canvas):
        start = row * count + canvas * across
        return lambda at: grad_ref[pl.ds(start + at, tile_rows)].astype(wide)

    def beside(mate, canvas):
        def values(at):
            span = pl.ds(canvas * across + at, tile_rows)
            return jnp.where(mate, mate_ref[span], other_ref[span]).astype(wide)

        return values

    for row_step in range(3):
        for col_step in range(3):
            lanes = slice((2 - col_step) * channels, (3 - col_step) * channels)
            turned = conv_weight_ref[2 - row_step, lanes].T
            back_ref[row_step, col_step * channels : (col_step + 1) * channels] = turned

    slabs = {}

    def slab_of(row, canvas):
        if (row, canvas) not in slabs:
            if row < 0:
                values = beside(places.odd, canvas)
            elif row == rows:
                values = beside(jnp.logical_not(places.odd), canvas)
            else:
                values = own(row, canvas)
            near = min(max(row, 0), rows - 1)
            sides = [
                places.masks(masks_ref, plane, near, canvas, across)
                for plane in (left_plane, right_plane)
            ]
            start = (row + 1) * count + canvas * across
            slabs[row, canvas] = tape.add(
                "vpu", 0.07, [], lambda: store_slab(slab_ref, start, *sides, values)
            )
        return slabs[row, canvas]

    def tile(place, row, canvas):
        inside = canvas * across
        above, below = [
            places.masks(masks_ref, plane, row, canvas, across) for plane in (up_plane, down_plane)
        ]
        spreads = [None] * 3

        def spread(row_step):
            def run():
                span = pl.ds((row + row_step) * count + inside, across)
                spreads[row_step] = mm(slab_ref[span], back_ref[row_step])

            return run

        def finish():
            for start, _ in steps:
                some = slice(start, start + tile_rows)
                total = masked(spreads[0][some], above(start).astype(wide))
                total = total + masked(spreads[2][some], below(start).astype(wide))
                total = total + spreads[1][some]
                near = pl.ds(start, tile_rows)
                _, twice = silu_slopes(0.5 * latent_ref[canvas, row, near].astype(wide))
                stream = branch_grad_ref[row, pl.ds(inside + start, tile_rows)]
                out_ref[place, canvas, near] = (stream.astype(wide) + total * twice).astype(low)

        needs = [slab_of(near, canvas) for near in (row - 1, row, row + 1)]
        made = [tape.add("mxu", 0.063, needs, spread(row_step)) for row_step in range(3)]
        tape.add("vpu", 0.12, made, finish)

    for canvas in range(canvases):
        for place, row in enumerate(mine):
            tile(place, row, canvas)
    tape.play()
    copies = []
    for place, row in enumerate(mine):
        copies.append(
            pltpu.make_async_copy(out_ref.at[place], latent_grad_ref.at[:, row], sems.at[place])
        )
        copies[-1].start()
    for copy in copies:
        copy.wait()


class Plan:
    def __init__(self, sizes, half_rows):
        self.sizes = sizes
        bits = {axis: [(axis, b) for b in range(size.bit_length() - 1)] for axis, size in sizes.items()}
        strip, canvas = bits["strip"], bits["canvas"]
        near, far = [*canvas[:1], *strip[1:2]], strip[2:4][::-1]
        rest = [*strip[4:], *canvas[1:]]
        rest = [rest[i : i + 2] for i in range(0, len(rest), 2)]
        even, odd = [near, far, *rest], [far, near, *rest]
        stages = [tuple(zip(*pair, strict=True)) for pair in zip(even, odd, strict=True) if pair[0]]
        self.split, self.whole = stages[0], stages[1:]
        self.core = ((("strip", 0), ("strip", 0)),)
        self.half = 2 ** len(self.split)
        self.piece_rows = -(-half_rows // (self.half * half_tile)) * half_tile
        self.half_rows = self.half * self.piece_rows

    def place(self, core):
        number = 0
        for spots in self.split:
            even, odd = [(lax.axis_index(axis) // 2**bit) % 2 for axis, bit in spots]
            number = number * 2 + jnp.where(core == 0, even, odd)
        return number

    def swap(self, values, stage, step):
        width = self.sizes["canvas"]
        pairs = []
        for strip in range(self.sizes["strip"]):
            change = {"strip": 0, "canvas": 0}
            for place, spots in enumerate(reversed(stage)):
                if step >> place & 1:
                    axis, bit = spots[strip % 2]
                    change[axis] |= 1 << bit
            for canvas in range(width):
                target = (strip ^ change["strip"]) * width + (canvas ^ change["canvas"])
                pairs.append((strip * width + canvas, target))
        return lax.ppermute(values, ("strip", "canvas"), pairs)


def add_kernel(count, after, *refs):
    ins, outs = refs[:count], refs[count + after :]
    depth = outs[0].shape[0]
    for place, out_ref in enumerate(outs):
        span = pl.ds(place * depth, depth)
        terms = [ref[span].astype(wide) for ref in ins]
        while len(terms) > 1:
            terms = [sum(terms[i + 1 : i + 2], terms[i]) for i in range(0, len(terms), 2)]
        out_ref[...] = terms[0].astype(low)


def add_split(arrays, parts, after=()):
    depth, rows, channels = arrays[0].shape
    shape = jax.ShapeDtypeStruct((depth // parts, rows, channels), low)
    return pl.pallas_call(
        functools.partial(add_kernel, len(arrays), len(after)),
        in_specs=[in_vmem] * len(arrays) + [anywhere] * len(after),
        out_specs=[in_vmem] * parts,
        out_shape=[shape] * parts,
        compiler_params=pltpu.CompilerParams(vmem_limit_bytes=vmem_bytes),
    )(*arrays, *after)


def gate_kernel(*refs):
    pass


def gate(array, *after):
    return pl.pallas_call(
        gate_kernel,
        in_specs=[in_vmem] + [anywhere] * len(after),
        out_specs=in_vmem,
        out_shape=jax.ShapeDtypeStruct(array.shape, array.dtype),
        input_output_aliases={0: 0},
        compiler_params=pltpu.CompilerParams(vmem_limit_bytes=vmem_bytes),
    )(array, *after)


def final_kernel(plan, mine, count, sizes, *refs):
    ins, outs, scratch = refs[:count], refs[-15:-6], refs[-6:]
    gathered_ref, *line_refs, sems = scratch
    channels, size, entries = sizes
    core = lax.axis_index("strip") % 2
    half = core if mine else 1 - core
    place = plan.place(half)
    conv_ref, conv_bias_ref, mix_ref, mix_bias_ref, proj_ref, proj_bias_ref = outs[:6]
    codebook_ref, decode_ref, decode_bias_ref = outs[6:]
    conv_rows = 5 * channels
    early = min(conv_rows, 9 * channels - conv_rows) // plan.piece_rows
    sent = []
    at = 0
    for ref in ins:
        for piece in range(ref.shape[0]):
            shard = place ^ at
            start = pl.multiple_of(shard * plan.piece_rows, tile_rows)
            gathered_ref[pl.ds(start, plan.piece_rows)] = ref[piece].astype(wide)

            def send(start=start, at=at):
                target = pl.multiple_of(half * conv_rows + start, tile_rows)
                return pltpu.make_async_copy(
                    gathered_ref.at[pl.ds(start, plan.piece_rows)],
                    conv_ref.at[pl.ds(target, plan.piece_rows)],
                    sems.at[12 + at],
                )

            pl.when(shard < early)(lambda send=send: send().start())
            sent.append((shard, send))
            at += 1

    def copy_all(pairs):
        copies = [
            pltpu.make_async_copy(source, target, sems.at[number])
            for number, (source, target) in enumerate(pairs)
        ]
        for copy in copies:
            copy.start()
        for copy in copies:
            copy.wait()

    def place_all(first, last, targets):
        pairs = []
        done = early * plan.piece_rows
        if last - first > done:
            rest = last - first - done
            source = gathered_ref.at[pl.ds(done, rest)]
            pairs.append((source, conv_ref.at[pl.ds(first + done, rest)]))
        at = last - first
        for target, depth in targets:
            pairs.append((gathered_ref.at[pl.ds(at, depth)], target))
            at += depth
        return pairs, at

    @pl.when(half == 0)
    def _():
        copy_all(place_all(0, conv_rows, [(proj_ref, size), (decode_ref, size)])[0])

    @pl.when(half == 1)
    def _():
        targets = [(mix_ref, channels)]
        for piece in range(0, entries, channels):
            targets.append((codebook_ref.at[:, pl.ds(piece, channels)], size))
        pairs, at = place_all(conv_rows, 9 * channels, targets)
        lines = gathered_ref[pl.ds(at, tile_rows)]
        targets = (conv_bias_ref, mix_bias_ref, decode_bias_ref, proj_bias_ref)
        for number, (line_ref, target) in enumerate(zip(line_refs, targets, strict=True)):
            line_ref[...] = lines[number : number + 1, : target.shape[1]]
            pairs.append((line_ref, target))
        copy_all(pairs)

    for shard, send in sent:
        pl.when(shard < early)(lambda send=send: send().wait())


def per_device(
    plan,
    latent_in,
    crop_code,
    code_index,
    conv_weight,
    conv_bias,
    mix_weight,
    mix_bias,
    proj_weight,
    proj_bias,
    codebook,
    decode_weight,
    decode_bias,
    out_grad,
):
    canvases, rows, across, channels = latent_in.shape
    entries, size = codebook.shape
    count = canvases * across
    total = rows * count
    strips = plan.sizes["strip"]
    struct = jax.ShapeDtypeStruct
    flat_weight = conv_weight.reshape(3, 3 * channels, channels)

    def far_away(*arrays):
        return [pltpu.with_memory_space_constraint(array, pltpu.HBM) for array in arrays]

    def call(kernel, ins, outs, shapes, scratch=(), flops=0, aliases=None):
        return pl.pallas_call(
            kernel,
            in_specs=list(ins),
            out_specs=list(outs),
            out_shape=list(shapes),
            scratch_shapes=list(scratch),
            input_output_aliases=aliases or {},
            compiler_params=pltpu.CompilerParams(vmem_limit_bytes=vmem_bytes),
            cost_estimate=pl.CostEstimate(flops=flops, bytes_accessed=0, transcendentals=0),
        )

    def trade(mate, other, split=True):
        near = [(i, i ^ 1) for i in range(strips)]
        far = [(i, i + 1) for i in range(1, strips - 1, 2)]
        far += [(target, source) for source, target in far]
        if not split:
            return lax.ppermute(mate, "strip", near), lax.ppermute(other, "strip", far)
        half = other.shape[0] // 2
        others = [lax.ppermute(part, "strip", far) for part in (other[:half], other[half:])]
        return (lax.ppermute(mate, "strip", near), *others)

    edge_shape = struct((canvases, across, channels), low)
    starts = [
        struct(crop_code.shape, crop_code.dtype),
        struct(code_index.shape, code_index.dtype),
        struct((size, entries), low),
        struct((size, channels), low),
    ]
    *edges, crop, index, near_codebook, near_decode = call(
        edge_kernel,
        [in_hbm] * 5,
        [in_vmem] * 6,
        [edge_shape, edge_shape, *starts],
        [pltpu.SemaphoreType.DMA((6,))],
    )(*far_away(latent_in, crop_code, code_index, codebook.T, decode_weight))
    mate, other = trade(*edges, split=False)
    outs = [
        struct((rows, count, 2 * size), wide),
        struct((total, entries), low),
        struct((len(bits), total, 128), low),
        struct((1, channels), wide),
        struct((rows, canvases, across, channels), low),
        struct(latent_in.shape, low),
        struct(flat_weight.shape, low),
        struct(mix_weight.shape, low),
    ]
    held = [pltpu.SemaphoreType.DMA((rows + 3,))]
    term, picks, masks, decode_bias_grad, near_grad, latent, near_weight, near_mix = call(
        code_kernel,
        [in_vmem] * 4 + [in_hbm] * 4,
        [in_vmem] * 8,
        outs,
        held,
        flops=6 * total * channels * channels,
    )(
        crop,
        index,
        near_codebook,
        near_decode,
        *far_away(out_grad, latent_in, flat_weight, mix_weight),
    )
    slab_shape = struct((total + 2 * count, 3 * channels), low)
    flat = struct((total, channels), low)
    kept = [slab_shape, flat, flat, flat, flat, flat, struct((total, 2 * size), low)]
    kept += [struct((rows, count, channels), low), struct((8, channels), wide)]
    edge_shape = struct((count, channels), low)
    inner, outer = tuple(range(1, rows - 1)), tuple(sorted({0, rows - 1}))
    shared = [masks, latent, term, near_weight, conv_bias, near_mix, mix_bias, proj_weight.T, proj_bias]

    def block_rows(beyond, halo, also, before, more):
        ins = [*shared, halo, also, *before]
        first = len(ins) - len(before)
        return call(
            functools.partial(rows_kernel, beyond),
            [in_vmem] * len(ins),
            [in_vmem] * (len(kept) + 1 + len(more)),
            [*kept, edge_shape, *more],
            flops=20 * total * channels * channels,
            aliases={first + i: i for i in range(len(before))},
        )(*ins)

    more = [struct((size, channels), wide), struct((count, channels), wide)]
    *before, edge_mate, decode_weight_grad, partial = block_rows("mate", mate, near_grad, (), more)
    *before, edge_other = block_rows("other", other, partial, before, ())
    slab, grad, up, down, second, stream, codes, branch_grad, sums = before
    edges = (edge_mate, edge_other)

    def weight_half(mine, after):
        ins = [slab, grad, up, down, second, stream, codes, branch_grad, sums, picks]
        ins += [decode_weight_grad, decode_bias_grad]
        return call(
            functools.partial(weight_kernel, plan, mine),
            [in_vmem] * len(ins) + [anywhere],
            [in_vmem],
            [struct((plan.half, plan.piece_rows, channels), low)],
            flops=10 * total * channels * channels,
        )(*ins, after)[0]

    send = weight_half(False, edge_other)
    keep = weight_half(True, send)

    def input_rows(mine, halo, after, *before):
        return call(
            functools.partial(input_kernel, mine),
            [in_vmem] * 7 + [anywhere] + [in_hbm] * len(before),
            [in_hbm],
            [pltpu.HBM(latent_in.shape, low)],
            [
                pltpu.VMEM(slab_shape.shape, low),
                pltpu.VMEM(flat_weight.shape, low),
                pltpu.VMEM((len(mine), canvases, across, channels), low),
                pltpu.SemaphoreType.DMA((len(mine),)),
            ],
            flops=11 * total * channels * channels,
            aliases={8: 0} if before else {},
        )(masks, latent, grad, *halo, branch_grad, near_weight, after, *before)[0]

    parts = add_split([keep, plan.swap(send, plan.core, 1)], plan.half)
    halo = trade(*edges, split=False)
    swaps = [plan.swap(parts[i], plan.split, i) for i in reversed(range(1, plan.half))]
    piece = add_split([parts[0], *swaps], 1)[0]
    latent_grad = input_rows(inner, edges, piece)
    decoded = call(
        decoded_kernel,
        [in_vmem, in_vmem, in_vmem, anywhere],
        [pl.BlockSpec()],
        [pltpu.HBM(out_grad.shape, low)],
        flops=4 * total * channels * channels,
    )(term, near_decode, decode_bias, piece)[0]
    after = far_away(decoded, latent_grad)
    for stage in plan.whole:
        swaps = [plan.swap(piece, stage, i) for i in range(1, 2 ** len(stage))]
        piece = add_split([piece, *swaps], 1, after)[0]
        after = []
    others = [plan.swap(piece, plan.split, i) for i in range(1, plan.half)]
    latent_grad = input_rows(outer, halo, piece, latent_grad)
    done = far_away(latent_grad)
    pieces = [piece, *[gate(other, *done) for other in others]]
    swapped = [plan.swap(piece, plan.core, 1) for piece in pieces]
    shapes = [
        (9 * channels, channels),
        (1, channels),
        (channels, channels),
        (1, channels),
        (size, channels),
        (1, size),
        (size, entries),
        (size, channels),
        (1, channels),
    ]

    def finish(mine, arrays, *before):
        count = len(arrays)
        return call(
            functools.partial(final_kernel, plan, mine, count, (channels, size, entries)),
            [in_vmem] * count + [in_hbm] * len(before),
            [in_hbm] * len(shapes),
            [pltpu.HBM(shape, wide) for shape in shapes],
            [
                pltpu.VMEM((plan.half_rows, channels), wide),
                *[pltpu.VMEM((1, channels), wide)] * 3,
                pltpu.VMEM((1, size), wide),
                pltpu.SemaphoreType.DMA((16,)),
            ],
            aliases={count + i: i for i in range(len(before))},
        )(*arrays, *before)

    results = finish(True, pieces)
    results = finish(False, swapped, *results)
    return (
        decoded,
        latent_grad,
        results[0].reshape(3, 3, channels, channels),
        results[1].reshape(-1),
        results[2],
        results[3].reshape(-1),
        results[4].T,
        results[5].reshape(-1),
        results[6].T,
        results[7],
        results[8].reshape(-1),
    )


def solution(mesh):
    sizes = {axis: mesh.shape[axis] for axis in ("strip", "canvas")}
    shared = P("canvas", "strip", None, None)
    codes = P("canvas", "strip", None)

    def wrapped(*args):
        channels = args[0].shape[3]
        entries, size = args[9].shape
        others = 5 * channels + size * (entries // channels) + tile_rows
        plan = Plan(sizes, max(5 * channels + 2 * size, others))
        return jax.shard_map(
            functools.partial(per_device, plan),
            mesh=mesh,
            in_specs=(shared, codes, codes, *[P()] * 9, shared),
            out_specs=(shared, shared, *[P()] * 9),
            check_vma=False,
        )(*args)

    return wrapped
```
